32 devices in a mesh: ctx: 4 (over x, core), tp: 4 (over z), fsdp: 2 (over y).
Axes of the slice: x: 2, y: 2, z: 4, core: 2. Of those that a mesh axis runs over, the one named last changes fastest.
Arguments:
- tokens: bfloat16 [8192, 8192], P(('ctx', 'fsdp'), 'tp'), may hold values from -6 to 6
- weight: bfloat16 [8192, 3, 4096], P('fsdp', None, 'tp'), may hold values from -0.0625 to 0.0625
- rate: float32 [4096, 16], P(('tp', 'fsdp')), may hold values from 1.2207031e-06 to 0.1
- residue: float32 [4096, 16], P(('tp', 'fsdp')), may hold values from -3 to 3
- skip: float32 [4096], P(('tp', 'fsdp')), may hold values from 0.5 to 1.5
- order: int32 [8], replicated, may hold values from 0 to 7, each once
Outputs:
- gated: bfloat16 [4096, 8192], P(('tp', 'fsdp'), 'ctx')
The draws below stay inside these ranges and needn't reach their ends.
Inputs may be any that keep to these rules, and one draw needn't show every extreme that they name: order is a permutation: every segment number appears once.
All inputs are finite; a program needn't handle non-finite values.
Results may differ from the reference program's by a relative error of at most 0.006.
Values may be sent and summed in bfloat16 or wider, within the bound.
No kernel may reach another device: no remote copies, remote signals or barrier semaphores. Data moves between devices by JAX's collectives and lax.ppermute only.
A program may use at most 256 MiB of HBM per device.

```python
import math
import jax
import jax.numpy as jnp
from jax import lax

D = 8192
CHAN = 4096
POLES = 16
SEG_LEN = 1024
SEQ = 8192
N_CTX = 4


def draw_rate(key, part):
    key = jax.random.fold_in(key, 11)
    lowest = 0.01 / SEQ
    uniform_part = jax.random.uniform(key, (CHAN, POLES), jnp.float32)
    return lowest * jnp.exp(uniform_part * math.log(0.1 / lowest))


def block_levels(rng, shape, shards, low, high):
    def one(dim, blocks):
        draws = jax.random.uniform(jax.random.fold_in(jax.random.fold_in(rng, 6), dim), (blocks,), jnp.float32, low / len(shards), high / len(shards))
        return jnp.repeat(jnp.exp(draws), shape[dim] // blocks).reshape((-1,) + (1,) * (len(shape) - dim - 1))

    loudness = one(*shards[0])
    for cut in shards[1:]:
        loudness = loudness * one(*cut)
    return loudness


def gaussian(stream_key, shape, spread, limit, shards=(), kind=jnp.bfloat16):
    values = spread * jax.random.normal(stream_key, shape, jnp.float32)
    if shards:
        values = values * block_levels(stream_key, shape, shards, -0.22, 0.18)
    return jnp.clip(values, -limit, limit).astype(kind)


def setup_inputs(seed: int = 0) -> dict:
    key_of = jax.random.split(jax.random.key(seed), 7)
    tokens = gaussian(key_of[0], (SEQ, D), 1.0, 6.0, ((0, 8), (1, 4)))
    weight = gaussian(key_of[1], (D, 3, CHAN), D ** -0.5, 0.0625, ((0, 2), (2, 4)))
    rate = draw_rate(jax.random.fold_in(key_of[6], 71), 0)
    residue = gaussian(key_of[3], (CHAN, POLES), 0.5, 3.0, ((0, 8),), jnp.float32)
    skip = jnp.clip(0.5 + 1.0 * jax.random.uniform(key_of[4], (CHAN,), jnp.float32) ** block_levels(key_of[4], (CHAN,), ((0, 8),), -0.2, 0.2), 0.5, 1.5)
    order = jax.random.permutation(key_of[5], 2 * N_CTX).astype(jnp.int32)
    return {"tokens": tokens, "weight": weight, "rate": rate, "residue": residue, "skip": skip, "order": order}


def pole_gain(rate, residue, length):
    return residue * jnp.sqrt(jnp.maximum(-jnp.expm1(-2.0 * rate), 1.0 / length))

def reference(tokens, weight, rate, residue, skip, order):
    count = 2 * N_CTX
    group = math.gcd(CHAN, 256)
    n_groups = CHAN // group
    w_groups = weight.reshape(D, 3, n_groups, group).transpose(2, 0, 1, 3)
    r_groups = rate.reshape(n_groups, group, POLES)
    res_groups = residue.reshape(n_groups, group, POLES)
    skip_groups = skip.reshape(n_groups, group)
    tokens_wide = tokens.astype(jnp.float32)
    times = jnp.arange(SEQ).astype(jnp.float32)
    length = 2 * SEQ

    def one_group(args):
        w_part, r_part, res_part, skip_part = args
        projected = jnp.einsum('dkc,td->ckt', w_part.astype(jnp.float32), tokens_wide, precision=lax.Precision.HIGHEST).astype(jnp.bfloat16)
        query = projected[:, 0].astype(jnp.float32)
        product = projected[:, 1].astype(jnp.float32) * projected[:, 2].astype(jnp.float32)
        gain = pole_gain(r_part, res_part, SEQ)
        filt = jnp.einsum('cr,crt->ct', gain, jnp.exp(-r_part[:, :, None] * times[None, None, :]), precision=lax.Precision.HIGHEST)
        blocks = product.reshape(group, count, SEG_LEN)
        in_seq = jnp.zeros_like(blocks).at[:, order].set(blocks).reshape(group, SEQ)
        conv = jnp.fft.irfft(jnp.fft.rfft(in_seq, n=length) * jnp.fft.rfft(filt, n=length), n=length)[:, :SEQ]
        back = conv.reshape(group, count, SEG_LEN)[:, order].reshape(group, SEQ)
        return (query * (back + skip_part[:, None] * product)).astype(jnp.bfloat16)
    result = lax.map(one_group, (w_groups, r_groups, res_groups, skip_groups))
    return result.reshape(CHAN, SEQ)
```

```python
import functools

import jax
import jax.numpy as jnp
from jax import lax
from jax.experimental import pallas as pl
from jax.experimental.pallas import tpu as pltpu
from jax.sharding import PartitionSpec as P

MIB = 1 << 20
DEPTH = 512
CHUNKS = (256, 256, 256, 256)


def exchanged(block, axis, mask):
    count = lax.axis_size(axis)
    return lax.ppermute(block, axis, [(i, i ^ mask) for i in range(count)])


def pole_gain(rate, residue, length):
    return residue * jnp.sqrt(jnp.maximum(-jnp.expm1(-2.0 * rate), 1.0 / length))


def project_kernel(n_own, n_pieces, per_part, has_init, final, place, *refs):
    refs = list(refs)
    tokens = refs.pop(0)
    own = refs.pop(0) if n_own else None
    pieces = [refs.pop(0) for _ in range(n_pieces)]
    init = refs.pop(0) if has_init else None
    outs = [refs.pop(0) for _ in range(2 if final else 1)]
    x_buf, w_buf, x_sem, w_sem = refs[:4]
    acc = refs[4] if final else outs[0]
    rows = x_buf.shape[1]
    per_quarter = tokens.shape[2] // DEPTH
    pair, ctx = place[0], place[1]
    n_half = tokens.shape[0] * per_quarter // 2
    steps = n_own + n_pieces
    slots = x_buf.shape[0]

    def start(step):
        slot = lax.rem(step, slots)
        rest = step - n_own
        part = jnp.bitwise_xor(ctx, lax.div(rest, per_part))
        theirs = (1 - pair) * n_half + part * per_part + lax.rem(rest, per_part)
        block = jnp.where(step < n_own, pair * n_half + step, theirs)
        quarter = lax.div(block, per_quarter)
        column = pl.multiple_of(lax.rem(block, per_quarter) * DEPTH, DEPTH)
        pltpu.make_async_copy(
            tokens.at[quarter, :, pl.ds(column, DEPTH)], x_buf.at[slot], x_sem.at[slot]
        ).start()

        if n_own:
            @pl.when(step < n_own)
            def _():
                row = pl.multiple_of(step * DEPTH, DEPTH)
                pltpu.make_async_copy(
                    own.at[:, pl.ds(row, DEPTH), :], w_buf.at[slot], w_sem.at[slot]
                ).start()

        for n, piece in enumerate(pieces):
            @pl.when(rest == n)
            def _():
                pltpu.make_async_copy(piece, w_buf.at[slot], w_sem.at[slot]).start()

    for ahead in range(slots - 1):
        start(jnp.int32(ahead))
    if has_init:
        acc[...] = init[...]
    else:
        acc[...] = jnp.zeros_like(acc)

    def body(step, carry):
        slot = lax.rem(step, slots)

        @pl.when(step + slots - 1 < steps)
        def _():
            start(step + slots - 1)

        pltpu.make_async_copy(x_buf.at[slot], x_buf.at[slot], x_sem.at[slot]).wait()
        pltpu.make_async_copy(w_buf.at[slot], w_buf.at[slot], w_sem.at[slot]).wait()
        block = x_buf[slot]
        for p in range(3):
            acc[p] += jnp.dot(block, w_buf[slot, p], preferred_element_type=jnp.float32)
        return carry

    lax.fori_loop(0, steps, body, 0)
    if final:
        kept, given = outs
        half = kept.shape[2]
        mine = pl.multiple_of(pair * half, 128)
        other = pl.multiple_of((1 - pair) * half, 128)
        for p in range(3):
            kept[p] = acc[p, :, pl.ds(mine, half)].astype(jnp.bfloat16)
            given[p] = acc[p, :, pl.ds(other, half)].astype(jnp.bfloat16)


def project(place, tokens, own, pieces, per_part, init, final):
    rows = tokens.shape[1]
    some = own if own is not None else pieces[0]
    width = some.shape[2]
    n_own = 0 if own is None else own.shape[1] // DEPTH
    slots = 3
    anywhere = pl.BlockSpec(memory_space=pl.ANY)
    local = pl.BlockSpec(memory_space=pltpu.VMEM)
    operands = [tokens] + ([own] if own is not None else []) + list(pieces)
    in_specs = [anywhere] * len(operands)
    if init is not None:
        operands.append(init)
        in_specs.append(local)
    scratch = [
        pltpu.VMEM((slots, rows, DEPTH), jnp.bfloat16),
        pltpu.VMEM((slots, 3, DEPTH, width), jnp.bfloat16),
        pltpu.SemaphoreType.DMA((slots,)),
        pltpu.SemaphoreType.DMA((slots,)),
    ]
    if final:
        scratch.append(pltpu.VMEM((3, rows, width), jnp.float32))
        out_shape = [jax.ShapeDtypeStruct((3, rows, width // 2), jnp.bfloat16)] * 2
        out_specs = [local, local]
    else:
        out_shape = jax.ShapeDtypeStruct((3, rows, width), jnp.float32)
        out_specs = local
    steps = n_own + len(pieces)
    return pl.pallas_call(
        functools.partial(project_kernel, n_own, len(pieces), per_part, init is not None, final),
        grid_spec=pltpu.PrefetchScalarGridSpec(
            num_scalar_prefetch=1,
            grid=(),
            in_specs=in_specs,
            out_specs=out_specs,
            scratch_shapes=scratch,
        ),
        out_shape=out_shape,
        compiler_params=pltpu.CompilerParams(vmem_limit_bytes=40 * MIB),
        cost_estimate=pl.CostEstimate(
            flops=2 * rows * steps * DEPTH * 3 * width,
            bytes_accessed=steps * DEPTH * (3 * width + rows) * 2,
            transcendentals=0,
        ),
        name="project",
    )(place, *operands)


def scan_kernel(kept, given, decay, gain, skip, state_in, local_ref, state_out, prod):
    poles = decay.shape[0]
    rows = kept.shape[1]
    groups = kept.shape[2] // 128
    for side, ref in enumerate((kept, given)):
        for g in range(groups):
            lanes = slice(g * 128, (g + 1) * 128)
            key = ref[1, :, lanes].astype(jnp.float32)
            value = ref[2, :, lanes].astype(jnp.float32)
            prod[:, side * groups + g, :] = key * value
    direct = skip[...]
    factors = [decay[r] for r in range(poles)]
    gains = [gain[r] for r in range(poles)]

    def step(t, states):
        p = prod[t]
        new = [factors[r] * states[r] + gains[r] * p for r in range(poles)]
        total = list(new)
        while len(total) > 1:
            total = [a + b for a, b in zip(total[::2], total[1::2])]
        local_ref[t] = total[0] + direct * p
        return tuple(new)

    states = lax.fori_loop(0, rows, step, tuple(state_in[r] for r in range(poles)), unroll=8)
    for r in range(poles):
        state_out[r] = states[r]


def scan(kept, given, decay, gain, skip, state):
    rows = kept.shape[1]
    local = pl.BlockSpec(memory_space=pltpu.VMEM)
    lanes = decay.shape[1:]
    return pl.pallas_call(
        scan_kernel,
        in_specs=[local] * 6,
        out_specs=[local] * 2,
        out_shape=[
            jax.ShapeDtypeStruct((rows,) + lanes, jnp.float32),
            jax.ShapeDtypeStruct(decay.shape, jnp.float32),
        ],
        scratch_shapes=[pltpu.VMEM((rows,) + lanes, jnp.float32)],
        compiler_params=pltpu.CompilerParams(vmem_limit_bytes=24 * MIB),
        cost_estimate=pl.CostEstimate(
            flops=64 * rows * lanes[0] * lanes[1],
            bytes_accessed=rows * lanes[0] * lanes[1] * 8,
            transcendentals=0,
        ),
        name="scan",
    )(kept, given, decay, gain, skip, state)


def finish_kernel(n_ctx, n_chunks, seg_len, place, order, *refs):
    refs = list(refs)
    ends = [refs.pop(0) for _ in range(n_ctx)]
    rate = refs.pop(0)
    decay = refs.pop(0)
    locals_ = [refs.pop(0) for _ in range(n_chunks)]
    kept = [refs.pop(0) for _ in range(n_chunks)]
    given = [refs.pop(0) for _ in range(n_chunks)]
    out = refs.pop(0)
    conv = refs.pop(0)
    poles, sublanes, _ = decay.shape
    groups = sublanes // 2
    pair, ctx = place[0], place[1]
    upper = lax.broadcasted_iota(jnp.int32, decay.shape[1:], 0) < groups
    targets = (order[2 * ctx + pair], order[2 * ctx + 1 - pair])
    states = [jnp.zeros(decay.shape[1:], jnp.float32) for _ in range(poles)]
    for mask in range(n_ctx):
        origin = jnp.bitwise_xor(ctx, mask)
        sources = (order[2 * origin + pair], order[2 * origin + 1 - pair])
        for cross in (0, 1):
            gaps = [targets[s] - 1 - sources[s ^ cross] for s in (0, 1)]
            gap = jnp.where(upper, gaps[0], gaps[1])
            span = jnp.maximum(gap, 0).astype(jnp.float32) * seg_len
            for r in range(poles):
                end = ends[mask][r]
                if cross:
                    end = jnp.concatenate([end[groups:], end[:groups]], axis=0)
                factor = jnp.where(gap >= 0, jnp.exp(-rate[r] * span), 0.0)
                states[r] = states[r] + factor * end
    factors = [decay[r] for r in range(poles)]
    states = tuple(states)
    base = 0
    for k in range(n_chunks):
        rows = locals_[k].shape[0]

        def step(t, states):
            new = [factors[r] * states[r] for r in range(poles)]
            total = list(new)
            while len(total) > 1:
                total = [a + b for a, b in zip(total[::2], total[1::2])]
            conv[t] = total[0] + locals_[k][t]
            return tuple(new)

        states = lax.fori_loop(0, rows, step, states, unroll=8)
        for side, ref in enumerate((kept[k], given[k])):
            segment = pair if side == 0 else 1 - pair
            column = pl.multiple_of(segment * seg_len + base, 128)
            for g in range(groups):
                lanes = slice(g * 128, (g + 1) * 128)
                query = ref[0, :, lanes].astype(jnp.float32)
                gated = query * conv[:rows, side * groups + g, :]
                out[lanes, pl.ds(column, rows)] = gated.T.astype(jnp.bfloat16)
        base += rows


def finish(place, order, ends, rate, decay, locals_, kept, given, seg_len):
    n_chunks = len(locals_)
    local = pl.BlockSpec(memory_space=pltpu.VMEM)
    operands = list(ends) + [rate, decay] + list(locals_) + list(kept) + list(given)
    lanes = decay.shape[1:]
    channels = kept[0].shape[2]
    longest = max(k.shape[1] for k in kept)
    return pl.pallas_call(
        functools.partial(finish_kernel, len(ends), n_chunks, seg_len),
        grid_spec=pltpu.PrefetchScalarGridSpec(
            num_scalar_prefetch=2,
            grid=(),
            in_specs=[local] * len(operands),
            out_specs=local,
            scratch_shapes=[pltpu.VMEM((longest,) + lanes, jnp.float32)],
        ),
        out_shape=jax.ShapeDtypeStruct((channels, 2 * seg_len), jnp.bfloat16),
        compiler_params=pltpu.CompilerParams(vmem_limit_bytes=40 * MIB),
        cost_estimate=pl.CostEstimate(
            flops=32 * seg_len * lanes[0] * lanes[1],
            bytes_accessed=seg_len * lanes[0] * lanes[1] * 8,
            transcendentals=0,
        ),
        name="finish",
    )(place, order, *operands)


def per_device(tokens, weight, rate, residue, skip, order):
    seg_len = tokens.shape[0]
    n_ctx = lax.axis_size("ctx")
    seq_len = 2 * n_ctx * seg_len
    pair_index = lax.axis_index("fsdp")
    ctx_index = lax.axis_index("ctx")
    place = jnp.stack([pair_index, ctx_index]).astype(jnp.int32)

    own = weight.transpose(1, 0, 2)
    part = own.shape[1] // n_ctx
    per_part = part // DEPTH
    pieces = {}
    for sub in range(per_part):
        piece = lax.dynamic_slice_in_dim(own, ctx_index * part + sub * DEPTH, DEPTH, 1)
        held = {0: exchanged(piece, "fsdp", 1)}
        bit = n_ctx // 2
        while bit:
            for mask in list(held):
                held[mask | bit] = exchanged(held[mask], "ctx", bit)
            bit //= 2
        for mask in range(n_ctx):
            pieces[mask, sub] = held[mask]
    ordered = [pieces[mask, sub] for mask in range(n_ctx) for sub in range(per_part)]

    channels = rate.shape[0]
    groups = channels // 128

    def spread(values):
        lanes = values.T.reshape(-1, groups, 128)
        return jnp.concatenate([lanes, lanes], axis=1)

    rates = spread(rate)
    decay = jnp.exp(-rates)
    gain = spread(pole_gain(rate, residue, float(seq_len)))
    direct = spread(skip[:, None])[0]

    kept, given, locals_ = [], [], []
    state = jnp.zeros_like(decay)
    base = 0
    for k, rows in enumerate(CHUNKS):
        block = lax.slice_in_dim(tokens, base, base + rows, axis=0)
        base += rows
        whole = lax.all_gather(block, "tp", axis=0, tiled=False)
        if k < 2:
            partial = project(place, whole, own, [], 1, None, False)
            keep, give = project(place, whole, None, ordered, per_part, partial, True)
        else:
            keep, give = project(place, whole, own, ordered, per_part, None, True)
        got = exchanged(give, "fsdp", 1)
        local, state = scan(keep, got, decay, gain, direct, state)
        kept.append(keep)
        given.append(got)
        locals_.append(local)

    ends = [state] + [exchanged(state, "ctx", mask) for mask in range(1, n_ctx)]
    return finish(place, order, ends, rates, decay, locals_, kept, given, seg_len)


def solution(mesh):
    placed = (
        P(("ctx", "fsdp"), "tp"),
        P("fsdp", None, "tp"),
        P(("tp", "fsdp"), None),
        P(("tp", "fsdp"), None),
        P(("tp", "fsdp")),
        P(),
    )
    return jax.shard_map(
        per_device, mesh=mesh, in_specs=placed, out_specs=P(("tp", "fsdp"), "ctx"), check_vma=False
    )
```

```python
import functools
from typing import NamedTuple

import jax
import jax.numpy as jnp
from jax import lax
from jax.experimental import pallas as pl
from jax.experimental.pallas import tpu as pltpu
from jax.sharding import PartitionSpec as P

MIB = 1 << 20
DEPTH = 512
CHUNKS = (256, 256, 256, 128, 128)
HALVES = (1024,)
FAR = (1024,)


class Plan(NamedTuple):
    half_blocks: int
    part_blocks: int
    n_pieces: int


def exchanged(block, axis, mask):
    count = lax.axis_size(axis)
    return lax.ppermute(block, axis, [(i, i ^ mask) for i in range(count)])


def after(value, *others):
    return lax.optimization_barrier((value, *others))[0]


def pole_gain(rate, residue, length):
    return residue * jnp.sqrt(jnp.maximum(-jnp.expm1(-2.0 * rate), 1.0 / length))


def project_kernel(plan, n_inputs, has_init, final, blocks, x_plan, place, *refs):
    refs = list(refs)
    inputs = [refs.pop(0) for _ in range(n_inputs)]
    own = refs.pop(0)
    pieces = [refs.pop(0) for _ in range(plan.n_pieces)]
    init = refs.pop(0) if has_init else None
    outs = [refs.pop(0) for _ in range(2 if final else 1)]
    x_buf, w_buf, x_sem, w_sem = refs[:4]
    acc = refs[4] if final else outs[0]
    pair, ctx, tp = place[0], place[1], place[2]
    slots = x_buf.shape[0]

    def start(step):
        slot = lax.rem(step, slots)
        block = x_plan(tp, step, inputs, x_buf.at[slot], x_sem.at[slot])
        local = lax.rem(block, plan.half_blocks)
        here = lax.div(block, plan.half_blocks) == pair

        @pl.when(here)
        def _():
            row = pl.multiple_of(local * DEPTH, DEPTH)
            pltpu.make_async_copy(
                own.at[:, pl.ds(row, DEPTH), :], w_buf.at[slot], w_sem.at[slot]
            ).start()

        part = lax.div(local, plan.part_blocks)
        number = jnp.bitwise_xor(part, ctx) * plan.part_blocks + lax.rem(local, plan.part_blocks)
        for n in range(len(pieces) // 2):
            @pl.when(jnp.logical_not(here) & (number == n))
            def _():
                for side in (0, 1):
                    pltpu.make_async_copy(
                        pieces[2 * n + side],
                        w_buf.at[slot, :, pl.ds(side * (DEPTH // 2), DEPTH // 2), :],
                        w_sem.at[slot],
                    ).start()

    for ahead in range(min(slots - 1, blocks)):
        start(jnp.int32(ahead))
    if has_init:
        acc[...] = init[...]
    else:
        acc[...] = jnp.zeros_like(acc)

    def body(step, carry):
        slot = lax.rem(step, slots)

        @pl.when(step + slots - 1 < blocks)
        def _():
            start(step + slots - 1)

        pltpu.make_async_copy(x_buf.at[slot], x_buf.at[slot], x_sem.at[slot]).wait()
        pltpu.make_async_copy(w_buf.at[slot], w_buf.at[slot], w_sem.at[slot]).wait()
        block = x_buf[slot]
        for p in range(3):
            acc[p] += jnp.dot(block, w_buf[slot, p], preferred_element_type=jnp.float32)
        return carry

    lax.fori_loop(0, blocks, body, 0)
    if final:
        kept, given = outs
        half = kept.shape[2]
        mine = pl.multiple_of(pair * half, 128)
        other = pl.multiple_of((1 - pair) * half, 128)
        for p in range(3):
            kept[p] = acc[p, :, pl.ds(mine, half)].astype(jnp.bfloat16)
            given[p] = acc[p, :, pl.ds(other, half)].astype(jnp.bfloat16)


def project(plan, place, inputs, own, pieces, init, base, rows, blocks, x_plan, final):
    width = own.shape[2]
    slots = 3
    anywhere = pl.BlockSpec(memory_space=pl.ANY)
    local = pl.BlockSpec(memory_space=pltpu.VMEM)
    operands = list(inputs) + [own] + list(pieces)
    in_specs = [anywhere] * len(operands)
    if init is not None:
        operands.append(init)
        in_specs.append(pl.BlockSpec((3, rows, width), lambda i, place: (0, base // rows, 0)))
    scratch = [
        pltpu.VMEM((slots, rows, DEPTH), jnp.bfloat16),
        pltpu.VMEM((slots, 3, DEPTH, width), jnp.bfloat16),
        pltpu.SemaphoreType.DMA((slots,)),
        pltpu.SemaphoreType.DMA((slots,)),
    ]
    if final:
        scratch.append(pltpu.VMEM((3, rows, width), jnp.float32))
        out_shape = [jax.ShapeDtypeStruct((3, rows, width // 2), jnp.bfloat16)] * 2
        out_specs = [local, local]
    else:
        out_shape = jax.ShapeDtypeStruct((3, rows, width), jnp.float32)
        out_specs = local
    return pl.pallas_call(
        functools.partial(
            project_kernel, plan, len(inputs), init is not None, final, blocks, x_plan
        ),
        grid_spec=pltpu.PrefetchScalarGridSpec(
            num_scalar_prefetch=1,
            grid=(1,),
            in_specs=in_specs,
            out_specs=out_specs,
            scratch_shapes=scratch,
        ),
        out_shape=out_shape,
        compiler_params=pltpu.CompilerParams(vmem_limit_bytes=44 * MIB),
        cost_estimate=pl.CostEstimate(
            flops=0,
            bytes_accessed=0,
            transcendentals=0,
        ),
        name="project",
    )(place, *operands)


def columns(quarter_block):
    return pl.ds(pl.multiple_of(quarter_block * DEPTH, DEPTH), DEPTH)


def gathered_plan(per_quarter):
    def plan(tp, step, inputs, target, sem):
        source = inputs[0].at[lax.div(step, per_quarter), :, columns(lax.rem(step, per_quarter))]
        pltpu.make_async_copy(source, target, sem).start()
        return step

    return plan


def line_ends(tp):
    return (tp == 0) | (tp == 3)


def first_plan(per_quarter, n_halves):
    def plan(tp, step, inputs, target, sem):
        own, near, *rest = inputs
        middle, ends = rest[:n_halves], rest[n_halves:]
        high = lax.div(tp, 2)
        early = step < 2 * per_quarter
        block = jnp.where(
            early,
            high * 2 * per_quarter + step,
            (2 - high) * per_quarter + step - 2 * per_quarter,
        )
        quarter = lax.div(block, per_quarter)
        where = columns(lax.rem(block, per_quarter))

        @pl.when(early & (quarter == tp))
        def _():
            pltpu.make_async_copy(own.at[:, where], target, sem).start()

        @pl.when(early & (quarter != tp))
        def _():
            pltpu.make_async_copy(near.at[:, where], target, sem).start()

        for at_end, sources in ((False, middle), (True, ends)):
            @pl.when(jnp.logical_not(early) & (line_ends(tp) == at_end))
            def _():
                row = 0
                for source in sources:
                    size = source.shape[0]
                    pltpu.make_async_copy(
                        source.at[:, where], target.at[pl.ds(row, size), :], sem
                    ).start()
                    row += size

        return block

    return plan


def last_plan(per_quarter, row, rows):
    def plan(tp, step, inputs, target, sem):
        middle, ends = inputs
        where = columns(step)

        @pl.when(line_ends(tp))
        def _():
            pltpu.make_async_copy(ends.at[:, where], target, sem).start()

        @pl.when(jnp.logical_not(line_ends(tp)))
        def _():
            pltpu.make_async_copy(middle.at[pl.ds(row, rows), where], target, sem).start()

        return jnp.where(tp < 2, 3, 0) * per_quarter + step

    return plan


def scan_kernel(kept, given, decay, gain, skip, state_in, local_ref, state_out, prod):
    poles = decay.shape[0]
    rows = kept.shape[1]
    groups = kept.shape[2] // 128
    for side, ref in enumerate((kept, given)):
        for g in range(groups):
            lanes = slice(g * 128, (g + 1) * 128)
            key = ref[1, :, lanes].astype(jnp.float32)
            value = ref[2, :, lanes].astype(jnp.float32)
            prod[:, side * groups + g, :] = key * value
    direct = skip[...]
    factors = [decay[r] for r in range(poles)]
    gains = [gain[r] for r in range(poles)]

    def step(t, states):
        p = prod[t]
        new = [factors[r] * states[r] + gains[r] * p for r in range(poles)]
        total = list(new)
        while len(total) > 1:
            total = [a + b for a, b in zip(total[::2], total[1::2])]
        local_ref[t] = total[0] + direct * p
        return tuple(new)

    states = lax.fori_loop(0, rows, step, tuple(state_in[r] for r in range(poles)), unroll=8)
    for r in range(poles):
        state_out[r] = states[r]


def scan(kept, given, decay, gain, skip, state):
    rows = kept.shape[1]
    local = pl.BlockSpec(memory_space=pltpu.VMEM)
    lanes = decay.shape[1:]
    return pl.pallas_call(
        scan_kernel,
        in_specs=[local] * 6,
        out_specs=[local] * 2,
        out_shape=[
            jax.ShapeDtypeStruct((rows,) + lanes, jnp.float32),
            jax.ShapeDtypeStruct(decay.shape, jnp.float32),
        ],
        scratch_shapes=[pltpu.VMEM((rows,) + lanes, jnp.float32)],
        compiler_params=pltpu.CompilerParams(vmem_limit_bytes=24 * MIB),
        cost_estimate=pl.CostEstimate(
            flops=0,
            bytes_accessed=0,
            transcendentals=0,
        ),
        name="scan",
    )(kept, given, decay, gain, skip, state)


def finish_kernel(n_ctx, n_chunks, seg_len, place, order, *refs):
    refs = list(refs)
    ends = [refs.pop(0) for _ in range(n_ctx)]
    rate = refs.pop(0)
    decay = refs.pop(0)
    locals_ = [refs.pop(0) for _ in range(n_chunks)]
    kept = [refs.pop(0) for _ in range(n_chunks)]
    given = [refs.pop(0) for _ in range(n_chunks)]
    out = refs.pop(0)
    conv = refs.pop(0)
    poles, sublanes, _ = decay.shape
    groups = sublanes // 2
    pair, ctx = place[0], place[1]
    upper = lax.broadcasted_iota(jnp.int32, decay.shape[1:], 0) < groups
    targets = (order[2 * ctx + pair], order[2 * ctx + 1 - pair])
    states = [jnp.zeros(decay.shape[1:], jnp.float32) for _ in range(poles)]
    for mask in range(n_ctx):
        origin = jnp.bitwise_xor(ctx, mask)
        sources = (order[2 * origin + pair], order[2 * origin + 1 - pair])
        for cross in (0, 1):
            gaps = [targets[s] - 1 - sources[s ^ cross] for s in (0, 1)]
            gap = jnp.where(upper, gaps[0], gaps[1])
            span = jnp.maximum(gap, 0).astype(jnp.float32) * seg_len
            for r in range(poles):
                end = ends[mask][r]
                if cross:
                    end = jnp.concatenate([end[groups:], end[:groups]], axis=0)
                factor = jnp.where(gap >= 0, jnp.exp(-rate[r] * span), 0.0)
                states[r] = states[r] + factor * end
    factors = [decay[r] for r in range(poles)]
    states = tuple(states)
    base = 0
    for k in range(n_chunks):
        rows = locals_[k].shape[0]

        def step(t, states):
            new = [factors[r] * states[r] for r in range(poles)]
            total = list(new)
            while len(total) > 1:
                total = [a + b for a, b in zip(total[::2], total[1::2])]
            conv[t] = total[0] + locals_[k][t]
            return tuple(new)

        states = lax.fori_loop(0, rows, step, states, unroll=8)
        for side, ref in enumerate((kept[k], given[k])):
            segment = pair if side == 0 else 1 - pair
            column = pl.multiple_of(segment * seg_len + base, 128)
            for g in range(groups):
                lanes = slice(g * 128, (g + 1) * 128)
                query = ref[0, :, lanes].astype(jnp.float32)
                gated = query * conv[:rows, side * groups + g, :]
                out[lanes, pl.ds(column, rows)] = gated.T.astype(jnp.bfloat16)
        base += rows


def finish(place, order, ends, rate, decay, locals_, kept, given, seg_len):
    n_chunks = len(locals_)
    local = pl.BlockSpec(memory_space=pltpu.VMEM)
    operands = list(ends) + [rate, decay] + list(locals_) + list(kept) + list(given)
    lanes = decay.shape[1:]
    channels = kept[0].shape[2]
    longest = max(k.shape[1] for k in kept)
    return pl.pallas_call(
        functools.partial(finish_kernel, len(ends), n_chunks, seg_len),
        grid_spec=pltpu.PrefetchScalarGridSpec(
            num_scalar_prefetch=2,
            grid=(),
            in_specs=[local] * len(operands),
            out_specs=local,
            scratch_shapes=[pltpu.VMEM((longest,) + lanes, jnp.float32)],
        ),
        out_shape=jax.ShapeDtypeStruct((channels, 2 * seg_len), jnp.bfloat16),
        compiler_params=pltpu.CompilerParams(vmem_limit_bytes=40 * MIB),
        cost_estimate=pl.CostEstimate(
            flops=32 * seg_len * lanes[0] * lanes[1],
            bytes_accessed=seg_len * lanes[0] * lanes[1] * 8,
            transcendentals=0,
        ),
        name="finish",
    )(place, order, *operands)


def per_device(tokens, weight, rate, residue, skip, order):
    seg_len = tokens.shape[0]
    n_ctx = lax.axis_size("ctx")
    seq_len = 2 * n_ctx * seg_len
    pair_index = lax.axis_index("fsdp")
    ctx_index = lax.axis_index("ctx")
    place = jnp.stack([pair_index, ctx_index, lax.axis_index("tp")]).astype(jnp.int32)

    starts = [sum(CHUNKS[:k]) for k in range(len(CHUNKS))]
    on_line = lax.axis_size("tp") == 4
    passed, arrived = [], []
    if on_line:
        near = lax.ppermute(tokens, "tp", [(0, 1), (1, 0), (2, 3), (3, 2)])
        middle, ends, row = [], [], 0
        for rows in HALVES:
            block = lax.slice_in_dim(tokens, row, row + rows, axis=0)
            middle.append(lax.ppermute(block, "tp", [(1, 2), (2, 1)]))
            ends.append(lax.ppermute(middle[-1], "tp", [(1, 0), (2, 3)]))
            row += rows
        far_middle, row = [], 0
        for rows in FAR:
            block = lax.slice_in_dim(near, row, row + rows, axis=0)
            far_middle.append(lax.ppermute(block, "tp", [(1, 2), (2, 1)]))
            row += rows
        passed = ends + far_middle
        arrived = [near] + middle

    own = weight.transpose(1, 0, 2)
    part = own.shape[1] // n_ctx
    piece_len = DEPTH // 2
    per_part = part // piece_len
    pieces = {}
    bits = []
    while 1 << len(bits) < n_ctx:
        bits.insert(0, 1 << len(bits))
    first = []
    for sub in range(per_part):
        piece = lax.dynamic_slice_in_dim(own, ctx_index * part + sub * piece_len, piece_len, 1)
        if sub >= 2:
            piece = after(piece, first[sub - 2])
        if sub >= 3:
            piece = after(piece, *[pieces[m, sub - 3] for m in range(n_ctx)])
        first.append(exchanged(piece, "fsdp", 1))
        held = {0: first[sub]}
        for bit in bits:
            for mask in list(held):
                block = held[mask]
                if bit == bits[0] and sub:
                    block = after(block, pieces[bit, sub - 1])
                if bit == bits[0] and sub >= 2:
                    block = after(block, *[pieces[m, sub - 2] for m in range(n_ctx)])
                if bit == bits[-1] and sub == per_part - 1:
                    block = after(block, *passed)
                if bit == bits[-1] and mask and sub in (0, per_part - 1):
                    block = after(block, latest)
                latest = exchanged(block, "ctx", bit)
                held[mask | bit] = latest
        for mask in range(n_ctx):
            pieces[mask, sub] = held[mask]
    ordered = [pieces[mask, sub] for mask in range(n_ctx) for sub in range(per_part)]
    plan = Plan(own.shape[1] // DEPTH, part // DEPTH, len(ordered))
    per_quarter = tokens.shape[1] // DEPTH

    channels = rate.shape[0]
    groups = channels // 128

    def spread(values):
        lanes = values.T.reshape(-1, groups, 128)
        return jnp.concatenate([lanes, lanes], axis=1)

    rates = spread(rate)
    decay = jnp.exp(-rates)
    gain = spread(pole_gain(rate, residue, float(seq_len)))
    direct = spread(skip[:, None])[0]

    if on_line:
        far_ends, where = [], []
        for k, (base, rows) in enumerate(zip(starts, CHUNKS)):
            row, n = base, 0
            while row >= FAR[n]:
                row -= FAR[n]
                n += 1
            where.append((n, row))
            block = lax.slice_in_dim(far_middle[n], row, row + rows, axis=0)
            if k >= 3:
                block = after(block, far_ends[k - 3])
            far_ends.append(lax.ppermute(block, "tp", [(1, 0), (2, 3)]))
        near = after(near, *far_middle)
        partial = project(
            plan, place, [tokens, near, *middle, *ends], own, ordered, None, 0, seg_len,
            3 * per_quarter, first_plan(per_quarter, len(HALVES)), False,
        )
    else:
        partial = None

    kept, given, locals_ = [], [], []
    state = jnp.zeros_like(decay)
    states = []
    for k, (base, rows) in enumerate(zip(starts, CHUNKS)):
        if partial is not None:
            last = far_ends[k]
            if k == len(CHUNKS) - 1:
                last = after(last, states[k - 3])
            n, row = where[k]
            keep, give = project(
                plan, place, [far_middle[n], last], own, ordered, partial, base, rows,
                per_quarter, last_plan(per_quarter, row, rows), True,
            )
        else:
            block = lax.slice_in_dim(tokens, base, base + rows, axis=0)
            whole = lax.all_gather(block, "tp", axis=0, tiled=False)
            keep, give = project(
                plan, place, [whole], own, ordered, None, 0, rows,
                2 * plan.half_blocks, gathered_plan(per_quarter), True,
            )
        got = exchanged(give, "fsdp", 1)
        local, state = scan(keep, got, decay, gain, direct, state)
        states.append(state)
        kept.append(keep)
        given.append(got)
        locals_.append(local)

    ends = [state] + [exchanged(state, "ctx", mask) for mask in range(1, n_ctx)]
    return finish(place, order, ends, rates, decay, locals_, kept, given, seg_len)


def solution(mesh):
    placed = (
        P(("ctx", "fsdp"), "tp"),
        P("fsdp", None, "tp"),
        P(("tp", "fsdp"), None),
        P(("tp", "fsdp"), None),
        P(("tp", "fsdp")),
        P(),
    )
    return jax.shard_map(
        per_device, mesh=mesh, in_specs=placed, out_specs=P(("tp", "fsdp"), "ctx"), check_vma=False
    )
```

```python
import functools
from typing import NamedTuple

import jax
import jax.numpy as jnp
from jax import lax
from jax.experimental import pallas as pl
from jax.experimental.pallas import tpu as pltpu
from jax.sharding import PartitionSpec as P

MIB = 1 << 20
DEPTH = 512
CHUNKS = (256, 256, 256, 128, 128)
PASSED = (1024,)
T = {'y_y': True, 'y3_c0': True, 'y2_A': False, 'x_x': [0, 1, 1, 1], 'x_c': [0, 0, 1, 1], 'Ka': 'c3', 'x2_A': False, 'c_A': 9, 'c_P': [3], 'x_P': [], 'c_ser': [1, 0, 0, 1], 'copy': None, 'E': {2: 0, 3: 1, 4: 2}, 'S': {3: 0, 4: 1}}
FREE = pl.CostEstimate(flops=0, bytes_accessed=0, transcendentals=0)


class Plan(NamedTuple):
    half_blocks: int
    part_blocks: int
    n_pieces: int


def exchanged(block, axis, mask):
    count = lax.axis_size(axis)
    return lax.ppermute(block, axis, [(i, i ^ mask) for i in range(count)])


def after(value, *others):
    return lax.optimization_barrier((value, *others))[0]


def pole_gain(rate, residue, length):
    return residue * jnp.sqrt(jnp.maximum(-jnp.expm1(-2.0 * rate), 1.0 / length))


def fetch_weights(plan, place, block, own, pieces, stride, target, sem):
    pair, ctx = place[0], place[1]
    local = lax.rem(block, plan.half_blocks)
    here = lax.div(block, plan.half_blocks) == pair

    @pl.when(here)
    def _():
        row = pl.multiple_of(local * DEPTH, DEPTH)
        pltpu.make_async_copy(own.at[:, pl.ds(row, DEPTH), :], target, sem).start()

    number = jnp.bitwise_xor(lax.div(local, plan.part_blocks), ctx)
    if stride == 1:
        number = number * plan.part_blocks + lax.rem(local, plan.part_blocks)
    for n in range(len(pieces) // 2):
        @pl.when(jnp.logical_not(here) & (number == n))
        def _():
            for side in (0, 1):
                rows = pl.ds(side * (DEPTH // 2), DEPTH // 2)
                pltpu.make_async_copy(pieces[2 * n + side], target.at[:, rows, :], sem).start()


def project_kernel(plan, n_inputs, stride, base, final, blocks, x_plan, place, *refs):
    refs = list(refs)
    inputs = [refs.pop(0) for _ in range(n_inputs)]
    own = refs.pop(0)
    pieces = [refs.pop(0) for _ in range(plan.n_pieces // stride)]
    init = refs.pop(0) if base is not None else None
    outs = [refs.pop(0) for _ in range(2 if final else 1)]
    x_buf, w_buf, x_sem, w_sem, acc_sem = refs[:5]
    acc = refs[5] if final else outs[0]
    pair, tp = place[0], place[2]
    slots = x_buf.shape[0]

    def start(step):
        slot = lax.rem(step, slots)
        block = x_plan(tp, step, inputs, x_buf.at[slot], x_sem.at[slot])
        fetch_weights(
            plan, place, block, own, pieces, stride, w_buf.at[slot], w_sem.at[slot]
        )

    if init is not None:
        pltpu.make_async_copy(init.at[:, pl.ds(base, acc.shape[1]), :], acc, acc_sem).start()
    for ahead in range(min(slots - 1, blocks)):
        start(jnp.int32(ahead))
    if init is None:
        acc[...] = jnp.zeros_like(acc)
    else:
        pltpu.make_async_copy(acc, acc, acc_sem).wait()

    def body(step, carry):
        slot = lax.rem(step, slots)

        @pl.when(step + slots - 1 < blocks)
        def _():
            start(step + slots - 1)

        pltpu.make_async_copy(x_buf.at[slot], x_buf.at[slot], x_sem.at[slot]).wait()
        pltpu.make_async_copy(w_buf.at[slot], w_buf.at[slot], w_sem.at[slot]).wait()
        block = x_buf[slot]
        for p in range(3):
            acc[p] += jnp.dot(block, w_buf[slot, p], preferred_element_type=jnp.float32)
        return carry

    lax.fori_loop(0, blocks, body, 0)
    if not final:
        return
    kept, given = outs
    half = kept.shape[2]
    mine = pl.multiple_of(pair * half, 128)
    other = pl.multiple_of((1 - pair) * half, 128)
    for p in range(3):
        kept[p] = acc[p, :, pl.ds(mine, half)].astype(jnp.bfloat16)
        given[p] = acc[p, :, pl.ds(other, half)].astype(jnp.bfloat16)


def project(plan, place, inputs, own, pieces, stride, init, base, rows, blocks, x_plan, final):
    width = own.shape[2]
    slots = 4 if final else 3
    anywhere = pl.BlockSpec(memory_space=pl.ANY)
    local = pl.BlockSpec(memory_space=pltpu.VMEM)
    operands = list(inputs) + [own] + list(pieces) + ([] if init is None else [init])
    total = (3, rows, width)
    scratch = [
        pltpu.VMEM((slots, rows, DEPTH), jnp.bfloat16),
        pltpu.VMEM((slots, 3, DEPTH, width), jnp.bfloat16),
        pltpu.SemaphoreType.DMA((slots,)),
        pltpu.SemaphoreType.DMA((slots,)),
        pltpu.SemaphoreType.DMA,
    ]
    out_shape = jax.ShapeDtypeStruct(total, jnp.float32)
    if final:
        scratch.append(pltpu.VMEM(total, jnp.float32))
        out_shape = [jax.ShapeDtypeStruct((3, rows, width // 2), jnp.bfloat16)] * 2
    return pl.pallas_call(
        functools.partial(
            project_kernel, plan, len(inputs), stride, None if init is None else base, final,
            blocks, x_plan,
        ),
        grid_spec=pltpu.PrefetchScalarGridSpec(
            num_scalar_prefetch=1,
            grid=(),
            in_specs=[anywhere] * len(operands),
            out_specs=[local, local] if final else local,
            scratch_shapes=scratch,
        ),
        out_shape=out_shape,
        compiler_params=pltpu.CompilerParams(vmem_limit_bytes=30 * MIB),
        cost_estimate=FREE,
        name="project" if final else "project_part",
    )(place, *operands)


def columns(quarter_block):
    return pl.ds(pl.multiple_of(quarter_block * DEPTH, DEPTH), DEPTH)


def gathered_plan(per_quarter):
    def plan(tp, step, inputs, target, sem):
        source = inputs[0].at[lax.div(step, per_quarter), :, columns(lax.rem(step, per_quarter))]
        pltpu.make_async_copy(source, target, sem).start()
        return step

    return plan


def line_ends(tp):
    return (tp == 0) | (tp == 3)


def near_block(plan, tp, step, number, base, inputs, target, sem):
    span = plan.half_blocks // 2 // plan.part_blocks
    mine = step < span
    side = jnp.where(mine, lax.rem(tp, 2), 1 - lax.rem(tp, 2))
    within = lax.rem(step, span)
    where = columns(within * plan.part_blocks + number)
    for at, source in ((True, inputs[0]), (False, inputs[1])):
        @pl.when(mine == at)
        def _():
            rows = pl.ds(base, target.shape[0])
            pltpu.make_async_copy(source.at[rows, where], target, sem).start()

    part = side * span + within
    return lax.div(tp, 2) * plan.half_blocks + part * plan.part_blocks + number


def near_plan(plan, number, base):
    def x_plan(tp, step, inputs, target, sem):
        return near_block(plan, tp, step, number, base, inputs, target, sem)

    return x_plan


def middle_plan(plan, number, base, segments):
    span = plan.half_blocks // plan.part_blocks
    per_quarter = plan.half_blocks // 2

    def x_plan(tp, step, inputs, target, sem):
        middle, ends = inputs[2], inputs[3:]
        late = step - span
        where = columns(jnp.maximum(late, 0))

        @pl.when(step < span)
        def _():
            near_block(plan, tp, step, number, base, inputs, target, sem)

        @pl.when((late >= 0) & jnp.logical_not(line_ends(tp)))
        def _():
            rows = pl.ds(base, target.shape[0])
            pltpu.make_async_copy(middle.at[rows, where], target, sem).start()

        @pl.when((late >= 0) & line_ends(tp))
        def _():
            row = 0
            for source, (first, size) in zip(ends, segments):
                pltpu.make_async_copy(
                    source.at[pl.ds(first, size), where], target.at[pl.ds(row, size), :], sem
                ).start()
                row += size

        half = span // 2
        side = jnp.where(step < half, lax.rem(tp, 2), 1 - lax.rem(tp, 2))
        part = side * half + lax.rem(step, half)
        near = lax.div(tp, 2) * plan.half_blocks + part * plan.part_blocks + number
        return jnp.where(late < 0, near, (2 - lax.div(tp, 2)) * per_quarter + late)

    return x_plan


def last_plan(per_quarter, row, rows):
    def plan(tp, step, inputs, target, sem):
        middle, ends = inputs
        where = columns(step)

        @pl.when(line_ends(tp))
        def _():
            pltpu.make_async_copy(ends.at[:, where], target, sem).start()

        @pl.when(jnp.logical_not(line_ends(tp)))
        def _():
            pltpu.make_async_copy(middle.at[pl.ds(row, rows), where], target, sem).start()

        return jnp.where(tp < 2, 3, 0) * per_quarter + step

    return plan


def scan_kernel(kept, given, decay, gain, skip, state_in, local_ref, state_out, prod):
    poles = decay.shape[0]
    rows = kept.shape[1]
    groups = kept.shape[2] // 128
    for side, ref in enumerate((kept, given)):
        for g in range(groups):
            lanes = slice(g * 128, (g + 1) * 128)
            key = ref[1, :, lanes].astype(jnp.float32)
            value = ref[2, :, lanes].astype(jnp.float32)
            prod[:, side * groups + g, :] = key * value
    direct = skip[...]
    factors = [decay[r] for r in range(poles)]
    gains = [gain[r] for r in range(poles)]

    def step(t, states):
        p = prod[t]
        new = [factors[r] * states[r] + gains[r] * p for r in range(poles)]
        total = list(new)
        while len(total) > 1:
            total = [a + b for a, b in zip(total[::2], total[1::2])]
        local_ref[t] = total[0] + direct * p
        return tuple(new)

    states = lax.fori_loop(0, rows, step, tuple(state_in[r] for r in range(poles)), unroll=8)
    for r in range(poles):
        state_out[r] = states[r]


def scan(kept, given, decay, gain, skip, state):
    rows = kept.shape[1]
    local = pl.BlockSpec(memory_space=pltpu.VMEM)
    lanes = decay.shape[1:]
    return pl.pallas_call(
        scan_kernel,
        in_specs=[local] * 6,
        out_specs=[local] * 2,
        out_shape=[
            jax.ShapeDtypeStruct((rows,) + lanes, jnp.float32),
            jax.ShapeDtypeStruct(decay.shape, jnp.float32),
        ],
        scratch_shapes=[pltpu.VMEM((rows,) + lanes, jnp.float32)],
        compiler_params=pltpu.CompilerParams(vmem_limit_bytes=24 * MIB),
        cost_estimate=FREE,
        name="scan",
    )(kept, given, decay, gain, skip, state)


def finish_kernel(n_ctx, n_chunks, seg_len, place, order, *refs):
    refs = list(refs)
    ends = [refs.pop(0) for _ in range(n_ctx)]
    rate = refs.pop(0)
    decay = refs.pop(0)
    locals_ = [refs.pop(0) for _ in range(n_chunks)]
    kept = [refs.pop(0) for _ in range(n_chunks)]
    given = [refs.pop(0) for _ in range(n_chunks)]
    out = refs.pop(0)
    conv = refs.pop(0)
    poles, sublanes, _ = decay.shape
    groups = sublanes // 2
    pair, ctx = place[0], place[1]
    upper = lax.broadcasted_iota(jnp.int32, decay.shape[1:], 0) < groups
    targets = (order[2 * ctx + pair], order[2 * ctx + 1 - pair])
    states = [jnp.zeros(decay.shape[1:], jnp.float32) for _ in range(poles)]
    for mask in range(n_ctx):
        origin = jnp.bitwise_xor(ctx, mask)
        sources = (order[2 * origin + pair], order[2 * origin + 1 - pair])
        for cross in (0, 1):
            gaps = [targets[s] - 1 - sources[s ^ cross] for s in (0, 1)]
            gap = jnp.where(upper, gaps[0], gaps[1])
            span = jnp.maximum(gap, 0).astype(jnp.float32) * seg_len
            for r in range(poles):
                end = ends[mask][r]
                if cross:
                    end = jnp.concatenate([end[groups:], end[:groups]], axis=0)
                factor = jnp.where(gap >= 0, jnp.exp(-rate[r] * span), 0.0)
                states[r] = states[r] + factor * end
    factors = [decay[r] for r in range(poles)]
    states = tuple(states)
    base = 0
    for k in range(n_chunks):
        rows = locals_[k].shape[0]

        def step(t, states):
            new = [factors[r] * states[r] for r in range(poles)]
            total = list(new)
            while len(total) > 1:
                total = [a + b for a, b in zip(total[::2], total[1::2])]
            conv[t] = total[0] + locals_[k][t]
            return tuple(new)

        states = lax.fori_loop(0, rows, step, states, unroll=8)
        for side, ref in enumerate((kept[k], given[k])):
            segment = pair if side == 0 else 1 - pair
            column = pl.multiple_of(segment * seg_len + base, 128)
            for g in range(groups):
                lanes = slice(g * 128, (g + 1) * 128)
                query = ref[0, :, lanes].astype(jnp.float32)
                gated = query * conv[:rows, side * groups + g, :]
                out[lanes, pl.ds(column, rows)] = gated.T.astype(jnp.bfloat16)
        base += rows


def finish(place, order, ends, rate, decay, locals_, kept, given, seg_len):
    n_chunks = len(locals_)
    local = pl.BlockSpec(memory_space=pltpu.VMEM)
    operands = list(ends) + [rate, decay] + list(locals_) + list(kept) + list(given)
    lanes = decay.shape[1:]
    channels = kept[0].shape[2]
    longest = max(k.shape[1] for k in kept)
    return pl.pallas_call(
        functools.partial(finish_kernel, len(ends), n_chunks, seg_len),
        grid_spec=pltpu.PrefetchScalarGridSpec(
            num_scalar_prefetch=2,
            grid=(),
            in_specs=[local] * len(operands),
            out_specs=local,
            scratch_shapes=[pltpu.VMEM((longest,) + lanes, jnp.float32)],
        ),
        out_shape=jax.ShapeDtypeStruct((channels, 2 * seg_len), jnp.bfloat16),
        compiler_params=pltpu.CompilerParams(vmem_limit_bytes=40 * MIB),
        cost_estimate=pl.CostEstimate(
            flops=32 * seg_len * lanes[0] * lanes[1],
            bytes_accessed=seg_len * lanes[0] * lanes[1] * 8,
            transcendentals=0,
        ),
        name="finish",
    )(place, order, *operands)


def per_device(tokens, weight, rate, residue, skip, order):
    seg_len = tokens.shape[0]
    n_ctx = lax.axis_size("ctx")
    seq_len = 2 * n_ctx * seg_len
    pair_index = lax.axis_index("fsdp")
    ctx_index = lax.axis_index("ctx")
    place = jnp.stack([pair_index, ctx_index, lax.axis_index("tp")]).astype(jnp.int32)

    starts = [sum(CHUNKS[:k]) for k in range(len(CHUNKS))]
    on_line = lax.axis_size("tp") == 4 and n_ctx == 4
    passed = []
    if on_line:
        near = lax.ppermute(tokens, "tp", [(0, 1), (1, 0), (2, 3), (3, 2)])
        middle = lax.ppermute(tokens, "tp", [(1, 2), (2, 1)])
        ends, far_middle, row = [], [], 0
        for rows in PASSED:
            if T["copy"] is None:
                block = lax.slice_in_dim(middle, row, row + rows, axis=0)
                far = lax.slice_in_dim(near, row, row + rows, axis=0)
            else:
                block, far = take_rows(row, rows, middle, near)
            ends.append(lax.ppermute(block, "tp", [(1, 0), (2, 3)]))
            far_middle.append(lax.ppermute(far, "tp", [(1, 2), (2, 1)]))
            row += rows
        passed = [ends[0], far_middle[0]]

    own = weight.transpose(1, 0, 2)
    part = own.shape[1] // n_ctx
    piece_len = DEPTH // 2
    per_part = part // piece_len
    plan = Plan(own.shape[1] // DEPTH, part // DEPTH, n_ctx * per_part)
    per_quarter = tokens.shape[1] // DEPTH
    partials = [None]

    def add_part():
        some = [pieces[m, n] for m in range(n_ctx) for n in (0, 1)]
        return project(
            plan, place, [tokens, near], own, some, plan.part_blocks, None, 0, seg_len,
            plan.half_blocks // plan.part_blocks, near_plan(plan, 0, 0), False,
        )

    pieces = {}
    bits = []
    while 1 << len(bits) < n_ctx:
        bits.insert(0, 1 << len(bits))
    first = []
    for sub in range(per_part):
        piece = lax.dynamic_slice_in_dim(own, ctx_index * part + sub * piece_len, piece_len, 1)
        if sub >= 2 and T["y_y"]:
            piece = after(piece, first[sub - 2])
        if sub == 3 and T["y3_c0"]:
            piece = after(piece, *[pieces[m, 0] for m in range(n_ctx)])
        if sub == 2 and T["y2_A"] and on_line:
            piece = after(piece, near, middle)
        first.append(exchanged(piece, "fsdp", 1))
        held = {0: first[sub]}
        for bit in bits:
            for mask in list(held):
                block = held[mask]
                if bit == bits[0] and sub and T["x_x"][sub]:
                    block = after(block, pieces[bit, sub - 1])
                if bit == bits[0] and sub >= 2 and T["x_c"][sub]:
                    block = after(block, *[pieces[m, sub - 2] for m in range(n_ctx)])
                if on_line:
                    if bit == bits[0] and sub == 3 and T["Ka"] == "x3":
                        block = after(block, partials[1])
                    if bit == bits[-1] and T["Ka"] == "c%d" % sub:
                        block = after(block, partials[1])
                    if bit == bits[0] and sub == 2 and T["x2_A"]:
                        block = after(block, near, middle)
                    if bit == bits[-1] and T["c_A"] == sub:
                        block = after(block, near, middle)
                    if bit == bits[-1] and sub in T["c_P"]:
                        block = after(block, *passed)
                    if bit == bits[0] and sub in T["x_P"]:
                        block = after(block, *passed)
                if bit == bits[-1] and mask and T["c_ser"][sub]:
                    block = after(block, latest)
                latest = exchanged(block, "ctx", bit)
                held[mask | bit] = latest
        for mask in range(n_ctx):
            pieces[mask, sub] = held[mask]
        if sub == 1 and on_line:
            partials.append(add_part())
    ordered = [pieces[mask, sub] for mask in range(n_ctx) for sub in range(per_part)]

    channels = rate.shape[0]
    groups = channels // 128

    def spread(values):
        lanes = values.T.reshape(-1, groups, 128)
        return jnp.concatenate([lanes, lanes], axis=1)

    rates = spread(rate)
    decay = jnp.exp(-rates)
    gain = spread(pole_gain(rate, residue, float(seq_len)))
    direct = spread(skip[:, None])[0]

    if on_line:
        far_ends, where = [], []
        for k, (base, rows) in enumerate(zip(starts, CHUNKS)):
            row, n = base, 0
            while row >= PASSED[n]:
                row -= PASSED[n]
                n += 1
            where.append((n, row))
            block = lax.slice_in_dim(far_middle[n], row, row + rows, axis=0)
            if k in T["E"]:
                block = after(block, far_ends[T["E"][k]])
            far_ends.append(lax.ppermute(block, "tp", [(1, 0), (2, 3)]))
        segments = {1024: (((0, 512),), ((512, 512),)), 768: (((0, 512),), ((512, 256), (0, 256)))}[PASSED[0]]
        halves = []

        def add_half(h):
            sources = [tokens, near, middle] + ends[: len(segments[h])]
            return project(
                plan, place, sources, own, ordered, 1, partials[-1], h * 512, 512,
                plan.half_blocks // plan.part_blocks + plan.half_blocks // 2,
                middle_plan(plan, 1, h * 512, segments[h]), False,
            )


    kept, given, locals_ = [], [], []
    state = jnp.zeros_like(decay)
    states = []
    for k, (base, rows) in enumerate(zip(starts, CHUNKS)):
        if on_line:
            last = far_ends[k]
            if base % 512 == 0:
                halves.append(add_half(base // 512))
            if k in T["S"]:
                last = after(last, states[T["S"][k]])
            n, row = where[k]
            keep, give = project(
                plan, place, [far_middle[n], last], own, ordered, 1, halves[-1], base % 512, rows,
                per_quarter, last_plan(per_quarter, row, rows), True,
            )
        else:
            block = lax.slice_in_dim(tokens, base, base + rows, axis=0)
            whole = lax.all_gather(block, "tp", axis=0, tiled=False)
            keep, give = project(
                plan, place, [whole], own, ordered, 1, None, 0, rows,
                2 * plan.half_blocks, gathered_plan(per_quarter), True,
            )
        got = exchanged(give, "fsdp", 1)
        local, state = scan(keep, got, decay, gain, direct, state)
        states.append(state)
        kept.append(keep)
        given.append(got)
        locals_.append(local)

    ends = [state] + [exchanged(state, "ctx", mask) for mask in range(1, n_ctx)]
    return finish(place, order, ends, rates, decay, locals_, kept, given, seg_len)


def solution(mesh):
    placed = (
        P(("ctx", "fsdp"), "tp"),
        P("fsdp", None, "tp"),
        P(("tp", "fsdp"), None),
        P(("tp", "fsdp"), None),
        P(("tp", "fsdp")),
        P(),
    )
    return jax.shard_map(
        per_device, mesh=mesh, in_specs=placed, out_specs=P(("tp", "fsdp"), "ctx"), check_vma=False
    )
```

```python
import functools
from typing import NamedTuple

import jax
import jax.numpy as jnp
from jax import lax
from jax.experimental import pallas as pl
from jax.experimental.pallas import tpu as pltpu
from jax.sharding import PartitionSpec as P

MIB = 1 << 20
DEPTH = 512
CHUNKS = (256, 256, 256, 128, 128)
PASSED = (1024,)
T = {'y_y': True, 'y3_c0': True, 'y2_A': False, 'x_x': [0, 1, 1, 1], 'x_c': [0, 0, 1, 1], 'Ka': 'c3', 'x2_A': False, 'c_A': 9, 'c_P': [3], 'x_P': [], 'c_ser': [1, 0, 0, 1], 'E': [0, 1], 'S': {3: 0, 4: 1}, 'cK': 0, 'cP': 0}
FREE = pl.CostEstimate(flops=0, bytes_accessed=0, transcendentals=0)


class Plan(NamedTuple):
    half_blocks: int
    part_blocks: int
    n_pieces: int


def exchanged(block, axis, mask):
    count = lax.axis_size(axis)
    return lax.ppermute(block, axis, [(i, i ^ mask) for i in range(count)])


def after(value, *others):
    return lax.optimization_barrier((value, *others))[0]


def pole_gain(rate, residue, length):
    return residue * jnp.sqrt(jnp.maximum(-jnp.expm1(-2.0 * rate), 1.0 / length))


def fetch_weights(plan, place, p, block, own, pieces, stride, target, sem):
    pair, ctx = place[0], place[1]
    local = lax.rem(block, plan.half_blocks)
    here = lax.div(block, plan.half_blocks) == pair

    @pl.when(here)
    def _():
        row = pl.multiple_of(local * DEPTH, DEPTH)
        pltpu.make_async_copy(own.at[p, pl.ds(row, DEPTH), :], target, sem).start()

    number = jnp.bitwise_xor(lax.div(local, plan.part_blocks), ctx)
    if stride == 1:
        number = number * plan.part_blocks + lax.rem(local, plan.part_blocks)
    for n in range(len(pieces) // 2):
        @pl.when(jnp.logical_not(here) & (number == n))
        def _():
            for side in (0, 1):
                rows = pl.ds(side * (DEPTH // 2), DEPTH // 2)
                pltpu.make_async_copy(pieces[2 * n + side].at[p], target.at[rows, :], sem).start()


def project_kernel(plan, n_inputs, stride, base, final, blocks, x_plan, place, *refs):
    refs = list(refs)
    inputs = [refs.pop(0) for _ in range(n_inputs)]
    own = refs.pop(0)
    pieces = [refs.pop(0) for _ in range(plan.n_pieces // stride)]
    init = refs.pop(0) if base is not None else None
    outs = [refs.pop(0) for _ in range(2 if final else 1)]
    x_buf, w_buf, x_sem, w_sem = refs[:4]
    if init is not None:
        i_buf, i_sem = refs[4:6]
    pair, tp = place[0], place[2]
    rows = x_buf.shape[0]

    def fetch(p):
        if init is not None:
            pltpu.make_async_copy(
                init.at[p, pl.ds(base, rows), :], i_buf.at[p], i_sem.at[p]
            ).start()

        def one(step, carry):
            depth = pl.ds(pl.multiple_of(step * DEPTH, DEPTH), DEPTH)
            block = x_plan(tp, step, inputs, x_buf.at[:, depth], x_sem, p == 0)
            fetch_weights(
                plan, place, p, block, own, pieces, stride, w_buf.at[p, depth, :], w_sem.at[p]
            )
            return carry

        lax.fori_loop(0, blocks, one, 0)

    fetch(0)
    fetch(1)
    pltpu.make_async_copy(x_buf, x_buf, x_sem).wait()
    for p in range(3):
        pltpu.make_async_copy(w_buf.at[p], w_buf.at[p], w_sem.at[p]).wait()
        if init is not None:
            pltpu.make_async_copy(i_buf.at[p], i_buf.at[p], i_sem.at[p]).wait()
        if p == 0:
            fetch(2)
        if not final:
            chunk = min(rows, 256)

            def multiply(m, carry):
                some = pl.ds(pl.multiple_of(m * chunk, chunk), chunk)
                new = jnp.dot(x_buf[some, :], w_buf[p], preferred_element_type=jnp.float32)
                outs[0][p, some, :] = new if init is None else i_buf[p, some, :] + new
                return carry

            lax.fori_loop(0, rows // chunk, multiply, 0)
            continue
        kept, given = outs
        half = kept.shape[2]
        for mine, out in ((True, kept), (False, given)):
            lanes = pl.ds(pl.multiple_of((pair if mine else 1 - pair) * half, 128), half)
            new = jnp.dot(x_buf[...], w_buf[p, :, lanes], preferred_element_type=jnp.float32)
            if init is not None:
                new = i_buf[p, :, lanes] + new
            new = new.astype(jnp.bfloat16)
            if mine or p == 0:
                out[p] = new
            elif p == 1:
                out[1] = new
            else:
                product = out[1].astype(jnp.float32) * new.astype(jnp.float32)
                out[1] = product.astype(jnp.bfloat16)


def project(plan, place, inputs, own, pieces, stride, init, base, rows, blocks, x_plan, final):
    width = own.shape[2]
    anywhere = pl.BlockSpec(memory_space=pl.ANY)
    local = pl.BlockSpec(memory_space=pltpu.VMEM)
    operands = list(inputs) + [own] + list(pieces) + ([] if init is None else [init])
    depth = blocks * DEPTH
    scratch = [
        pltpu.VMEM((rows, depth), jnp.bfloat16),
        pltpu.VMEM((3, depth, width), jnp.bfloat16),
        pltpu.SemaphoreType.DMA,
        pltpu.SemaphoreType.DMA((3,)),
    ]
    if init is not None:
        scratch.append(pltpu.VMEM((3, rows, width), jnp.float32))
        scratch.append(pltpu.SemaphoreType.DMA((3,)))
    out_shape = jax.ShapeDtypeStruct((3, rows, width), jnp.float32)
    if final:
        out_shape = [
            jax.ShapeDtypeStruct((n, rows, width // 2), jnp.bfloat16) for n in (3, 2)
        ]
    return pl.pallas_call(
        functools.partial(
            project_kernel, plan, len(inputs), stride, None if init is None else base, final,
            blocks, x_plan,
        ),
        grid_spec=pltpu.PrefetchScalarGridSpec(
            num_scalar_prefetch=1,
            grid=(),
            in_specs=[anywhere] * len(operands),
            out_specs=[local, local] if final else local,
            scratch_shapes=scratch,
        ),
        out_shape=out_shape,
        compiler_params=pltpu.CompilerParams(vmem_limit_bytes=56 * MIB),
        cost_estimate=pl.CostEstimate(
            flops=T["cP"] if final else T["cK"], bytes_accessed=0, transcendentals=0
        ),
        name="project" if final else "project_part",
    )(place, *operands)


def columns(quarter_block):
    return pl.ds(pl.multiple_of(quarter_block * DEPTH, DEPTH), DEPTH)


def gathered_plan(per_quarter):
    def plan(tp, step, inputs, target, sem, copy):
        source = inputs[0].at[lax.div(step, per_quarter), :, columns(lax.rem(step, per_quarter))]
        if copy:
            pltpu.make_async_copy(source, target, sem).start()
        return step

    return plan


def line_ends(tp):
    return (tp == 0) | (tp == 3)


def near_block(plan, tp, step, number, base, inputs, target, sem, copy):
    span = plan.half_blocks // 2 // plan.part_blocks
    mine = step < span
    side = jnp.where(mine, lax.rem(tp, 2), 1 - lax.rem(tp, 2))
    within = lax.rem(step, span)
    where = columns(within * plan.part_blocks + number)
    part = side * span + within
    block = lax.div(tp, 2) * plan.half_blocks + part * plan.part_blocks + number
    if not copy:
        return block
    for at, source in ((True, inputs[0]), (False, inputs[1])):
        @pl.when(mine == at)
        def _():
            rows = pl.ds(base, target.shape[0])
            pltpu.make_async_copy(source.at[rows, where], target, sem).start()

    return block


def near_plan(plan, number, base):
    def x_plan(tp, step, inputs, target, sem, copy):
        return near_block(plan, tp, step, number, base, inputs, target, sem, copy)

    return x_plan


def middle_plan(plan, number, base, segments):
    span = plan.half_blocks // plan.part_blocks
    per_quarter = plan.half_blocks // 2

    def x_plan(tp, step, inputs, target, sem, copy):
        middle, ends = inputs[2], inputs[3:]
        late = step - span
        half = span // 2
        side = jnp.where(step < half, lax.rem(tp, 2), 1 - lax.rem(tp, 2))
        part = side * half + lax.rem(step, half)
        near = lax.div(tp, 2) * plan.half_blocks + part * plan.part_blocks + number
        block = jnp.where(late < 0, near, (2 - lax.div(tp, 2)) * per_quarter + late)
        if not copy:
            return block
        where = columns(jnp.maximum(late, 0))

        @pl.when(step < span)
        def _():
            near_block(plan, tp, step, number, base, inputs, target, sem, copy)

        @pl.when((late >= 0) & jnp.logical_not(line_ends(tp)))
        def _():
            rows = pl.ds(base, target.shape[0])
            pltpu.make_async_copy(middle.at[rows, where], target, sem).start()

        @pl.when((late >= 0) & line_ends(tp))
        def _():
            row = 0
            for source, (first, size) in zip(ends, segments):
                pltpu.make_async_copy(
                    source.at[pl.ds(first, size), where], target.at[pl.ds(row, size), :], sem
                ).start()
                row += size

        return block

    return x_plan


def last_plan(per_quarter, row, rows):
    def plan(tp, step, inputs, target, sem, copy):
        block = jnp.where(tp < 2, 3, 0) * per_quarter + step
        if not copy:
            return block
        middle, ends = inputs
        where = columns(step)

        @pl.when(line_ends(tp))
        def _():
            pltpu.make_async_copy(ends.at[:, where], target, sem).start()

        @pl.when(jnp.logical_not(line_ends(tp)))
        def _():
            pltpu.make_async_copy(middle.at[pl.ds(row, rows), where], target, sem).start()

        return block

    return plan


def scan_kernel(kept, given, decay, gain, skip, state_in, local_ref, state_out, prod):
    poles = decay.shape[0]
    rows = kept.shape[1]
    groups = kept.shape[2] // 128
    for side, ref in enumerate((kept, given)):
        for g in range(groups):
            lanes = slice(g * 128, (g + 1) * 128)
            product = ref[1, :, lanes].astype(jnp.float32)
            if side == 0:
                product = product * ref[2, :, lanes].astype(jnp.float32)
            prod[:, side * groups + g, :] = product
    direct = skip[...]
    factors = [decay[r] for r in range(poles)]
    gains = [gain[r] for r in range(poles)]

    def step(t, states):
        p = prod[t]
        new = [factors[r] * states[r] + gains[r] * p for r in range(poles)]
        total = list(new)
        while len(total) > 1:
            total = [a + b for a, b in zip(total[::2], total[1::2])]
        local_ref[t] = total[0] + direct * p
        return tuple(new)

    states = lax.fori_loop(0, rows, step, tuple(state_in[r] for r in range(poles)), unroll=8)
    for r in range(poles):
        state_out[r] = states[r]


def scan(kept, given, decay, gain, skip, state):
    rows = kept.shape[1]
    local = pl.BlockSpec(memory_space=pltpu.VMEM)
    lanes = decay.shape[1:]
    return pl.pallas_call(
        scan_kernel,
        in_specs=[local] * 6,
        out_specs=[local] * 2,
        out_shape=[
            jax.ShapeDtypeStruct((rows,) + lanes, jnp.float32),
            jax.ShapeDtypeStruct(decay.shape, jnp.float32),
        ],
        scratch_shapes=[pltpu.VMEM((rows,) + lanes, jnp.float32)],
        compiler_params=pltpu.CompilerParams(vmem_limit_bytes=24 * MIB),
        cost_estimate=FREE,
        name="scan",
    )(kept, given, decay, gain, skip, state)


def finish_kernel(n_ctx, n_chunks, seg_len, place, order, *refs):
    refs = list(refs)
    ends = [refs.pop(0) for _ in range(n_ctx)]
    rate = refs.pop(0)
    decay = refs.pop(0)
    locals_ = [refs.pop(0) for _ in range(n_chunks)]
    kept = [refs.pop(0) for _ in range(n_chunks)]
    given = [refs.pop(0) for _ in range(n_chunks)]
    out = refs.pop(0)
    conv = refs.pop(0)
    poles, sublanes, _ = decay.shape
    groups = sublanes // 2
    pair, ctx = place[0], place[1]
    upper = lax.broadcasted_iota(jnp.int32, decay.shape[1:], 0) < groups
    targets = (order[2 * ctx + pair], order[2 * ctx + 1 - pair])
    states = [jnp.zeros(decay.shape[1:], jnp.float32) for _ in range(poles)]
    for mask in range(n_ctx):
        origin = jnp.bitwise_xor(ctx, mask)
        sources = (order[2 * origin + pair], order[2 * origin + 1 - pair])
        for cross in (0, 1):
            gaps = [targets[s] - 1 - sources[s ^ cross] for s in (0, 1)]
            gap = jnp.where(upper, gaps[0], gaps[1])
            span = jnp.maximum(gap, 0).astype(jnp.float32) * seg_len
            for r in range(poles):
                end = ends[mask][r]
                if cross:
                    end = jnp.concatenate([end[groups:], end[:groups]], axis=0)
                factor = jnp.where(gap >= 0, jnp.exp(-rate[r] * span), 0.0)
                states[r] = states[r] + factor * end
    factors = [decay[r] for r in range(poles)]
    states = tuple(states)
    base = 0
    for k in range(n_chunks):
        rows = locals_[k].shape[0]

        def step(t, states):
            new = [factors[r] * states[r] for r in range(poles)]
            total = list(new)
            while len(total) > 1:
                total = [a + b for a, b in zip(total[::2], total[1::2])]
            conv[t] = total[0] + locals_[k][t]
            return tuple(new)

        states = lax.fori_loop(0, rows, step, states, unroll=8)
        for side, ref in enumerate((kept[k], given[k])):
            segment = pair if side == 0 else 1 - pair
            column = pl.multiple_of(segment * seg_len + base, 128)
            for g in range(groups):
                lanes = slice(g * 128, (g + 1) * 128)
                query = ref[0, :, lanes].astype(jnp.float32)
                gated = query * conv[:rows, side * groups + g, :]
                out[lanes, pl.ds(column, rows)] = gated.T.astype(jnp.bfloat16)
        base += rows


def finish(place, order, ends, rate, decay, locals_, kept, given, seg_len):
    n_chunks = len(locals_)
    local = pl.BlockSpec(memory_space=pltpu.VMEM)
    operands = list(ends) + [rate, decay] + list(locals_) + list(kept) + list(given)
    lanes = decay.shape[1:]
    channels = kept[0].shape[2]
    longest = max(k.shape[1] for k in kept)
    return pl.pallas_call(
        functools.partial(finish_kernel, len(ends), n_chunks, seg_len),
        grid_spec=pltpu.PrefetchScalarGridSpec(
            num_scalar_prefetch=2,
            grid=(),
            in_specs=[local] * len(operands),
            out_specs=local,
            scratch_shapes=[pltpu.VMEM((longest,) + lanes, jnp.float32)],
        ),
        out_shape=jax.ShapeDtypeStruct((channels, 2 * seg_len), jnp.bfloat16),
        compiler_params=pltpu.CompilerParams(vmem_limit_bytes=40 * MIB),
        cost_estimate=pl.CostEstimate(
            flops=32 * seg_len * lanes[0] * lanes[1],
            bytes_accessed=seg_len * lanes[0] * lanes[1] * 8,
            transcendentals=0,
        ),
        name="finish",
    )(place, order, *operands)


def per_device(tokens, weight, rate, residue, skip, order):
    seg_len = tokens.shape[0]
    n_ctx = lax.axis_size("ctx")
    seq_len = 2 * n_ctx * seg_len
    pair_index = lax.axis_index("fsdp")
    ctx_index = lax.axis_index("ctx")
    place = jnp.stack([pair_index, ctx_index, lax.axis_index("tp")]).astype(jnp.int32)

    starts = [sum(CHUNKS[:k]) for k in range(len(CHUNKS))]
    on_line = lax.axis_size("tp") == 4 and n_ctx == 4
    passed = []
    if on_line:
        near = lax.ppermute(tokens, "tp", [(0, 1), (1, 0), (2, 3), (3, 2)])
        middle = lax.ppermute(tokens, "tp", [(1, 2), (2, 1)])
        ends, far_middle, row = [], [], 0
        for rows in PASSED:
            block = lax.slice_in_dim(middle, row, row + rows, axis=0)
            far = lax.slice_in_dim(near, row, row + rows, axis=0)
            ends.append(lax.ppermute(block, "tp", [(1, 0), (2, 3)]))
            far_middle.append(lax.ppermute(far, "tp", [(1, 2), (2, 1)]))
            row += rows
        passed = [ends[0], far_middle[0]]

    own = weight.transpose(1, 0, 2)
    part = own.shape[1] // n_ctx
    piece_len = DEPTH // 2
    per_part = part // piece_len
    plan = Plan(own.shape[1] // DEPTH, part // DEPTH, n_ctx * per_part)
    per_quarter = tokens.shape[1] // DEPTH
    partials = [None]

    def add_part():
        some = [pieces[m, n] for m in range(n_ctx) for n in (0, 1)]
        return project(
            plan, place, [tokens, near], own, some, plan.part_blocks, None, 0, seg_len,
            plan.half_blocks // plan.part_blocks, near_plan(plan, 0, 0), False,
        )

    pieces = {}
    bits = []
    while 1 << len(bits) < n_ctx:
        bits.insert(0, 1 << len(bits))
    first = []
    for sub in range(per_part):
        piece = lax.dynamic_slice_in_dim(own, ctx_index * part + sub * piece_len, piece_len, 1)
        if sub >= 2 and T["y_y"]:
            piece = after(piece, first[sub - 2])
        if sub == 3 and T["y3_c0"]:
            piece = after(piece, *[pieces[m, 0] for m in range(n_ctx)])
        if sub == 2 and T["y2_A"] and on_line:
            piece = after(piece, near, middle)
        first.append(exchanged(piece, "fsdp", 1))
        held = {0: first[sub]}
        for bit in bits:
            for mask in list(held):
                block = held[mask]
                if bit == bits[0] and sub and T["x_x"][sub]:
                    block = after(block, pieces[bit, sub - 1])
                if bit == bits[0] and sub >= 2 and T["x_c"][sub]:
                    block = after(block, *[pieces[m, sub - 2] for m in range(n_ctx)])
                if on_line:
                    if bit == bits[0] and sub == 3 and T["Ka"] == "x3":
                        block = after(block, partials[1])
                    if bit == bits[-1] and T["Ka"] == "c%d" % sub:
                        block = after(block, partials[1])
                    if bit == bits[0] and sub == 2 and T["x2_A"]:
                        block = after(block, near, middle)
                    if bit == bits[-1] and T["c_A"] == sub:
                        block = after(block, near, middle)
                    if bit == bits[-1] and sub in T["c_P"]:
                        block = after(block, *passed)
                    if bit == bits[0] and sub in T["x_P"]:
                        block = after(block, *passed)
                if bit == bits[-1] and mask and T["c_ser"][sub]:
                    block = after(block, latest)
                latest = exchanged(block, "ctx", bit)
                held[mask | bit] = latest
        for mask in range(n_ctx):
            pieces[mask, sub] = held[mask]
        if sub == 1 and on_line:
            partials.append(add_part())
    ordered = [pieces[mask, sub] for mask in range(n_ctx) for sub in range(per_part)]

    channels = rate.shape[0]
    groups = channels // 128

    def spread(values):
        lanes = values.T.reshape(-1, groups, 128)
        return jnp.concatenate([lanes, lanes], axis=1)

    rates = spread(rate)
    decay = jnp.exp(-rates)
    gain = spread(pole_gain(rate, residue, float(seq_len)))
    direct = spread(skip[:, None])[0]

    if on_line:
        segments = {1024: (((0, 512),), ((512, 512),)), 768: (((0, 512),), ((512, 256), (0, 256)))}[PASSED[0]]

        def add_half(h, first):
            sources = [first, near, middle] + ends[: len(segments[h])]
            return project(
                plan, place, sources, own, ordered, 1, partials[-1], h * 512, 512,
                plan.half_blocks // plan.part_blocks + plan.half_blocks // 2,
                middle_plan(plan, 1, h * 512, segments[h]), False,
            )

        halves = [add_half(0, tokens)]

    kept, given, locals_ = [], [], []
    state = jnp.zeros_like(decay)
    states = []
    for k, (base, rows) in enumerate(zip(starts, CHUNKS)):
        if on_line:
            n, row = 0, base
            while row >= PASSED[n]:
                row -= PASSED[n]
                n += 1
            if k == 1:
                halves.append(add_half(1, after(tokens, kept[0])))
            block = lax.slice_in_dim(far_middle[n], row, row + rows, axis=0)
            if k >= 3:
                block = after(block, halves[T["E"][k - 3]])
            last = lax.ppermute(block, "tp", [(1, 0), (2, 3)])
            if k == 1:
                last = after(last, halves[1])
            if k in T["S"]:
                last = after(last, states[T["S"][k]])
            keep, give = project(
                plan, place, [far_middle[n], last], own, ordered, 1, halves[base // 512], base % 512, rows,
                per_quarter, last_plan(per_quarter, row, rows), True,
            )
        else:
            block = lax.slice_in_dim(tokens, base, base + rows, axis=0)
            whole = lax.all_gather(block, "tp", axis=0, tiled=False)
            keep, give = project(
                plan, place, [whole], own, ordered, 1, None, 0, rows,
                2 * plan.half_blocks, gathered_plan(per_quarter), True,
            )
        got = exchanged(give, "fsdp", 1)
        local, state = scan(keep, got, decay, gain, direct, state)
        states.append(state)
        kept.append(keep)
        given.append(got)
        locals_.append(local)

    ends = [state] + [exchanged(state, "ctx", mask) for mask in range(1, n_ctx)]
    return finish(place, order, ends, rates, decay, locals_, kept, given, seg_len)


def solution(mesh):
    placed = (
        P(("ctx", "fsdp"), "tp"),
        P("fsdp", None, "tp"),
        P(("tp", "fsdp"), None),
        P(("tp", "fsdp"), None),
        P(("tp", "fsdp")),
        P(),
    )
    return jax.shard_map(
        per_device, mesh=mesh, in_specs=placed, out_specs=P(("tp", "fsdp"), "ctx"), check_vma=False
    )
```

```python
import functools
from typing import NamedTuple

import jax
import jax.numpy as jnp
from jax import lax
from jax.experimental import pallas as pl
from jax.experimental.pallas import tpu as pltpu
from jax.sharding import PartitionSpec as P

MIB = 1 << 20
DEPTH = 256
CHUNKS = (256, 256, 256, 128, 128)
PASSED = (1024,)
T = {'y_y': True, 'y3_c0': True, 'y2_A': False, 'x_x': [0, 1, 1, 1], 'x_c': [0, 0, 1, 1], 'Ka': 'c3', 'x2_A': False, 'c_A': 9, 'c_P': [3], 'x_P': [], 'c_ser': [1, 0, 0, 1], 'E': [0, 1], 'S': {3: 0, 4: 1}, 'Kb': 'c3', 'cost': {'part_a': 0, 'part_b': 0, 'part_c': 0, 'project': 0}}
FREE = pl.CostEstimate(flops=0, bytes_accessed=0, transcendentals=0)


class Plan(NamedTuple):
    half_blocks: int
    part_blocks: int
    n_parts: int


def exchanged(block, axis, mask):
    count = lax.axis_size(axis)
    return lax.ppermute(block, axis, [(i, i ^ mask) for i in range(count)])


def after(value, *others):
    return lax.optimization_barrier((value, *others))[0]


def pole_gain(rate, residue, length):
    return residue * jnp.sqrt(jnp.maximum(-jnp.expm1(-2.0 * rate), 1.0 / length))


def choose(low, high, number, act):
    if high - low == 1:
        act(low)
        return
    middle = (low + high) // 2

    @pl.when(number < middle)
    def _():
        choose(low, middle, number, act)

    @pl.when(number >= middle)
    def _():
        choose(middle, high, number, act)


def fetch_weights(plan, place, p, block, own, pieces, first, target, sem):
    pair, ctx = place[0], place[1]
    local = lax.rem(block, plan.half_blocks)
    here = lax.div(block, plan.half_blocks) == pair

    @pl.when(here)
    def _():
        row = pl.multiple_of(local * DEPTH, DEPTH)
        pltpu.make_async_copy(own.at[p, pl.ds(row, DEPTH), :], target, sem).start()

    @pl.when(jnp.logical_not(here))
    def _():
        stride = len(pieces) // plan.n_parts
        number = jnp.bitwise_xor(lax.div(local, plan.part_blocks), ctx) * stride
        number = number + lax.rem(local, plan.part_blocks) - first

        def act(n):
            pltpu.make_async_copy(pieces[n].at[p], target, sem).start()

        choose(0, len(pieces), number, act)


def project_kernel(plan, n_inputs, n_pieces, first, base, final, blocks, x_plan, place, *refs):
    refs = list(refs)
    inputs = [refs.pop(0) for _ in range(n_inputs)]
    own = refs.pop(0)
    pieces = [refs.pop(0) for _ in range(n_pieces)]
    init = refs.pop(0) if base is not None else None
    outs = [refs.pop(0) for _ in range(2 if final else 1)]
    x_buf, w_buf, x_sem, w_sem = refs[:4]
    refs = refs[4:]
    if init is not None:
        i_buf, i_sem = refs.pop(0), refs.pop(0)
    if not final:
        o_buf, o_sem = refs
    pair, tp = place[0], place[2]
    rows, depth = x_buf.shape
    spans = (slice(0, depth // 2), slice(depth // 2, depth))

    def fetch(p):
        if init is not None:
            pltpu.make_async_copy(
                init.at[p, pl.ds(base, rows), :], i_buf.at[p], i_sem.at[p]
            ).start()
        for part in (0, 1):

            def one(step, carry):
                where = pl.ds(pl.multiple_of(step * DEPTH, DEPTH), DEPTH)
                block = x_plan(tp, step, inputs, x_buf.at[:, where], x_sem.at[part], p == 0)
                target = w_buf.at[p, where, :]
                fetch_weights(
                    plan, place, p, block, own, pieces, first, target, w_sem.at[p, part]
                )
                return carry

            lax.fori_loop(part * blocks // 2, (part + 1) * blocks // 2, one, 0)

    def await_part(p, part):
        if p == 0:
            target = x_buf.at[:, spans[part]]
            pltpu.make_async_copy(target, target, x_sem.at[part]).wait()
        target = w_buf.at[p, spans[part], :]
        pltpu.make_async_copy(target, target, w_sem.at[p, part]).wait()

    fetch(0)
    fetch(1)
    for p in range(3):
        if init is not None:
            pltpu.make_async_copy(i_buf.at[p], i_buf.at[p], i_sem.at[p]).wait()
        await_part(p, 0)
        if p:
            await_part(p, 1)
        if not final:
            chunk = min(rows, 256)

            def multiply(span, add, m, carry):
                some = pl.ds(pl.multiple_of(m * chunk, chunk), chunk)
                new = jnp.dot(
                    x_buf[some, span], w_buf[p, span, :], preferred_element_type=jnp.float32
                )
                if add:
                    new = o_buf[p, some, :] + new
                elif init is not None:
                    new = i_buf[p, some, :] + new
                o_buf[p, some, :] = new
                return carry

            if p == 0:
                lax.fori_loop(0, rows // chunk, functools.partial(multiply, spans[0], False), 0)
                await_part(0, 1)
                fetch(2)
                lax.fori_loop(0, rows // chunk, functools.partial(multiply, spans[1], True), 0)
            else:
                whole = slice(0, depth)
                lax.fori_loop(0, rows // chunk, functools.partial(multiply, whole, False), 0)
            pltpu.make_async_copy(o_buf.at[p], outs[0].at[p], o_sem.at[p]).start()
            continue
        kept, given = outs
        half = kept.shape[2]
        lanes = [pl.ds(pl.multiple_of(x * half, 128), half) for x in (pair, 1 - pair)]

        def product(span, n):
            return jnp.dot(
                x_buf[:, span], w_buf[p, span, lanes[n]], preferred_element_type=jnp.float32
            )

        if p == 0:
            early = [product(spans[0], n) for n in (0, 1)]
            await_part(0, 1)
            fetch(2)
            sums = [early[n] + product(spans[1], n) for n in (0, 1)]
        else:
            sums = [product(slice(0, depth), n) for n in (0, 1)]
        for n in (0, 1):
            new = sums[n]
            if init is not None:
                new = i_buf[p, :, lanes[n]] + new
            new = new.astype(jnp.bfloat16)
            if n == 0 or p == 0:
                outs[n][p] = new
            elif p == 1:
                given[1] = new
            else:
                both = given[1].astype(jnp.float32) * new.astype(jnp.float32)
                given[1] = both.astype(jnp.bfloat16)
    if not final:
        for p in range(3):
            pltpu.make_async_copy(o_buf.at[p], outs[0].at[p], o_sem.at[p]).wait()


def project(plan, place, inputs, own, pieces, first, init, base, rows, blocks, x_plan, name):
    final = name == "project"
    width = own.shape[2]
    anywhere = pl.BlockSpec(memory_space=pl.ANY)
    local = pl.BlockSpec(memory_space=pltpu.VMEM)
    operands = list(inputs) + [own] + list(pieces) + ([] if init is None else [init])
    depth = blocks * DEPTH
    total = (3, rows, width)
    scratch = [
        pltpu.VMEM((rows, depth), jnp.bfloat16),
        pltpu.VMEM((3, depth, width), jnp.bfloat16),
        pltpu.SemaphoreType.DMA((2,)),
        pltpu.SemaphoreType.DMA((3, 2)),
    ]
    if init is not None:
        scratch += [pltpu.VMEM(total, jnp.float32), pltpu.SemaphoreType.DMA((3,))]
    if final:
        out_shape = [
            jax.ShapeDtypeStruct((n, rows, width // 2), jnp.bfloat16) for n in (3, 2)
        ]
    else:
        scratch += [pltpu.VMEM(total, jnp.float32), pltpu.SemaphoreType.DMA((3,))]
        out_shape = jax.ShapeDtypeStruct(total, jnp.float32)
    return pl.pallas_call(
        functools.partial(
            project_kernel, plan, len(inputs), len(pieces), first,
            None if init is None else base, final, blocks, x_plan,
        ),
        grid_spec=pltpu.PrefetchScalarGridSpec(
            num_scalar_prefetch=1,
            grid=(),
            in_specs=[anywhere] * len(operands),
            out_specs=[local, local] if final else anywhere,
            scratch_shapes=scratch,
        ),
        out_shape=out_shape,
        compiler_params=pltpu.CompilerParams(vmem_limit_bytes=56 * MIB),
        cost_estimate=pl.CostEstimate(
            flops=T["cost"][name], bytes_accessed=0, transcendentals=0
        ),
        name=name,
    )(place, *operands)


def columns(quarter_block):
    return pl.ds(pl.multiple_of(quarter_block * DEPTH, DEPTH), DEPTH)


def gathered_plan(per_quarter):
    def plan(tp, step, inputs, target, sem, copy):
        source = inputs[0].at[lax.div(step, per_quarter), :, columns(lax.rem(step, per_quarter))]
        if copy:
            pltpu.make_async_copy(source, target, sem).start()
        return step

    return plan


def line_ends(tp):
    return (tp == 0) | (tp == 3)


def near_block(plan, tp, step, subs, base, inputs, target, sem, copy):
    span = plan.half_blocks // 2 // plan.part_blocks
    place = lax.div(step, len(subs))
    sub = subs[0] + lax.rem(step, len(subs))
    mine = place < span
    side = jnp.where(mine, lax.rem(tp, 2), 1 - lax.rem(tp, 2))
    within = lax.rem(place, span) * plan.part_blocks + sub
    block = lax.div(tp, 2) * plan.half_blocks + side * span * plan.part_blocks + within
    if not copy:
        return block
    where = columns(within)
    for at, source in ((True, inputs[0]), (False, inputs[1])):
        @pl.when(mine == at)
        def _():
            rows = pl.ds(base, target.shape[0])
            pltpu.make_async_copy(source.at[rows, where], target, sem).start()

    return block


def near_plan(plan, subs, base):
    def x_plan(tp, step, inputs, target, sem, copy):
        return near_block(plan, tp, step, subs, base, inputs, target, sem, copy)

    return x_plan


def middle_plan(plan, subs, base, segments):
    span = plan.half_blocks // plan.part_blocks * len(subs)
    per_quarter = plan.half_blocks // 2

    def x_plan(tp, step, inputs, target, sem, copy):
        middle, ends = inputs[2], inputs[3:]
        late = step - span
        early = jnp.minimum(step, span - 1)
        near = near_block(plan, tp, early, subs, base, inputs, target, sem, False)
        block = jnp.where(late < 0, near, (2 - lax.div(tp, 2)) * per_quarter + late)
        if not copy:
            return block
        where = columns(jnp.maximum(late, 0))

        @pl.when(late < 0)
        def _():
            near_block(plan, tp, early, subs, base, inputs, target, sem, True)

        @pl.when((late >= 0) & jnp.logical_not(line_ends(tp)))
        def _():
            rows = pl.ds(base, target.shape[0])
            pltpu.make_async_copy(middle.at[rows, where], target, sem).start()

        @pl.when((late >= 0) & line_ends(tp))
        def _():
            row = 0
            for source, (first, size) in zip(ends, segments):
                pltpu.make_async_copy(
                    source.at[pl.ds(first, size), where], target.at[pl.ds(row, size), :], sem
                ).start()
                row += size

        return block

    return x_plan


def last_plan(per_quarter, row, rows):
    def plan(tp, step, inputs, target, sem, copy):
        block = jnp.where(tp < 2, 3, 0) * per_quarter + step
        if not copy:
            return block
        middle, ends = inputs
        where = columns(step)

        @pl.when(line_ends(tp))
        def _():
            pltpu.make_async_copy(ends.at[:, where], target, sem).start()

        @pl.when(jnp.logical_not(line_ends(tp)))
        def _():
            pltpu.make_async_copy(middle.at[pl.ds(row, rows), where], target, sem).start()

        return block

    return plan


def scan_kernel(kept, given, decay, gain, skip, state_in, local_ref, state_out, prod):
    poles = decay.shape[0]
    rows = kept.shape[1]
    groups = kept.shape[2] // 128
    for side, ref in enumerate((kept, given)):
        for g in range(groups):
            lanes = slice(g * 128, (g + 1) * 128)
            product = ref[1, :, lanes].astype(jnp.float32)
            if side == 0:
                product = product * ref[2, :, lanes].astype(jnp.float32)
            prod[:, side * groups + g, :] = product
    direct = skip[...]
    factors = [decay[r] for r in range(poles)]
    gains = [gain[r] for r in range(poles)]

    def step(t, states):
        p = prod[t]
        new = [factors[r] * states[r] + gains[r] * p for r in range(poles)]
        total = list(new)
        while len(total) > 1:
            total = [a + b for a, b in zip(total[::2], total[1::2])]
        local_ref[t] = total[0] + direct * p
        return tuple(new)

    states = lax.fori_loop(0, rows, step, tuple(state_in[r] for r in range(poles)), unroll=8)
    for r in range(poles):
        state_out[r] = states[r]


def scan(kept, given, decay, gain, skip, state):
    rows = kept.shape[1]
    local = pl.BlockSpec(memory_space=pltpu.VMEM)
    lanes = decay.shape[1:]
    return pl.pallas_call(
        scan_kernel,
        in_specs=[local] * 6,
        out_specs=[local] * 2,
        out_shape=[
            jax.ShapeDtypeStruct((rows,) + lanes, jnp.float32),
            jax.ShapeDtypeStruct(decay.shape, jnp.float32),
        ],
        scratch_shapes=[pltpu.VMEM((rows,) + lanes, jnp.float32)],
        compiler_params=pltpu.CompilerParams(vmem_limit_bytes=24 * MIB),
        cost_estimate=FREE,
        name="scan",
    )(kept, given, decay, gain, skip, state)


def finish_kernel(n_ctx, n_chunks, seg_len, place, order, *refs):
    refs = list(refs)
    ends = [refs.pop(0) for _ in range(n_ctx)]
    rate = refs.pop(0)
    decay = refs.pop(0)
    locals_ = [refs.pop(0) for _ in range(n_chunks)]
    kept = [refs.pop(0) for _ in range(n_chunks)]
    given = [refs.pop(0) for _ in range(n_chunks)]
    out = refs.pop(0)
    conv = refs.pop(0)
    poles, sublanes, _ = decay.shape
    groups = sublanes // 2
    pair, ctx = place[0], place[1]
    upper = lax.broadcasted_iota(jnp.int32, decay.shape[1:], 0) < groups
    targets = (order[2 * ctx + pair], order[2 * ctx + 1 - pair])
    states = [jnp.zeros(decay.shape[1:], jnp.float32) for _ in range(poles)]
    for mask in range(n_ctx):
        origin = jnp.bitwise_xor(ctx, mask)
        sources = (order[2 * origin + pair], order[2 * origin + 1 - pair])
        for cross in (0, 1):
            gaps = [targets[s] - 1 - sources[s ^ cross] for s in (0, 1)]
            gap = jnp.where(upper, gaps[0], gaps[1])
            span = jnp.maximum(gap, 0).astype(jnp.float32) * seg_len
            for r in range(poles):
                end = ends[mask][r]
                if cross:
                    end = jnp.concatenate([end[groups:], end[:groups]], axis=0)
                factor = jnp.where(gap >= 0, jnp.exp(-rate[r] * span), 0.0)
                states[r] = states[r] + factor * end
    factors = [decay[r] for r in range(poles)]
    states = tuple(states)
    base = 0
    for k in range(n_chunks):
        rows = locals_[k].shape[0]

        def step(t, states):
            new = [factors[r] * states[r] for r in range(poles)]
            total = list(new)
            while len(total) > 1:
                total = [a + b for a, b in zip(total[::2], total[1::2])]
            conv[t] = total[0] + locals_[k][t]
            return tuple(new)

        states = lax.fori_loop(0, rows, step, states, unroll=8)
        for side, ref in enumerate((kept[k], given[k])):
            segment = pair if side == 0 else 1 - pair
            column = pl.multiple_of(segment * seg_len + base, 128)
            for g in range(groups):
                lanes = slice(g * 128, (g + 1) * 128)
                query = ref[0, :, lanes].astype(jnp.float32)
                gated = query * conv[:rows, side * groups + g, :]
                out[lanes, pl.ds(column, rows)] = gated.T.astype(jnp.bfloat16)
        base += rows


def finish(place, order, ends, rate, decay, locals_, kept, given, seg_len):
    n_chunks = len(locals_)
    local = pl.BlockSpec(memory_space=pltpu.VMEM)
    operands = list(ends) + [rate, decay] + list(locals_) + list(kept) + list(given)
    lanes = decay.shape[1:]
    channels = kept[0].shape[2]
    longest = max(k.shape[1] for k in kept)
    return pl.pallas_call(
        functools.partial(finish_kernel, len(ends), n_chunks, seg_len),
        grid_spec=pltpu.PrefetchScalarGridSpec(
            num_scalar_prefetch=2,
            grid=(),
            in_specs=[local] * len(operands),
            out_specs=local,
            scratch_shapes=[pltpu.VMEM((longest,) + lanes, jnp.float32)],
        ),
        out_shape=jax.ShapeDtypeStruct((channels, 2 * seg_len), jnp.bfloat16),
        compiler_params=pltpu.CompilerParams(vmem_limit_bytes=40 * MIB),
        cost_estimate=pl.CostEstimate(
            flops=32 * seg_len * lanes[0] * lanes[1],
            bytes_accessed=seg_len * lanes[0] * lanes[1] * 8,
            transcendentals=0,
        ),
        name="finish",
    )(place, order, *operands)


def per_device(tokens, weight, rate, residue, skip, order):
    seg_len = tokens.shape[0]
    n_ctx = lax.axis_size("ctx")
    seq_len = 2 * n_ctx * seg_len
    pair_index = lax.axis_index("fsdp")
    ctx_index = lax.axis_index("ctx")
    place = jnp.stack([pair_index, ctx_index, lax.axis_index("tp")]).astype(jnp.int32)

    starts = [sum(CHUNKS[:k]) for k in range(len(CHUNKS))]
    on_line = lax.axis_size("tp") == 4 and n_ctx == 4
    passed = []
    if on_line:
        near = lax.ppermute(tokens, "tp", [(0, 1), (1, 0), (2, 3), (3, 2)])
        middle = lax.ppermute(tokens, "tp", [(1, 2), (2, 1)])
        ends, far_middle, row = [], [], 0
        for rows in PASSED:
            block = lax.slice_in_dim(middle, row, row + rows, axis=0)
            far = lax.slice_in_dim(near, row, row + rows, axis=0)
            ends.append(lax.ppermute(block, "tp", [(1, 0), (2, 3)]))
            far_middle.append(lax.ppermute(far, "tp", [(1, 2), (2, 1)]))
            row += rows
        passed = [ends[0], far_middle[0]]

    own = weight.transpose(1, 0, 2)
    part = own.shape[1] // n_ctx
    piece_len = DEPTH
    per_part = part // piece_len
    plan = Plan(own.shape[1] // DEPTH, part // DEPTH, n_ctx)
    per_quarter = tokens.shape[1] // DEPTH
    partials = [None]

    def add_part(subs, name):
        some = [pieces[m, n] for m in range(n_ctx) for n in subs]
        return project(
            plan, place, [tokens, near], own, some, subs[0], partials[-1], 0, seg_len,
            n_ctx * len(subs), near_plan(plan, subs, 0), name,
        )

    pieces = {}
    bits = []
    while 1 << len(bits) < n_ctx:
        bits.insert(0, 1 << len(bits))
    first = []
    for sub in range(per_part):
        piece = lax.dynamic_slice_in_dim(own, ctx_index * part + sub * piece_len, piece_len, 1)
        if sub >= 2 and T["y_y"]:
            piece = after(piece, first[sub - 2])
        if sub == 3 and T["y3_c0"]:
            piece = after(piece, *[pieces[m, 0] for m in range(n_ctx)])
        if sub == 2 and T["y2_A"] and on_line:
            piece = after(piece, near, middle)
        first.append(exchanged(piece, "fsdp", 1))
        held = {0: first[sub]}
        for bit in bits:
            for mask in list(held):
                block = held[mask]
                if bit == bits[0] and sub and T["x_x"][sub]:
                    block = after(block, pieces[bit, sub - 1])
                if bit == bits[0] and sub >= 2 and T["x_c"][sub]:
                    block = after(block, *[pieces[m, sub - 2] for m in range(n_ctx)])
                if on_line:
                    if bit == bits[0] and sub == 3 and T["Ka"] == "x3":
                        block = after(block, partials[1])
                    if bit == bits[-1] and T["Ka"] == "c%d" % sub:
                        block = after(block, partials[1])
                    if bit == bits[0] and sub == 3 and T["Kb"] == "x3":
                        block = after(block, partials[2])
                    if bit == bits[-1] and sub == 3 and T["Kb"] == "c3":
                        block = after(block, partials[2])
                    if bit == bits[0] and sub == 2 and T["x2_A"]:
                        block = after(block, near, middle)
                    if bit == bits[-1] and T["c_A"] == sub:
                        block = after(block, near, middle)
                    if bit == bits[-1] and sub in T["c_P"]:
                        block = after(block, *passed)
                    if bit == bits[0] and sub in T["x_P"]:
                        block = after(block, *passed)
                if bit == bits[-1] and mask and T["c_ser"][sub]:
                    block = after(block, latest)
                latest = exchanged(block, "ctx", bit)
                held[mask | bit] = latest
        for mask in range(n_ctx):
            pieces[mask, sub] = held[mask]
        if sub == 1 and on_line:
            partials.append(add_part((0, 1), "part_a"))
        if sub == 2 and on_line:
            partials.append(add_part((2,), "part_b"))
    ordered = [pieces[mask, sub] for mask in range(n_ctx) for sub in range(per_part)]

    channels = rate.shape[0]
    groups = channels // 128

    def spread(values):
        lanes = values.T.reshape(-1, groups, 128)
        return jnp.concatenate([lanes, lanes], axis=1)

    rates = spread(rate)
    decay = jnp.exp(-rates)
    gain = spread(pole_gain(rate, residue, float(seq_len)))
    direct = spread(skip[:, None])[0]

    if on_line:
        segments = {1024: (((0, 512),), ((512, 512),)), 768: (((0, 512),), ((512, 256), (0, 256)))}[PASSED[0]]

        def add_half(h, first):
            sources = [first, near, middle] + ends[: len(segments[h])]
            return project(
                plan, place, sources, own, ordered, 0, partials[-1], h * 512, 512,
                n_ctx + plan.half_blocks // 2, middle_plan(plan, (3,), h * 512, segments[h]),
                "part_c",
            )

        halves = [add_half(0, tokens)]

    kept, given, locals_ = [], [], []
    state = jnp.zeros_like(decay)
    states = []
    for k, (base, rows) in enumerate(zip(starts, CHUNKS)):
        if on_line:
            n, row = 0, base
            while row >= PASSED[n]:
                row -= PASSED[n]
                n += 1
            if k == 1:
                halves.append(add_half(1, after(tokens, kept[0])))
            block = lax.slice_in_dim(far_middle[n], row, row + rows, axis=0)
            if k >= 3:
                block = after(block, halves[T["E"][k - 3]])
            last = lax.ppermute(block, "tp", [(1, 0), (2, 3)])
            if k == 1:
                last = after(last, halves[1])
            if k in T["S"]:
                last = after(last, states[T["S"][k]])
            keep, give = project(
                plan, place, [far_middle[n], last], own, ordered, 0, halves[base // 512], base % 512, rows,
                per_quarter, last_plan(per_quarter, row, rows), "project",
            )
        else:
            block = lax.slice_in_dim(tokens, base, base + rows, axis=0)
            whole = lax.all_gather(block, "tp", axis=0, tiled=False)
            keep, give = project(
                plan, place, [whole], own, ordered, 0, None, 0, rows,
                2 * plan.half_blocks, gathered_plan(per_quarter), "project",
            )
        got = exchanged(give, "fsdp", 1)
        local, state = scan(keep, got, decay, gain, direct, state)
        states.append(state)
        kept.append(keep)
        given.append(got)
        locals_.append(local)

    ends = [state] + [exchanged(state, "ctx", mask) for mask in range(1, n_ctx)]
    return finish(place, order, ends, rates, decay, locals_, kept, given, seg_len)


def solution(mesh):
    placed = (
        P(("ctx", "fsdp"), "tp"),
        P("fsdp", None, "tp"),
        P(("tp", "fsdp"), None),
        P(("tp", "fsdp"), None),
        P(("tp", "fsdp")),
        P(),
    )
    return jax.shard_map(
        per_device, mesh=mesh, in_specs=placed, out_specs=P(("tp", "fsdp"), "ctx"), check_vma=False
    )
```

```python
import functools
from typing import NamedTuple

import jax
import jax.numpy as jnp
from jax import lax
from jax.experimental import pallas as pl
from jax.experimental.pallas import tpu as pltpu
from jax.sharding import PartitionSpec as P

MIB = 1 << 20
DEPTH = 256
CHUNKS = (256, 256, 256, 256)
PASSED = (512, 512)
T = {'y_y': True, 'y3_c0': True, 'y2_A': False, 'x_x': [0, False, True, False], 'x_c': [0, 0, 1, 1], 'Ka': 'c3', 'x2_A': False, 'c_A': 9, 'c_P': [3], 'x_P': [], 'c_ser': [1, 0, 0, 0], 'E': [], 'FK': True, 'CH': [256, 256, 256, 256], 'S': {}, 'Kb': 'c3', 'cost': {'part_a': 0, 'part_b': 0, 'part_c': 0, 'project': 0}}
FREE = pl.CostEstimate(flops=0, bytes_accessed=0, transcendentals=0)


class Plan(NamedTuple):
    half_blocks: int
    part_blocks: int
    n_parts: int


def exchanged(block, axis, mask):
    count = lax.axis_size(axis)
    return lax.ppermute(block, axis, [(i, i ^ mask) for i in range(count)])


def after(value, *others):
    return lax.optimization_barrier((value, *others))[0]


def pole_gain(rate, residue, length):
    return residue * jnp.sqrt(jnp.maximum(-jnp.expm1(-2.0 * rate), 1.0 / length))


def choose(low, high, number, act):
    if high - low == 1:
        act(low)
        return
    middle = (low + high) // 2

    @pl.when(number < middle)
    def _():
        choose(low, middle, number, act)

    @pl.when(number >= middle)
    def _():
        choose(middle, high, number, act)


def fetch_weights(plan, place, p, block, own, pieces, first, target, sem):
    pair, ctx = place[0], place[1]
    local = lax.rem(block, plan.half_blocks)
    here = lax.div(block, plan.half_blocks) == pair

    @pl.when(here)
    def _():
        row = pl.multiple_of(local * DEPTH, DEPTH)
        pltpu.make_async_copy(own.at[p, pl.ds(row, DEPTH), :], target, sem).start()

    @pl.when(jnp.logical_not(here))
    def _():
        stride = len(pieces) // plan.n_parts
        number = jnp.bitwise_xor(lax.div(local, plan.part_blocks), ctx) * stride
        number = number + lax.rem(local, plan.part_blocks) - first

        def act(n):
            pltpu.make_async_copy(pieces[n].at[p], target, sem).start()

        choose(0, len(pieces), number, act)


def project_kernel(plan, n_inputs, n_pieces, first, base, final, blocks, x_plan, place, *refs):
    refs = list(refs)
    inputs = [refs.pop(0) for _ in range(n_inputs)]
    own = refs.pop(0)
    pieces = [refs.pop(0) for _ in range(n_pieces)]
    init = refs.pop(0) if base is not None else None
    outs = [refs.pop(0) for _ in range(2 if final else 1)]
    x_buf, w_buf, x_sem, w_sem = refs[:4]
    refs = refs[4:]
    if final:
        i_buf, i_sem = refs if init is not None else (None, None)
    else:
        o_buf, o_sem, i_sem = refs
        i_buf = o_buf
    pair, tp = place[0], place[2]
    rows, depth = x_buf.shape
    spans = (slice(0, depth // 2), slice(depth // 2, depth))

    def fetch(p):
        if init is not None:
            pltpu.make_async_copy(
                init.at[p, pl.ds(base, rows), :], i_buf.at[p], i_sem.at[p]
            ).start()
        for part in (0, 1):

            def one(step, carry):
                where = pl.ds(pl.multiple_of(step * DEPTH, DEPTH), DEPTH)
                block = x_plan(tp, step, inputs, x_buf.at[:, where], x_sem.at[part], p == 0)
                target = w_buf.at[p, where, :]
                fetch_weights(
                    plan, place, p, block, own, pieces, first, target, w_sem.at[p, part]
                )
                return carry

            lax.fori_loop(part * blocks // 2, (part + 1) * blocks // 2, one, 0)

    def await_part(p, part):
        if p == 0:
            target = x_buf.at[:, spans[part]]
            pltpu.make_async_copy(target, target, x_sem.at[part]).wait()
        target = w_buf.at[p, spans[part], :]
        pltpu.make_async_copy(target, target, w_sem.at[p, part]).wait()

    fetch(0)
    fetch(1)
    for p in range(3):
        if init is not None:
            pltpu.make_async_copy(i_buf.at[p], i_buf.at[p], i_sem.at[p]).wait()
        await_part(p, 0)
        if p:
            await_part(p, 1)
        if not final:
            chunk = min(rows, 256)

            def multiply(span, add, m, carry):
                some = pl.ds(pl.multiple_of(m * chunk, chunk), chunk)
                new = jnp.dot(
                    x_buf[some, span], w_buf[p, span, :], preferred_element_type=jnp.float32
                )
                if add or init is not None:
                    new = o_buf[p, some, :] + new
                o_buf[p, some, :] = new
                return carry

            if p == 0:
                lax.fori_loop(0, rows // chunk, functools.partial(multiply, spans[0], False), 0)
                await_part(0, 1)
                fetch(2)
                lax.fori_loop(0, rows // chunk, functools.partial(multiply, spans[1], True), 0)
            else:
                whole = slice(0, depth)
                lax.fori_loop(0, rows // chunk, functools.partial(multiply, whole, False), 0)
            pltpu.make_async_copy(o_buf.at[p], outs[0].at[p], o_sem.at[p]).start()
            continue
        kept, given = outs
        half = kept.shape[2]
        lanes = [pl.ds(pl.multiple_of(x * half, 128), half) for x in (pair, 1 - pair)]

        def product(span, n):
            return jnp.dot(
                x_buf[:, span], w_buf[p, span, lanes[n]], preferred_element_type=jnp.float32
            )

        if p == 0:
            early = [product(spans[0], n) for n in (0, 1)]
            await_part(0, 1)
            fetch(2)
            sums = [early[n] + product(spans[1], n) for n in (0, 1)]
        else:
            sums = [product(slice(0, depth), n) for n in (0, 1)]
        for n in (0, 1):
            new = sums[n]
            if init is not None:
                new = i_buf[p, :, lanes[n]] + new
            new = new.astype(jnp.bfloat16)
            if n == 0 or p == 0:
                outs[n][p] = new
            elif p == 1:
                given[1] = new
            else:
                both = given[1].astype(jnp.float32) * new.astype(jnp.float32)
                given[1] = both.astype(jnp.bfloat16)
    if not final:
        for p in range(3):
            pltpu.make_async_copy(o_buf.at[p], outs[0].at[p], o_sem.at[p]).wait()


def project(plan, place, inputs, own, pieces, first, init, base, rows, blocks, x_plan, name):
    final = name == "project"
    width = own.shape[2]
    anywhere = pl.BlockSpec(memory_space=pl.ANY)
    local = pl.BlockSpec(memory_space=pltpu.VMEM)
    operands = list(inputs) + [own] + list(pieces) + ([] if init is None else [init])
    depth = blocks * DEPTH
    total = (3, rows, width)
    scratch = [
        pltpu.VMEM((rows, depth), jnp.bfloat16),
        pltpu.VMEM((3, depth, width), jnp.bfloat16),
        pltpu.SemaphoreType.DMA((2,)),
        pltpu.SemaphoreType.DMA((3, 2)),
    ]
    if final:
        if init is not None:
            scratch += [pltpu.VMEM(total, jnp.float32), pltpu.SemaphoreType.DMA((3,))]
        out_shape = [
            jax.ShapeDtypeStruct((n, rows, width // 2), jnp.bfloat16) for n in (3, 2)
        ]
    else:
        scratch += [pltpu.VMEM(total, jnp.float32)] + [pltpu.SemaphoreType.DMA((3,))] * 2
        out_shape = jax.ShapeDtypeStruct(total, jnp.float32)
    return pl.pallas_call(
        functools.partial(
            project_kernel, plan, len(inputs), len(pieces), first,
            None if init is None else base, final, blocks, x_plan,
        ),
        grid_spec=pltpu.PrefetchScalarGridSpec(
            num_scalar_prefetch=1,
            grid=(),
            in_specs=[anywhere] * len(operands),
            out_specs=[local, local] if final else anywhere,
            scratch_shapes=scratch,
        ),
        out_shape=out_shape,
        compiler_params=pltpu.CompilerParams(vmem_limit_bytes=56 * MIB),
        cost_estimate=pl.CostEstimate(
            flops=T["cost"][name], bytes_accessed=0, transcendentals=0
        ),
        name=name,
    )(place, *operands)


def columns(quarter_block):
    return pl.ds(pl.multiple_of(quarter_block * DEPTH, DEPTH), DEPTH)


def gathered_plan(per_quarter):
    def plan(tp, step, inputs, target, sem, copy):
        source = inputs[0].at[lax.div(step, per_quarter), :, columns(lax.rem(step, per_quarter))]
        if copy:
            pltpu.make_async_copy(source, target, sem).start()
        return step

    return plan


def line_ends(tp):
    return (tp == 0) | (tp == 3)


def near_block(plan, tp, step, subs, base, inputs, target, sem, copy):
    span = plan.half_blocks // 2 // plan.part_blocks
    place = lax.div(step, len(subs))
    sub = subs[0] + lax.rem(step, len(subs))
    mine = place < span
    side = jnp.where(mine, lax.rem(tp, 2), 1 - lax.rem(tp, 2))
    within = lax.rem(place, span) * plan.part_blocks + sub
    block = lax.div(tp, 2) * plan.half_blocks + side * span * plan.part_blocks + within
    if not copy:
        return block
    where = columns(within)
    for at, source in ((True, inputs[0]), (False, inputs[1])):
        @pl.when(mine == at)
        def _():
            rows = pl.ds(base, target.shape[0])
            pltpu.make_async_copy(source.at[rows, where], target, sem).start()

    return block


def near_plan(plan, subs, base):
    def x_plan(tp, step, inputs, target, sem, copy):
        return near_block(plan, tp, step, subs, base, inputs, target, sem, copy)

    return x_plan


def middle_plan(plan, subs, late_subs):
    span = plan.half_blocks // plan.part_blocks * len(subs)
    per_quarter = plan.half_blocks // 2

    def x_plan(tp, step, inputs, target, sem, copy):
        middle, ends = inputs[2:]
        late = step - span
        early = jnp.minimum(step, span - 1)
        near = near_block(plan, tp, early, subs, 0, inputs, target, sem, False)
        part, sub = lax.div(late, len(late_subs)), lax.rem(late, len(late_subs))
        within = jnp.maximum(part * plan.part_blocks + late_subs[0] + sub, 0)
        block = jnp.where(late < 0, near, (2 - lax.div(tp, 2)) * per_quarter + within)
        if not copy:
            return block
        where = columns(within)

        @pl.when(late < 0)
        def _():
            near_block(plan, tp, early, subs, 0, inputs, target, sem, True)

        for at_end, source in ((False, middle), (True, ends)):
            @pl.when((late >= 0) & (line_ends(tp) == at_end))
            def _():
                pltpu.make_async_copy(source.at[:, where], target, sem).start()

        return block

    return x_plan


def last_plan(per_quarter, row, rows):
    def plan(tp, step, inputs, target, sem, copy):
        block = jnp.where(tp < 2, 3, 0) * per_quarter + step
        if not copy:
            return block
        middle, ends = inputs
        where = columns(step)

        @pl.when(line_ends(tp))
        def _():
            pltpu.make_async_copy(ends.at[:, where], target, sem).start()

        @pl.when(jnp.logical_not(line_ends(tp)))
        def _():
            pltpu.make_async_copy(middle.at[pl.ds(row, rows), where], target, sem).start()

        return block

    return plan


def scan_kernel(kept, given, decay, gain, skip, state_in, local_ref, state_out, prod):
    poles = decay.shape[0]
    rows = kept.shape[1]
    groups = kept.shape[2] // 128
    for side, ref in enumerate((kept, given)):
        for g in range(groups):
            lanes = slice(g * 128, (g + 1) * 128)
            product = ref[1, :, lanes].astype(jnp.float32)
            if side == 0:
                product = product * ref[2, :, lanes].astype(jnp.float32)
            prod[:, side * groups + g, :] = product
    direct = skip[...]
    factors = [decay[r] for r in range(poles)]
    gains = [gain[r] for r in range(poles)]

    def step(t, states):
        p = prod[t]
        new = [factors[r] * states[r] + gains[r] * p for r in range(poles)]
        total = list(new)
        while len(total) > 1:
            total = [a + b for a, b in zip(total[::2], total[1::2])]
        local_ref[t] = total[0] + direct * p
        return tuple(new)

    states = lax.fori_loop(0, rows, step, tuple(state_in[r] for r in range(poles)), unroll=8)
    for r in range(poles):
        state_out[r] = states[r]


def scan(kept, given, decay, gain, skip, state):
    rows = kept.shape[1]
    local = pl.BlockSpec(memory_space=pltpu.VMEM)
    lanes = decay.shape[1:]
    return pl.pallas_call(
        scan_kernel,
        in_specs=[local] * 6,
        out_specs=[local] * 2,
        out_shape=[
            jax.ShapeDtypeStruct((rows,) + lanes, jnp.float32),
            jax.ShapeDtypeStruct(decay.shape, jnp.float32),
        ],
        scratch_shapes=[pltpu.VMEM((rows,) + lanes, jnp.float32)],
        compiler_params=pltpu.CompilerParams(vmem_limit_bytes=24 * MIB),
        cost_estimate=FREE,
        name="scan",
    )(kept, given, decay, gain, skip, state)


def carry_kernel(n_ctx, seg_len, place, order, rate, weights):
    poles, sublanes, _ = rate.shape
    pair, ctx = place[0], place[1]
    upper = lax.broadcasted_iota(jnp.int32, rate.shape[1:], 0) < sublanes // 2
    targets = (order[2 * ctx + pair], order[2 * ctx + 1 - pair])
    for mask in range(n_ctx):
        origin = jnp.bitwise_xor(ctx, mask)
        sources = (order[2 * origin + pair], order[2 * origin + 1 - pair])
        for cross in (0, 1):
            gaps = [targets[s] - 1 - sources[s ^ cross] for s in (0, 1)]
            gap = jnp.where(upper, gaps[0], gaps[1])
            span = jnp.maximum(gap, 0).astype(jnp.float32) * seg_len
            for r in range(poles):
                weights[mask, cross, r] = jnp.where(gap >= 0, jnp.exp(-rate[r] * span), 0.0)


def carry(place, order, rate, n_ctx, seg_len):
    local = pl.BlockSpec(memory_space=pltpu.VMEM)
    return pl.pallas_call(
        functools.partial(carry_kernel, n_ctx, seg_len),
        grid_spec=pltpu.PrefetchScalarGridSpec(
            num_scalar_prefetch=2, grid=(), in_specs=[local], out_specs=local
        ),
        out_shape=jax.ShapeDtypeStruct((n_ctx, 2) + rate.shape, jnp.float32),
        cost_estimate=FREE,
        name="carry",
    )(place, order, rate)


def finish_kernel(n_ctx, n_chunks, seg_len, place, *refs):
    refs = list(refs)
    ends = [refs.pop(0) for _ in range(n_ctx)]
    weights = refs.pop(0)
    decay = refs.pop(0)
    locals_ = [refs.pop(0) for _ in range(n_chunks)]
    kept = [refs.pop(0) for _ in range(n_chunks)]
    given = [refs.pop(0) for _ in range(n_chunks)]
    out = refs.pop(0)
    conv = refs.pop(0)
    poles, sublanes, _ = decay.shape
    groups = sublanes // 2
    pair = place[0]
    states = [jnp.zeros(decay.shape[1:], jnp.float32) for _ in range(poles)]
    for mask in range(n_ctx):
        for r in range(poles):
            end = ends[mask][r]
            turned = jnp.concatenate([end[groups:], end[:groups]], axis=0)
            states[r] = states[r] + weights[mask, 0, r] * end + weights[mask, 1, r] * turned
    factors = [decay[r] for r in range(poles)]
    states = tuple(states)
    base = 0
    for k in range(n_chunks):
        rows = locals_[k].shape[0]

        def step(t, states):
            new = [factors[r] * states[r] for r in range(poles)]
            total = list(new)
            while len(total) > 1:
                total = [a + b for a, b in zip(total[::2], total[1::2])]
            conv[t] = total[0] + locals_[k][t]
            return tuple(new)

        states = lax.fori_loop(0, rows, step, states, unroll=8)
        for side, ref in enumerate((kept[k], given[k])):
            segment = pair if side == 0 else 1 - pair
            column = pl.multiple_of(segment * seg_len + base, 128)
            for g in range(groups):
                lanes = slice(g * 128, (g + 1) * 128)
                query = ref[0, :, lanes].astype(jnp.float32)
                gated = query * conv[:rows, side * groups + g, :]
                out[lanes, pl.ds(column, rows)] = gated.astype(jnp.bfloat16).T
        base += rows


def finish(place, ends, weights, decay, locals_, kept, given, seg_len):
    n_chunks = len(locals_)
    local = pl.BlockSpec(memory_space=pltpu.VMEM)
    operands = list(ends) + [weights, decay] + list(locals_) + list(kept) + list(given)
    lanes = decay.shape[1:]
    channels = kept[0].shape[2]
    longest = max(k.shape[1] for k in kept)
    return pl.pallas_call(
        functools.partial(finish_kernel, len(ends), n_chunks, seg_len),
        grid_spec=pltpu.PrefetchScalarGridSpec(
            num_scalar_prefetch=1,
            grid=(),
            in_specs=[local] * len(operands),
            out_specs=local,
            scratch_shapes=[pltpu.VMEM((longest,) + lanes, jnp.float32)],
        ),
        out_shape=jax.ShapeDtypeStruct((channels, 2 * seg_len), jnp.bfloat16),
        compiler_params=pltpu.CompilerParams(vmem_limit_bytes=40 * MIB),
        cost_estimate=pl.CostEstimate(
            flops=32 * seg_len * lanes[0] * lanes[1],
            bytes_accessed=seg_len * lanes[0] * lanes[1] * 8,
            transcendentals=0,
        ),
        name="finish",
    )(place, *operands)


def per_device(tokens, weight, rate, residue, skip, order):
    seg_len = tokens.shape[0]
    n_ctx = lax.axis_size("ctx")
    seq_len = 2 * n_ctx * seg_len
    pair_index = lax.axis_index("fsdp")
    ctx_index = lax.axis_index("ctx")
    place = jnp.stack([pair_index, ctx_index, lax.axis_index("tp")]).astype(jnp.int32)

    starts = [sum(CHUNKS[:k]) for k in range(len(CHUNKS))]
    on_line = lax.axis_size("tp") == 4 and n_ctx == 4
    passed = []
    if on_line:
        near = lax.ppermute(tokens, "tp", [(0, 1), (1, 0), (2, 3), (3, 2)])
        middle = lax.ppermute(tokens, "tp", [(1, 2), (2, 1)])
        ends = lax.ppermute(middle, "tp", [(1, 0), (2, 3)])
        block = lax.slice_in_dim(near, 0, PASSED[0], axis=0)
        far_middle = [lax.ppermute(block, "tp", [(1, 2), (2, 1)])]
        passed = [ends] + far_middle

    own = weight.transpose(1, 0, 2)
    part = own.shape[1] // n_ctx
    piece_len = DEPTH
    per_part = part // piece_len
    plan = Plan(own.shape[1] // DEPTH, part // DEPTH, n_ctx)
    per_quarter = tokens.shape[1] // DEPTH
    partials = [None]

    def add_part(subs, late_subs, name):
        known = range(max(late_subs) + 1) if subs[0] < per_part - 1 else subs
        some = [pieces[m, n] for m in range(n_ctx) for n in known]
        sources, x_plan = [tokens, near], near_plan(plan, subs, 0)
        if name != "part_a":
            sources, x_plan = sources + [middle, ends], middle_plan(plan, subs, late_subs)
        units = n_ctx * len(subs) + (n_ctx // 2 * len(late_subs) if name != "part_a" else 0)
        return project(
            plan, place, sources, own, some, known[0], partials[-1], 0, seg_len, units, x_plan, name
        )

    pieces = {}
    bits = []
    while 1 << len(bits) < n_ctx:
        bits.insert(0, 1 << len(bits))
    first = []
    for sub in range(per_part):
        piece = lax.dynamic_slice_in_dim(own, ctx_index * part + sub * piece_len, piece_len, 1)
        if sub >= 2 and T["y_y"]:
            piece = after(piece, first[sub - 2])
        if sub == 3 and T["y3_c0"]:
            piece = after(piece, *[pieces[m, 0] for m in range(n_ctx)])
        if sub == 2 and T["y2_A"] and on_line:
            piece = after(piece, near, middle)
        first.append(exchanged(piece, "fsdp", 1))
        held = {0: first[sub]}
        for bit in bits:
            for mask in list(held):
                block = held[mask]
                if bit == bits[0] and sub and T["x_x"][sub]:
                    block = after(block, pieces[bit, sub - 1])
                if bit == bits[0] and sub >= 2 and T["x_c"][sub]:
                    block = after(block, *[pieces[m, sub - 2] for m in range(n_ctx)])
                if on_line:
                    if bit == bits[0] and sub == 3 and T["Ka"] == "x3":
                        block = after(block, partials[1])
                    if bit == bits[-1] and T["Ka"] == "c%d" % sub:
                        block = after(block, partials[1])
                    if bit == bits[0] and sub == 3 and T["Kb"] == "x3":
                        block = after(block, partials[2])
                    if bit == bits[-1] and sub == 3 and T["Kb"] == "c3":
                        block = after(block, partials[2])
                    if bit == bits[0] and sub == 2 and T["x2_A"]:
                        block = after(block, near, middle)
                    if bit == bits[-1] and T["c_A"] == sub:
                        block = after(block, near, middle)
                    if bit == bits[-1] and sub in T["c_P"]:
                        block = after(block, *passed)
                    if bit == bits[0] and sub in T["x_P"]:
                        block = after(block, *passed)
                if bit == bits[-1] and mask and T["c_ser"][sub]:
                    block = after(block, latest)
                latest = exchanged(block, "ctx", bit)
                held[mask | bit] = latest
        for mask in range(n_ctx):
            pieces[mask, sub] = held[mask]
        if sub == 1 and on_line:
            partials.append(add_part((0, 1), (0, 1), "part_a"))
            block = lax.slice_in_dim(near, PASSED[0], seg_len, axis=0)
            if T["FK"]:
                block = after(block, partials[1])
            far_middle.append(lax.ppermute(block, "tp", [(1, 2), (2, 1)]))
        if sub == 2 and on_line:
            partials.append(add_part((2,), (0, 1, 2), "part_b"))
    ordered = [pieces[mask, sub] for mask in range(n_ctx) for sub in range(per_part)]

    channels = rate.shape[0]
    groups = channels // 128

    def spread(values):
        lanes = values.T.reshape(-1, groups, 128)
        return jnp.concatenate([lanes, lanes], axis=1)

    rates = spread(rate)
    decay = jnp.exp(-rates)
    gain = spread(pole_gain(rate, residue, float(seq_len)))
    direct = spread(skip[:, None])[0]

    if on_line:
        most = add_part((3,), (3,), "part_c")

    weights = carry(place, order, rates, n_ctx, seg_len)
    kept, given, locals_ = [], [], []
    state = jnp.zeros_like(decay)
    states = []
    for k, (base, rows) in enumerate(zip(starts, CHUNKS)):
        if on_line:
            n, row = 0, base
            while row >= PASSED[n]:
                row -= PASSED[n]
                n += 1
            block = lax.slice_in_dim(far_middle[n], row, row + rows, axis=0)
            if k in T["E"]:
                block = after(block, most)
            last = lax.ppermute(block, "tp", [(1, 0), (2, 3)])
            if k == 0:
                last = after(last, weights)
            if k in T["S"]:
                last = after(last, states[T["S"][k]])
            keep, give = project(
                plan, place, [far_middle[n], last], own, ordered, 0, most, base, rows,
                per_quarter, last_plan(per_quarter, row, rows), "project",
            )
        else:
            block = lax.slice_in_dim(tokens, base, base + rows, axis=0)
            whole = lax.all_gather(block, "tp", axis=0, tiled=False)
            keep, give = project(
                plan, place, [whole], own, ordered, 0, None, 0, rows,
                2 * plan.half_blocks, gathered_plan(per_quarter), "project",
            )
        got = exchanged(give, "fsdp", 1)
        local, state = scan(keep, got, decay, gain, direct, state)
        states.append(state)
        kept.append(keep)
        given.append(got)
        locals_.append(local)

    ends = [state] + [exchanged(state, "ctx", mask) for mask in range(1, n_ctx)]
    return finish(place, ends, weights, decay, locals_, kept, given, seg_len)


def solution(mesh):
    placed = (
        P(("ctx", "fsdp"), "tp"),
        P("fsdp", None, "tp"),
        P(("tp", "fsdp"), None),
        P(("tp", "fsdp"), None),
        P(("tp", "fsdp")),
        P(),
    )
    return jax.shard_map(
        per_device, mesh=mesh, in_specs=placed, out_specs=P(("tp", "fsdp"), "ctx"), check_vma=False
    )
```

```python
import functools
from typing import NamedTuple

import jax
import jax.numpy as jnp
from jax import lax
from jax.experimental import pallas as pl
from jax.experimental.pallas import tpu as pltpu
from jax.sharding import PartitionSpec as P

MIB = 1 << 20
DEPTH = 256
CHUNKS = (256, 256, 256, 256)
PASSED = (512, 512)
T = {'y_y': True, 'y3_c0': True, 'y2_A': False, 'x_x': [0, False, True, False], 'x_c': [0, 0, 1, 1], 'Ka': 'c3', 'x2_A': False, 'c_A': 9, 'c_P': [3], 'x_P': [], 'c_ser': [1, 0, 0, 0], 'E': [], 'FK': True, 'CH': [256, 256, 256, 256], 'S': {}, 'Kb': 'c3', 'cost': {'part_a': 0, 'part_b': 0, 'part_c': 0, 'project': 0}}
FREE = pl.CostEstimate(flops=0, bytes_accessed=0, transcendentals=0)


class Plan(NamedTuple):
    half_blocks: int
    part_blocks: int
    n_parts: int


def exchanged(block, axis, mask):
    count = lax.axis_size(axis)
    return lax.ppermute(block, axis, [(i, i ^ mask) for i in range(count)])


def after(value, *others):
    return lax.optimization_barrier((value, *others))[0]


def pole_gain(rate, residue, length):
    return residue * jnp.sqrt(jnp.maximum(-jnp.expm1(-2.0 * rate), 1.0 / length))


def choose(low, high, number, act):
    if high - low == 1:
        act(low)
        return
    middle = (low + high) // 2

    @pl.when(number < middle)
    def _():
        choose(low, middle, number, act)

    @pl.when(number >= middle)
    def _():
        choose(middle, high, number, act)


def fetch_weights(plan, place, p, block, own, pieces, first, lanes, target, sem):
    pair, ctx = place[0], place[1]
    local = lax.rem(block, plan.half_blocks)
    here = lax.div(block, plan.half_blocks) == pair

    @pl.when(here)
    def _():
        row = pl.multiple_of(local * DEPTH, DEPTH)
        pltpu.make_async_copy(own.at[p, pl.ds(row, DEPTH), lanes], target, sem).start()

    @pl.when(jnp.logical_not(here))
    def _():
        stride = len(pieces) // plan.n_parts
        number = jnp.bitwise_xor(lax.div(local, plan.part_blocks), ctx) * stride
        number = number + lax.rem(local, plan.part_blocks) - first

        def act(n):
            pltpu.make_async_copy(pieces[n].at[p, :, lanes], target, sem).start()

        choose(0, len(pieces), number, act)


def project_kernel(plan, n_inputs, n_pieces, first, base, sides, blocks, x_plan, place, *refs):
    refs = list(refs)
    inputs = [refs.pop(0) for _ in range(n_inputs)]
    own = refs.pop(0)
    pieces = [refs.pop(0) for _ in range(n_pieces)]
    init = refs.pop(0) if base is not None else None
    final = len(sides) > 0
    outs = [refs.pop(0) for _ in range(max(1, len(sides)))]
    x_buf, w_buf, x_sem, w_sem = refs[:4]
    refs = refs[4:]
    if final:
        i_buf, i_sem = refs if init is not None else (None, None)
    else:
        o_buf, o_sem, i_sem = refs
        i_buf = o_buf
    pair, tp = place[0], place[2]
    rows, depth = x_buf.shape
    width = w_buf.shape[2]
    taken = pl.ds(0, width)
    if len(sides) == 1:
        taken = pl.ds(pl.multiple_of((pair if sides[0] == 0 else 1 - pair) * width, 128), width)
    spans = (slice(0, depth // 2), slice(depth // 2, depth))

    def fetch(p):
        if init is not None:
            pltpu.make_async_copy(
                init.at[p, pl.ds(base, rows), taken], i_buf.at[p], i_sem.at[p]
            ).start()
        for part in (0, 1):

            def one(step, carry):
                where = pl.ds(pl.multiple_of(step * DEPTH, DEPTH), DEPTH)
                block = x_plan(tp, step, inputs, x_buf.at[:, where], x_sem.at[part], p == 0)
                target = w_buf.at[p, where, :]
                fetch_weights(
                    plan, place, p, block, own, pieces, first, taken, target, w_sem.at[p, part]
                )
                return carry

            lax.fori_loop(part * blocks // 2, (part + 1) * blocks // 2, one, 0)

    def await_part(p, part):
        if p == 0:
            target = x_buf.at[:, spans[part]]
            pltpu.make_async_copy(target, target, x_sem.at[part]).wait()
        target = w_buf.at[p, spans[part], :]
        pltpu.make_async_copy(target, target, w_sem.at[p, part]).wait()

    fetch(0)
    fetch(1)
    for p in range(3):
        if init is not None:
            pltpu.make_async_copy(i_buf.at[p], i_buf.at[p], i_sem.at[p]).wait()
        await_part(p, 0)
        if p:
            await_part(p, 1)
        if not final:
            chunk = min(rows, 256)

            def multiply(span, add, m, carry):
                some = pl.ds(pl.multiple_of(m * chunk, chunk), chunk)
                new = jnp.dot(
                    x_buf[some, span], w_buf[p, span, :], preferred_element_type=jnp.float32
                )
                if add or init is not None:
                    new = o_buf[p, some, :] + new
                o_buf[p, some, :] = new
                return carry

            if p == 0:
                lax.fori_loop(0, rows // chunk, functools.partial(multiply, spans[0], False), 0)
                await_part(0, 1)
                fetch(2)
                lax.fori_loop(0, rows // chunk, functools.partial(multiply, spans[1], True), 0)
            else:
                whole = slice(0, depth)
                lax.fori_loop(0, rows // chunk, functools.partial(multiply, whole, False), 0)
            pltpu.make_async_copy(o_buf.at[p], outs[0].at[p], o_sem.at[p]).start()
            continue
        half = outs[0].shape[2]
        lanes = [pl.ds(pl.multiple_of(x * half, 128), half) for x in (pair, 1 - pair)]
        if len(sides) == 1:
            lanes = [pl.ds(0, half)]

        def product(span, n):
            return jnp.dot(
                x_buf[:, span], w_buf[p, span, lanes[n]], preferred_element_type=jnp.float32
            )

        if p == 0:
            early = [product(spans[0], n) for n in range(len(sides))]
            await_part(0, 1)
            fetch(2)
            sums = [early[n] + product(spans[1], n) for n in range(len(sides))]
        else:
            sums = [product(slice(0, depth), n) for n in range(len(sides))]
        for n, side in enumerate(sides):
            new, out = sums[n], outs[n]
            if init is not None:
                new = i_buf[p, :, lanes[n]] + new
            new = new.astype(jnp.bfloat16)
            if side == 0 or p == 0:
                out[p] = new
            elif p == 1:
                out[1] = new
            else:
                both = out[1].astype(jnp.float32) * new.astype(jnp.float32)
                out[1] = both.astype(jnp.bfloat16)
    if not final:
        for p in range(3):
            pltpu.make_async_copy(o_buf.at[p], outs[0].at[p], o_sem.at[p]).wait()


def project(
    plan, place, inputs, own, pieces, first, init, base, rows, blocks, x_plan, name, sides=(0, 1)
):
    final = name == "project"
    sides = sides if final else ()
    width = own.shape[2]
    anywhere = pl.BlockSpec(memory_space=pl.ANY)
    local = pl.BlockSpec(memory_space=pltpu.VMEM)
    operands = list(inputs) + [own] + list(pieces) + ([] if init is None else [init])
    depth = blocks * DEPTH
    half = width // 2
    if len(sides) == 1:
        width = half
    total = (3, rows, width)
    scratch = [
        pltpu.VMEM((rows, depth), jnp.bfloat16),
        pltpu.VMEM((3, depth, width), jnp.bfloat16),
        pltpu.SemaphoreType.DMA((2,)),
        pltpu.SemaphoreType.DMA((3, 2)),
    ]
    if final:
        if init is not None:
            scratch += [pltpu.VMEM(total, jnp.float32), pltpu.SemaphoreType.DMA((3,))]
        out_shape = [
            jax.ShapeDtypeStruct((3 - side, rows, half), jnp.bfloat16) for side in sides
        ]
    else:
        scratch += [pltpu.VMEM(total, jnp.float32)] + [pltpu.SemaphoreType.DMA((3,))] * 2
        out_shape = jax.ShapeDtypeStruct(total, jnp.float32)
    return pl.pallas_call(
        functools.partial(
            project_kernel, plan, len(inputs), len(pieces), first,
            None if init is None else base, sides, blocks, x_plan,
        ),
        grid_spec=pltpu.PrefetchScalarGridSpec(
            num_scalar_prefetch=1,
            grid=(),
            in_specs=[anywhere] * len(operands),
            out_specs=[local] * len(sides) if final else anywhere,
            scratch_shapes=scratch,
        ),
        out_shape=out_shape,
        compiler_params=pltpu.CompilerParams(vmem_limit_bytes=56 * MIB),
        cost_estimate=pl.CostEstimate(
            flops=T["cost"][name], bytes_accessed=0, transcendentals=0
        ),
        name=name,
    )(place, *operands)


def columns(quarter_block):
    return pl.ds(pl.multiple_of(quarter_block * DEPTH, DEPTH), DEPTH)


def gathered_plan(per_quarter):
    def plan(tp, step, inputs, target, sem, copy):
        source = inputs[0].at[lax.div(step, per_quarter), :, columns(lax.rem(step, per_quarter))]
        if copy:
            pltpu.make_async_copy(source, target, sem).start()
        return step

    return plan


def line_ends(tp):
    return (tp == 0) | (tp == 3)


def near_block(plan, tp, step, subs, base, inputs, target, sem, copy):
    span = plan.half_blocks // 2 // plan.part_blocks
    place = lax.div(step, len(subs))
    sub = subs[0] + lax.rem(step, len(subs))
    mine = place < span
    side = jnp.where(mine, lax.rem(tp, 2), 1 - lax.rem(tp, 2))
    within = lax.rem(place, span) * plan.part_blocks + sub
    block = lax.div(tp, 2) * plan.half_blocks + side * span * plan.part_blocks + within
    if not copy:
        return block
    where = columns(within)
    for at, source in ((True, inputs[0]), (False, inputs[1])):
        @pl.when(mine == at)
        def _():
            rows = pl.ds(base, target.shape[0])
            pltpu.make_async_copy(source.at[rows, where], target, sem).start()

    return block


def near_plan(plan, subs, base):
    def x_plan(tp, step, inputs, target, sem, copy):
        return near_block(plan, tp, step, subs, base, inputs, target, sem, copy)

    return x_plan


def middle_plan(plan, subs, late_subs):
    span = plan.half_blocks // plan.part_blocks * len(subs)
    per_quarter = plan.half_blocks // 2

    def x_plan(tp, step, inputs, target, sem, copy):
        middle, ends = inputs[2:]
        late = step - span
        early = jnp.minimum(step, span - 1)
        near = near_block(plan, tp, early, subs, 0, inputs, target, sem, False)
        part, sub = lax.div(late, len(late_subs)), lax.rem(late, len(late_subs))
        within = jnp.maximum(part * plan.part_blocks + late_subs[0] + sub, 0)
        block = jnp.where(late < 0, near, (2 - lax.div(tp, 2)) * per_quarter + within)
        if not copy:
            return block
        where = columns(within)

        @pl.when(late < 0)
        def _():
            near_block(plan, tp, early, subs, 0, inputs, target, sem, True)

        for at_end, source in ((False, middle), (True, ends)):
            @pl.when((late >= 0) & (line_ends(tp) == at_end))
            def _():
                pltpu.make_async_copy(source.at[:, where], target, sem).start()

        return block

    return x_plan


def last_plan(per_quarter, row, rows):
    def plan(tp, step, inputs, target, sem, copy):
        block = jnp.where(tp < 2, 3, 0) * per_quarter + step
        if not copy:
            return block
        middle, ends = inputs
        where = columns(step)

        @pl.when(line_ends(tp))
        def _():
            pltpu.make_async_copy(ends.at[:, where], target, sem).start()

        @pl.when(jnp.logical_not(line_ends(tp)))
        def _():
            pltpu.make_async_copy(middle.at[pl.ds(row, rows), where], target, sem).start()

        return block

    return plan


def scan_kernel(kept, given, decay, gain, skip, state_in, local_ref, state_out, prod):
    poles = decay.shape[0]
    rows = kept.shape[1]
    groups = kept.shape[2] // 128
    for side, ref in enumerate((kept, given)):
        for g in range(groups):
            lanes = slice(g * 128, (g + 1) * 128)
            product = ref[1, :, lanes].astype(jnp.float32)
            if side == 0:
                product = product * ref[2, :, lanes].astype(jnp.float32)
            prod[:, side * groups + g, :] = product
    direct = skip[...]
    factors = [decay[r] for r in range(poles)]
    gains = [gain[r] for r in range(poles)]

    def step(t, states):
        p = prod[t]
        new = [factors[r] * states[r] + gains[r] * p for r in range(poles)]
        total = list(new)
        while len(total) > 1:
            total = [a + b for a, b in zip(total[::2], total[1::2])]
        local_ref[t] = total[0] + direct * p
        return tuple(new)

    states = lax.fori_loop(0, rows, step, tuple(state_in[r] for r in range(poles)), unroll=8)
    for r in range(poles):
        state_out[r] = states[r]


def scan(kept, given, decay, gain, skip, state):
    rows = kept.shape[1]
    local = pl.BlockSpec(memory_space=pltpu.VMEM)
    lanes = decay.shape[1:]
    return pl.pallas_call(
        scan_kernel,
        in_specs=[local] * 6,
        out_specs=[local] * 2,
        out_shape=[
            jax.ShapeDtypeStruct((rows,) + lanes, jnp.float32),
            jax.ShapeDtypeStruct(decay.shape, jnp.float32),
        ],
        scratch_shapes=[pltpu.VMEM((rows,) + lanes, jnp.float32)],
        compiler_params=pltpu.CompilerParams(vmem_limit_bytes=24 * MIB),
        cost_estimate=FREE,
        name="scan",
    )(kept, given, decay, gain, skip, state)


def carry_kernel(n_ctx, seg_len, place, order, rate, weights):
    poles, sublanes, _ = rate.shape
    pair, ctx = place[0], place[1]
    upper = lax.broadcasted_iota(jnp.int32, rate.shape[1:], 0) < sublanes // 2
    targets = (order[2 * ctx + pair], order[2 * ctx + 1 - pair])
    for mask in range(n_ctx):
        origin = jnp.bitwise_xor(ctx, mask)
        sources = (order[2 * origin + pair], order[2 * origin + 1 - pair])
        for cross in (0, 1):
            gaps = [targets[s] - 1 - sources[s ^ cross] for s in (0, 1)]
            gap = jnp.where(upper, gaps[0], gaps[1])
            span = jnp.maximum(gap, 0).astype(jnp.float32) * seg_len
            for r in range(poles):
                weights[mask, cross, r] = jnp.where(gap >= 0, jnp.exp(-rate[r] * span), 0.0)


def carry(place, order, rate, n_ctx, seg_len):
    local = pl.BlockSpec(memory_space=pltpu.VMEM)
    return pl.pallas_call(
        functools.partial(carry_kernel, n_ctx, seg_len),
        grid_spec=pltpu.PrefetchScalarGridSpec(
            num_scalar_prefetch=2, grid=(), in_specs=[local], out_specs=local
        ),
        out_shape=jax.ShapeDtypeStruct((n_ctx, 2) + rate.shape, jnp.float32),
        cost_estimate=FREE,
        name="carry",
    )(place, order, rate)


def finish_kernel(n_ctx, n_chunks, seg_len, place, *refs):
    refs = list(refs)
    ends = [refs.pop(0) for _ in range(n_ctx)]
    weights = refs.pop(0)
    decay = refs.pop(0)
    locals_ = [refs.pop(0) for _ in range(n_chunks)]
    kept = [refs.pop(0) for _ in range(n_chunks)]
    given = [refs.pop(0) for _ in range(n_chunks)]
    out = refs.pop(0)
    conv = refs.pop(0)
    poles, sublanes, _ = decay.shape
    groups = sublanes // 2
    pair = place[0]
    states = [jnp.zeros(decay.shape[1:], jnp.float32) for _ in range(poles)]
    for mask in range(n_ctx):
        for r in range(poles):
            end = ends[mask][r]
            turned = jnp.concatenate([end[groups:], end[:groups]], axis=0)
            states[r] = states[r] + weights[mask, 0, r] * end + weights[mask, 1, r] * turned
    factors = [decay[r] for r in range(poles)]
    states = tuple(states)
    base = 0
    for k in range(n_chunks):
        rows = locals_[k].shape[0]

        def step(t, states):
            new = [factors[r] * states[r] for r in range(poles)]
            total = list(new)
            while len(total) > 1:
                total = [a + b for a, b in zip(total[::2], total[1::2])]
            conv[t] = total[0] + locals_[k][t]
            return tuple(new)

        states = lax.fori_loop(0, rows, step, states, unroll=8)
        for side, ref in enumerate((kept[k], given[k])):
            segment = pair if side == 0 else 1 - pair
            column = pl.multiple_of(segment * seg_len + base, 128)
            for g in range(groups):
                lanes = slice(g * 128, (g + 1) * 128)
                query = ref[0, :, lanes].astype(jnp.float32)
                gated = query * conv[:rows, side * groups + g, :]
                out[lanes, pl.ds(column, rows)] = gated.T.astype(jnp.bfloat16)
        base += rows


def finish(place, ends, weights, decay, locals_, kept, given, seg_len):
    n_chunks = len(locals_)
    local = pl.BlockSpec(memory_space=pltpu.VMEM)
    operands = list(ends) + [weights, decay] + list(locals_) + list(kept) + list(given)
    lanes = decay.shape[1:]
    channels = kept[0].shape[2]
    longest = max(k.shape[1] for k in kept)
    return pl.pallas_call(
        functools.partial(finish_kernel, len(ends), n_chunks, seg_len),
        grid_spec=pltpu.PrefetchScalarGridSpec(
            num_scalar_prefetch=1,
            grid=(),
            in_specs=[local] * len(operands),
            out_specs=local,
            scratch_shapes=[pltpu.VMEM((longest,) + lanes, jnp.float32)],
        ),
        out_shape=jax.ShapeDtypeStruct((channels, 2 * seg_len), jnp.bfloat16),
        compiler_params=pltpu.CompilerParams(vmem_limit_bytes=40 * MIB),
        cost_estimate=pl.CostEstimate(
            flops=32 * seg_len * lanes[0] * lanes[1],
            bytes_accessed=seg_len * lanes[0] * lanes[1] * 8,
            transcendentals=0,
        ),
        name="finish",
    )(place, *operands)


def per_device(tokens, weight, rate, residue, skip, order):
    seg_len = tokens.shape[0]
    n_ctx = lax.axis_size("ctx")
    seq_len = 2 * n_ctx * seg_len
    pair_index = lax.axis_index("fsdp")
    ctx_index = lax.axis_index("ctx")
    place = jnp.stack([pair_index, ctx_index, lax.axis_index("tp")]).astype(jnp.int32)

    starts = [sum(CHUNKS[:k]) for k in range(len(CHUNKS))]
    on_line = lax.axis_size("tp") == 4 and n_ctx == 4
    passed = []
    if on_line:
        near = lax.ppermute(tokens, "tp", [(0, 1), (1, 0), (2, 3), (3, 2)])
        middle = lax.ppermute(tokens, "tp", [(1, 2), (2, 1)])
        ends = lax.ppermute(middle, "tp", [(1, 0), (2, 3)])
        block = lax.slice_in_dim(near, 0, PASSED[0], axis=0)
        far_middle = [lax.ppermute(block, "tp", [(1, 2), (2, 1)])]
        passed = [ends] + far_middle

    own = weight.transpose(1, 0, 2)
    part = own.shape[1] // n_ctx
    piece_len = DEPTH
    per_part = part // piece_len
    plan = Plan(own.shape[1] // DEPTH, part // DEPTH, n_ctx)
    per_quarter = tokens.shape[1] // DEPTH
    partials = [None]

    def add_part(subs, late_subs, name):
        known = range(max(late_subs) + 1) if subs[0] < per_part - 1 else subs
        some = [pieces[m, n] for m in range(n_ctx) for n in known]
        sources, x_plan = [tokens, near], near_plan(plan, subs, 0)
        if name != "part_a":
            sources, x_plan = sources + [middle, ends], middle_plan(plan, subs, late_subs)
        units = n_ctx * len(subs) + (n_ctx // 2 * len(late_subs) if name != "part_a" else 0)
        return project(
            plan, place, sources, own, some, known[0], partials[-1], 0, seg_len, units, x_plan, name
        )

    pieces = {}
    bits = []
    while 1 << len(bits) < n_ctx:
        bits.insert(0, 1 << len(bits))
    first = []
    for sub in range(per_part):
        piece = lax.dynamic_slice_in_dim(own, ctx_index * part + sub * piece_len, piece_len, 1)
        if sub >= 2 and T["y_y"]:
            piece = after(piece, first[sub - 2])
        if sub == 3 and T["y3_c0"]:
            piece = after(piece, *[pieces[m, 0] for m in range(n_ctx)])
        if sub == 2 and T["y2_A"] and on_line:
            piece = after(piece, near, middle)
        first.append(exchanged(piece, "fsdp", 1))
        held = {0: first[sub]}
        for bit in bits:
            for mask in list(held):
                block = held[mask]
                if bit == bits[0] and sub and T["x_x"][sub]:
                    block = after(block, pieces[bit, sub - 1])
                if bit == bits[0] and sub >= 2 and T["x_c"][sub]:
                    block = after(block, *[pieces[m, sub - 2] for m in range(n_ctx)])
                if on_line:
                    if bit == bits[0] and sub == 3 and T["Ka"] == "x3":
                        block = after(block, partials[1])
                    if bit == bits[-1] and T["Ka"] == "c%d" % sub:
                        block = after(block, partials[1])
                    if bit == bits[0] and sub == 3 and T["Kb"] == "x3":
                        block = after(block, partials[2])
                    if bit == bits[-1] and sub == 3 and T["Kb"] == "c3":
                        block = after(block, partials[2])
                    if bit == bits[0] and sub == 2 and T["x2_A"]:
                        block = after(block, near, middle)
                    if bit == bits[-1] and T["c_A"] == sub:
                        block = after(block, near, middle)
                    if bit == bits[-1] and sub in T["c_P"]:
                        block = after(block, *passed)
                    if bit == bits[0] and sub in T["x_P"]:
                        block = after(block, *passed)
                if bit == bits[-1] and mask and T["c_ser"][sub]:
                    block = after(block, latest)
                latest = exchanged(block, "ctx", bit)
                held[mask | bit] = latest
        for mask in range(n_ctx):
            pieces[mask, sub] = held[mask]
        if sub == 1 and on_line:
            partials.append(add_part((0, 1), (0, 1), "part_a"))
            block = lax.slice_in_dim(near, PASSED[0], seg_len, axis=0)
            if T["FK"]:
                block = after(block, partials[1])
            far_middle.append(lax.ppermute(block, "tp", [(1, 2), (2, 1)]))
        if sub == 2 and on_line:
            partials.append(add_part((2,), (0, 1, 2), "part_b"))
    ordered = [pieces[mask, sub] for mask in range(n_ctx) for sub in range(per_part)]

    channels = rate.shape[0]
    groups = channels // 128

    def spread(values):
        lanes = values.T.reshape(-1, groups, 128)
        return jnp.concatenate([lanes, lanes], axis=1)

    rates = spread(rate)
    decay = jnp.exp(-rates)
    gain = spread(pole_gain(rate, residue, float(seq_len)))
    direct = spread(skip[:, None])[0]

    if on_line:
        most = add_part((3,), (3,), "part_c")

    weights = carry(place, order, rates, n_ctx, seg_len)
    kept, given, locals_ = [], [], []
    state = jnp.zeros_like(decay)
    states = []
    for k, (base, rows) in enumerate(zip(starts, CHUNKS)):
        if on_line:
            n, row = 0, base
            while row >= PASSED[n]:
                row -= PASSED[n]
                n += 1
            block = lax.slice_in_dim(far_middle[n], row, row + rows, axis=0)
            if k in T["E"]:
                block = after(block, most)
            last = lax.ppermute(block, "tp", [(1, 0), (2, 3)])
            if k == 0:
                last = after(last, weights)
            if k in T["S"]:
                last = after(last, states[T["S"][k]])

            def last_part(x, sides):
                return project(
                    plan, place, [far_middle[n], x], own, ordered, 0, most, base, rows,
                    per_quarter, last_plan(per_quarter, row, rows), "project", sides,
                )

            if k < len(CHUNKS) - 1:
                keep, give = last_part(last, (0, 1))
            else:
                (give,) = last_part(last, (1,))
                (keep,) = last_part(after(last, give), (0,))
        else:
            block = lax.slice_in_dim(tokens, base, base + rows, axis=0)
            whole = lax.all_gather(block, "tp", axis=0, tiled=False)
            keep, give = project(
                plan, place, [whole], own, ordered, 0, None, 0, rows,
                2 * plan.half_blocks, gathered_plan(per_quarter), "project",
            )
        got = exchanged(give, "fsdp", 1)
        local, state = scan(keep, got, decay, gain, direct, state)
        states.append(state)
        kept.append(keep)
        given.append(got)
        locals_.append(local)

    ends = [state] + [exchanged(state, "ctx", mask) for mask in range(1, n_ctx)]
    return finish(place, ends, weights, decay, locals_, kept, given, seg_len)


def solution(mesh):
    placed = (
        P(("ctx", "fsdp"), "tp"),
        P("fsdp", None, "tp"),
        P(("tp", "fsdp"), None),
        P(("tp", "fsdp"), None),
        P(("tp", "fsdp")),
        P(),
    )
    return jax.shard_map(
        per_device, mesh=mesh, in_specs=placed, out_specs=P(("tp", "fsdp"), "ctx"), check_vma=False
    )
```

```python
import functools
from typing import NamedTuple

import jax
import jax.numpy as jnp
from jax import lax
from jax.experimental import pallas as pl
from jax.experimental.pallas import tpu as pltpu
from jax.sharding import PartitionSpec as P

MIB = 1 << 20
DEPTH = 256
CHUNKS = (256, 256, 256, 256)
PASSED = (512, 512)
T = {'y_y': True, 'y3_c0': True, 'y2_A': False, 'x_x': [0, False, True, False], 'x_c': [0, 0, 1, 1], 'Ka': 'c3', 'x2_A': False, 'c_A': 9, 'c_P': [3], 'x_P': [], 'c_ser': [1, 0, 0, 0], 'E': [], 'FK': True, 'CH': [256, 256, 256, 256], 'S': {}, 'Kb': 'c3', 'cost': {'part_a': 0, 'part_b': 0, 'part_c': 0, 'project': 0}}
FREE = pl.CostEstimate(flops=0, bytes_accessed=0, transcendentals=0)


class Plan(NamedTuple):
    half_blocks: int
    part_blocks: int
    n_parts: int


def exchanged(block, axis, mask):
    count = lax.axis_size(axis)
    return lax.ppermute(block, axis, [(i, i ^ mask) for i in range(count)])


def after(value, *others):
    return lax.optimization_barrier((value, *others))[0]


def pole_gain(rate, residue, length):
    return residue * jnp.sqrt(jnp.maximum(-jnp.expm1(-2.0 * rate), 1.0 / length))


def choose(low, high, number, act):
    if high - low == 1:
        act(low)
        return
    middle = (low + high) // 2

    @pl.when(number < middle)
    def _():
        choose(low, middle, number, act)

    @pl.when(number >= middle)
    def _():
        choose(middle, high, number, act)


def fetch_weights(plan, place, p, block, own, pieces, first, lanes, target, sem):
    pair, ctx = place[0], place[1]
    local = lax.rem(block, plan.half_blocks)
    here = lax.div(block, plan.half_blocks) == pair

    @pl.when(here)
    def _():
        row = pl.multiple_of(local * DEPTH, DEPTH)
        pltpu.make_async_copy(own.at[p, pl.ds(row, DEPTH), lanes], target, sem).start()

    @pl.when(jnp.logical_not(here))
    def _():
        stride = len(pieces) // plan.n_parts
        number = jnp.bitwise_xor(lax.div(local, plan.part_blocks), ctx) * stride
        number = number + lax.rem(local, plan.part_blocks) - first

        def act(n):
            pltpu.make_async_copy(pieces[n].at[p, :, lanes], target, sem).start()

        choose(0, len(pieces), number, act)


def project_kernel(plan, n_inputs, n_pieces, first, base, sides, blocks, x_plan, place, *refs):
    refs = list(refs)
    inputs = [refs.pop(0) for _ in range(n_inputs)]
    own = refs.pop(0)
    pieces = [refs.pop(0) for _ in range(n_pieces)]
    init = refs.pop(0) if base is not None else None
    final = len(sides) > 0
    outs = [refs.pop(0) for _ in range(max(1, len(sides)))]
    x_buf, w_buf, x_sem, w_sem = refs[:4]
    refs = refs[4:]
    if final:
        i_buf, i_sem = refs if init is not None else (None, None)
    else:
        o_buf, o_sem, i_sem = refs
        i_buf = o_buf
    pair, tp = place[0], place[2]
    rows, depth = x_buf.shape
    width = w_buf.shape[2]
    taken = pl.ds(0, width)
    if len(sides) == 1:
        taken = pl.ds(pl.multiple_of((pair if sides[0] == 0 else 1 - pair) * width, 128), width)
    spans = (slice(0, depth // 2), slice(depth // 2, depth))

    def fetch(p):
        if init is not None:
            pltpu.make_async_copy(
                init.at[p, pl.ds(base, rows), taken], i_buf.at[p], i_sem.at[p]
            ).start()
        for part in (0, 1):

            def one(step, carry):
                where = pl.ds(pl.multiple_of(step * DEPTH, DEPTH), DEPTH)
                block = x_plan(tp, step, inputs, x_buf.at[:, where], x_sem.at[part], p == 0)
                target = w_buf.at[p, where, :]
                fetch_weights(
                    plan, place, p, block, own, pieces, first, taken, target, w_sem.at[p, part]
                )
                return carry

            lax.fori_loop(part * blocks // 2, (part + 1) * blocks // 2, one, 0)

    def await_part(p, part):
        if p == 0:
            target = x_buf.at[:, spans[part]]
            pltpu.make_async_copy(target, target, x_sem.at[part]).wait()
        target = w_buf.at[p, spans[part], :]
        pltpu.make_async_copy(target, target, w_sem.at[p, part]).wait()

    fetch(0)
    fetch(1)
    for p in range(3):
        if init is not None:
            pltpu.make_async_copy(i_buf.at[p], i_buf.at[p], i_sem.at[p]).wait()
        await_part(p, 0)
        if p:
            await_part(p, 1)
        if not final:
            chunk = min(rows, 256)

            def multiply(span, add, m, carry):
                some = pl.ds(pl.multiple_of(m * chunk, chunk), chunk)
                new = jnp.dot(
                    x_buf[some, span], w_buf[p, span, :], preferred_element_type=jnp.float32
                )
                if add or init is not None:
                    new = o_buf[p, some, :] + new
                o_buf[p, some, :] = new
                return carry

            if p == 0:
                lax.fori_loop(0, rows // chunk, functools.partial(multiply, spans[0], False), 0)
                await_part(0, 1)
                fetch(2)
                lax.fori_loop(0, rows // chunk, functools.partial(multiply, spans[1], True), 0)
            else:
                whole = slice(0, depth)
                lax.fori_loop(0, rows // chunk, functools.partial(multiply, whole, False), 0)
            pltpu.make_async_copy(o_buf.at[p], outs[0].at[p], o_sem.at[p]).start()
            continue
        half = outs[0].shape[2]
        lanes = [pl.ds(pl.multiple_of(x * half, 128), half) for x in (pair, 1 - pair)]
        if len(sides) == 1:
            lanes = [pl.ds(0, half)]

        def product(span, n):
            return jnp.dot(
                x_buf[:, span], w_buf[p, span, lanes[n]], preferred_element_type=jnp.float32
            )

        if p == 0:
            early = [product(spans[0], n) for n in range(len(sides))]
            await_part(0, 1)
            fetch(2)
            sums = [early[n] + product(spans[1], n) for n in range(len(sides))]
        else:
            sums = [product(slice(0, depth), n) for n in range(len(sides))]
        for n, side in enumerate(sides):
            new, out = sums[n], outs[n]
            if init is not None:
                new = i_buf[p, :, lanes[n]] + new
            new = new.astype(jnp.bfloat16)
            if side == 0 or p == 0:
                out[p] = new
            elif p == 1:
                out[1] = new
            else:
                both = out[1].astype(jnp.float32) * new.astype(jnp.float32)
                out[1] = both.astype(jnp.bfloat16)
    if not final:
        for p in range(3):
            pltpu.make_async_copy(o_buf.at[p], outs[0].at[p], o_sem.at[p]).wait()


def project(
    plan, place, inputs, own, pieces, first, init, base, rows, blocks, x_plan, name, sides=(0, 1)
):
    final = name == "project"
    sides = sides if final else ()
    width = own.shape[2]
    anywhere = pl.BlockSpec(memory_space=pl.ANY)
    local = pl.BlockSpec(memory_space=pltpu.VMEM)
    operands = list(inputs) + [own] + list(pieces) + ([] if init is None else [init])
    depth = blocks * DEPTH
    half = width // 2
    if len(sides) == 1:
        width = half
    total = (3, rows, width)
    scratch = [
        pltpu.VMEM((rows, depth), jnp.bfloat16),
        pltpu.VMEM((3, depth, width), jnp.bfloat16),
        pltpu.SemaphoreType.DMA((2,)),
        pltpu.SemaphoreType.DMA((3, 2)),
    ]
    if final:
        if init is not None:
            scratch += [pltpu.VMEM(total, jnp.float32), pltpu.SemaphoreType.DMA((3,))]
        out_shape = [
            jax.ShapeDtypeStruct((3 - side, rows, half), jnp.bfloat16) for side in sides
        ]
    else:
        scratch += [pltpu.VMEM(total, jnp.float32)] + [pltpu.SemaphoreType.DMA((3,))] * 2
        out_shape = jax.ShapeDtypeStruct(total, jnp.float32)
    return pl.pallas_call(
        functools.partial(
            project_kernel, plan, len(inputs), len(pieces), first,
            None if init is None else base, sides, blocks, x_plan,
        ),
        grid_spec=pltpu.PrefetchScalarGridSpec(
            num_scalar_prefetch=1,
            grid=(),
            in_specs=[anywhere] * len(operands),
            out_specs=[local] * len(sides) if final else anywhere,
            scratch_shapes=scratch,
        ),
        out_shape=out_shape,
        compiler_params=pltpu.CompilerParams(vmem_limit_bytes=56 * MIB),
        cost_estimate=pl.CostEstimate(
            flops=T["cost"][name], bytes_accessed=0, transcendentals=0
        ),
        name=name,
    )(place, *operands)


def columns(quarter_block):
    return pl.ds(pl.multiple_of(quarter_block * DEPTH, DEPTH), DEPTH)


def gathered_plan(per_quarter):
    def plan(tp, step, inputs, target, sem, copy):
        source = inputs[0].at[lax.div(step, per_quarter), :, columns(lax.rem(step, per_quarter))]
        if copy:
            pltpu.make_async_copy(source, target, sem).start()
        return step

    return plan


def line_ends(tp):
    return (tp == 0) | (tp == 3)


def near_block(plan, tp, step, subs, base, inputs, target, sem, copy):
    span = plan.half_blocks // 2 // plan.part_blocks
    place = lax.div(step, len(subs))
    sub = subs[0] + lax.rem(step, len(subs))
    mine = place < span
    side = jnp.where(mine, lax.rem(tp, 2), 1 - lax.rem(tp, 2))
    within = lax.rem(place, span) * plan.part_blocks + sub
    block = lax.div(tp, 2) * plan.half_blocks + side * span * plan.part_blocks + within
    if not copy:
        return block
    where = columns(within)
    for at, source in ((True, inputs[0]), (False, inputs[1])):
        @pl.when(mine == at)
        def _():
            rows = pl.ds(base, target.shape[0])
            pltpu.make_async_copy(source.at[rows, where], target, sem).start()

    return block


def near_plan(plan, subs, base):
    def x_plan(tp, step, inputs, target, sem, copy):
        return near_block(plan, tp, step, subs, base, inputs, target, sem, copy)

    return x_plan


def middle_plan(plan, subs, late_subs):
    span = plan.half_blocks // plan.part_blocks * len(subs)
    per_quarter = plan.half_blocks // 2

    def x_plan(tp, step, inputs, target, sem, copy):
        middle, ends = inputs[2:]
        late = step - span
        early = jnp.minimum(step, span - 1)
        near = near_block(plan, tp, early, subs, 0, inputs, target, sem, False)
        part, sub = lax.div(late, len(late_subs)), lax.rem(late, len(late_subs))
        within = jnp.maximum(part * plan.part_blocks + late_subs[0] + sub, 0)
        block = jnp.where(late < 0, near, (2 - lax.div(tp, 2)) * per_quarter + within)
        if not copy:
            return block
        where = columns(within)

        @pl.when(late < 0)
        def _():
            near_block(plan, tp, early, subs, 0, inputs, target, sem, True)

        for at_end, source in ((False, middle), (True, ends)):
            @pl.when((late >= 0) & (line_ends(tp) == at_end))
            def _():
                pltpu.make_async_copy(source.at[:, where], target, sem).start()

        return block

    return x_plan


def last_plan(per_quarter, row, rows):
    def plan(tp, step, inputs, target, sem, copy):
        block = jnp.where(tp < 2, 3, 0) * per_quarter + step
        if not copy:
            return block
        middle, ends = inputs
        where = columns(step)

        @pl.when(line_ends(tp))
        def _():
            pltpu.make_async_copy(ends.at[:, where], target, sem).start()

        @pl.when(jnp.logical_not(line_ends(tp)))
        def _():
            pltpu.make_async_copy(middle.at[pl.ds(row, rows), where], target, sem).start()

        return block

    return plan


def scan_kernel(kept, given, decay, gain, skip, state_in, local_ref, state_out, prod):
    poles = decay.shape[0]
    rows = kept.shape[1]
    groups = kept.shape[2] // 128
    for side, ref in enumerate((kept, given)):
        for g in range(groups):
            lanes = slice(g * 128, (g + 1) * 128)
            product = ref[1, :, lanes].astype(jnp.float32)
            if side == 0:
                product = product * ref[2, :, lanes].astype(jnp.float32)
            prod[:, side * groups + g, :] = product
    direct = skip[...]
    factors = [decay[r] for r in range(poles)]
    gains = [gain[r] for r in range(poles)]

    def step(t, states):
        p = prod[t]
        new = [factors[r] * states[r] + gains[r] * p for r in range(poles)]
        total = list(new)
        while len(total) > 1:
            total = [a + b for a, b in zip(total[::2], total[1::2])]
        local_ref[t] = total[0] + direct * p
        return tuple(new)

    states = lax.fori_loop(0, rows, step, tuple(state_in[r] for r in range(poles)), unroll=8)
    for r in range(poles):
        state_out[r] = states[r]


def scan(kept, given, decay, gain, skip, state):
    rows = kept.shape[1]
    local = pl.BlockSpec(memory_space=pltpu.VMEM)
    lanes = decay.shape[1:]
    return pl.pallas_call(
        scan_kernel,
        in_specs=[local] * 6,
        out_specs=[local] * 2,
        out_shape=[
            jax.ShapeDtypeStruct((rows,) + lanes, jnp.float32),
            jax.ShapeDtypeStruct(decay.shape, jnp.float32),
        ],
        scratch_shapes=[pltpu.VMEM((rows,) + lanes, jnp.float32)],
        compiler_params=pltpu.CompilerParams(vmem_limit_bytes=24 * MIB),
        cost_estimate=FREE,
        name="scan",
    )(kept, given, decay, gain, skip, state)


def carry_kernel(n_ctx, seg_len, place, order, rate, weights):
    poles, sublanes, _ = rate.shape
    pair, ctx = place[0], place[1]
    upper = lax.broadcasted_iota(jnp.int32, rate.shape[1:], 0) < sublanes // 2
    targets = (order[2 * ctx + pair], order[2 * ctx + 1 - pair])
    for mask in range(n_ctx):
        origin = jnp.bitwise_xor(ctx, mask)
        sources = (order[2 * origin + pair], order[2 * origin + 1 - pair])
        for cross in (0, 1):
            gaps = [targets[s] - 1 - sources[s ^ cross] for s in (0, 1)]
            gap = jnp.where(upper, gaps[0], gaps[1])
            span = jnp.maximum(gap, 0).astype(jnp.float32) * seg_len
            for r in range(poles):
                weights[mask, cross, r] = jnp.where(gap >= 0, jnp.exp(-rate[r] * span), 0.0)


def carry(place, order, rate, n_ctx, seg_len):
    local = pl.BlockSpec(memory_space=pltpu.VMEM)
    return pl.pallas_call(
        functools.partial(carry_kernel, n_ctx, seg_len),
        grid_spec=pltpu.PrefetchScalarGridSpec(
            num_scalar_prefetch=2, grid=(), in_specs=[local], out_specs=local
        ),
        out_shape=jax.ShapeDtypeStruct((n_ctx, 2) + rate.shape, jnp.float32),
        cost_estimate=FREE,
        name="carry",
    )(place, order, rate)


def finish_kernel(n_ctx, n_chunks, seg_len, place, *refs):
    refs = list(refs)
    ends = [refs.pop(0) for _ in range(n_ctx)]
    weights = refs.pop(0)
    decay = refs.pop(0)
    locals_ = [refs.pop(0) for _ in range(n_chunks)]
    kept = [refs.pop(0) for _ in range(n_chunks)]
    given = [refs.pop(0) for _ in range(n_chunks)]
    out, conv, queries = refs
    poles, sublanes, _ = decay.shape
    groups = sublanes // 2
    pair = place[0]
    states = [jnp.zeros(decay.shape[1:], jnp.float32) for _ in range(poles)]
    for mask in range(n_ctx):
        for r in range(poles):
            end = ends[mask][r]
            turned = jnp.concatenate([end[groups:], end[:groups]], axis=0)
            states[r] = states[r] + weights[mask, 0, r] * end + weights[mask, 1, r] * turned
    factors = [decay[r] for r in range(poles)]
    states = tuple(states)
    rows = locals_[0].shape[0]
    per_lane = rows // 128
    tiles = sublanes * per_lane
    span = rows // tiles
    for k in range(n_chunks + 1):
        now, before = k % 2, (k + 1) % 2
        if k < n_chunks:
            queries[now, 0] = kept[k][0]
            queries[now, 1] = given[k][0]

        def body(tile, states):
            if k > 0:
                lane, part = lax.div(tile, per_lane), lax.rem(tile, per_lane)
                side, group = lax.div(lane, groups), lax.rem(lane, groups)
                first = pl.multiple_of(lane * rows + part * 128, 128)
                value = conv[before, pl.ds(first, 128), :]
                channels = pl.ds(pl.multiple_of(group * 128, 128), 128)
                times = pl.ds(pl.multiple_of(part * 128, 128), 128)
                query = queries[before, side, times, channels].astype(jnp.float32)
                segment = jnp.where(side == 0, pair, 1 - pair)
                column = segment * seg_len + (k - 1) * rows + part * 128
                out[channels, pl.ds(pl.multiple_of(column, 128), 128)] = (
                    (query * value).T.astype(jnp.bfloat16)
                )
            if k < n_chunks:
                for j in range(span):
                    t = tile * span + j
                    states = tuple(factors[r] * states[r] for r in range(poles))
                    total = list(states)
                    while len(total) > 1:
                        total = [a + b for a, b in zip(total[::2], total[1::2])]
                    conv[now, pl.ds(t, sublanes, stride=rows), :] = total[0] + locals_[k][t]
            return states

        states = lax.fori_loop(0, tiles, body, states)


def finish(place, ends, weights, decay, locals_, kept, given, seg_len):
    n_chunks = len(locals_)
    local = pl.BlockSpec(memory_space=pltpu.VMEM)
    operands = list(ends) + [weights, decay] + list(locals_) + list(kept) + list(given)
    lanes = decay.shape[1:]
    channels = kept[0].shape[2]
    rows = kept[0].shape[1]
    return pl.pallas_call(
        functools.partial(finish_kernel, len(ends), n_chunks, seg_len),
        grid_spec=pltpu.PrefetchScalarGridSpec(
            num_scalar_prefetch=1,
            grid=(),
            in_specs=[local] * len(operands),
            out_specs=local,
            scratch_shapes=[
                pltpu.VMEM((2, lanes[0] * rows, 128), jnp.float32),
                pltpu.VMEM((2, 2, rows, channels), jnp.bfloat16),
            ],
        ),
        out_shape=jax.ShapeDtypeStruct((channels, 2 * seg_len), jnp.bfloat16),
        compiler_params=pltpu.CompilerParams(vmem_limit_bytes=40 * MIB),
        cost_estimate=pl.CostEstimate(
            flops=32 * seg_len * lanes[0] * lanes[1],
            bytes_accessed=seg_len * lanes[0] * lanes[1] * 8,
            transcendentals=0,
        ),
        name="finish",
    )(place, *operands)


def per_device(tokens, weight, rate, residue, skip, order):
    seg_len = tokens.shape[0]
    n_ctx = lax.axis_size("ctx")
    seq_len = 2 * n_ctx * seg_len
    pair_index = lax.axis_index("fsdp")
    ctx_index = lax.axis_index("ctx")
    place = jnp.stack([pair_index, ctx_index, lax.axis_index("tp")]).astype(jnp.int32)

    starts = [sum(CHUNKS[:k]) for k in range(len(CHUNKS))]
    on_line = lax.axis_size("tp") == 4 and n_ctx == 4
    passed = []
    if on_line:
        near = lax.ppermute(tokens, "tp", [(0, 1), (1, 0), (2, 3), (3, 2)])
        middle = lax.ppermute(tokens, "tp", [(1, 2), (2, 1)])
        ends = lax.ppermute(middle, "tp", [(1, 0), (2, 3)])
        block = lax.slice_in_dim(near, 0, PASSED[0], axis=0)
        far_middle = [lax.ppermute(block, "tp", [(1, 2), (2, 1)])]
        passed = [ends] + far_middle

    own = weight.transpose(1, 0, 2)
    part = own.shape[1] // n_ctx
    piece_len = DEPTH
    per_part = part // piece_len
    plan = Plan(own.shape[1] // DEPTH, part // DEPTH, n_ctx)
    per_quarter = tokens.shape[1] // DEPTH
    partials = [None]

    def add_part(subs, late_subs, name):
        known = range(max(late_subs) + 1) if subs[0] < per_part - 1 else subs
        some = [pieces[m, n] for m in range(n_ctx) for n in known]
        sources, x_plan = [tokens, near], near_plan(plan, subs, 0)
        if name != "part_a":
            sources, x_plan = sources + [middle, ends], middle_plan(plan, subs, late_subs)
        units = n_ctx * len(subs) + (n_ctx // 2 * len(late_subs) if name != "part_a" else 0)
        return project(
            plan, place, sources, own, some, known[0], partials[-1], 0, seg_len, units, x_plan, name
        )

    pieces = {}
    bits = []
    while 1 << len(bits) < n_ctx:
        bits.insert(0, 1 << len(bits))
    first = []
    for sub in range(per_part):
        piece = lax.dynamic_slice_in_dim(own, ctx_index * part + sub * piece_len, piece_len, 1)
        if sub >= 2 and T["y_y"]:
            piece = after(piece, first[sub - 2])
        if sub == 3 and T["y3_c0"]:
            piece = after(piece, *[pieces[m, 0] for m in range(n_ctx)])
        if sub == 2 and T["y2_A"] and on_line:
            piece = after(piece, near, middle)
        first.append(exchanged(piece, "fsdp", 1))
        held = {0: first[sub]}
        for bit in bits:
            for mask in list(held):
                block = held[mask]
                if bit == bits[0] and sub and T["x_x"][sub]:
                    block = after(block, pieces[bit, sub - 1])
                if bit == bits[0] and sub >= 2 and T["x_c"][sub]:
                    block = after(block, *[pieces[m, sub - 2] for m in range(n_ctx)])
                if on_line:
                    if bit == bits[0] and sub == 3 and T["Ka"] == "x3":
                        block = after(block, partials[1])
                    if bit == bits[-1] and T["Ka"] == "c%d" % sub:
                        block = after(block, partials[1])
                    if bit == bits[0] and sub == 3 and T["Kb"] == "x3":
                        block = after(block, partials[2])
                    if bit == bits[-1] and sub == 3 and T["Kb"] == "c3":
                        block = after(block, partials[2])
                    if bit == bits[0] and sub == 2 and T["x2_A"]:
                        block = after(block, near, middle)
                    if bit == bits[-1] and T["c_A"] == sub:
                        block = after(block, near, middle)
                    if bit == bits[-1] and sub in T["c_P"]:
                        block = after(block, *passed)
                    if bit == bits[0] and sub in T["x_P"]:
                        block = after(block, *passed)
                if bit == bits[-1] and mask and T["c_ser"][sub]:
                    block = after(block, latest)
                latest = exchanged(block, "ctx", bit)
                held[mask | bit] = latest
        for mask in range(n_ctx):
            pieces[mask, sub] = held[mask]
        if sub == 1 and on_line:
            partials.append(add_part((0, 1), (0, 1), "part_a"))
            block = lax.slice_in_dim(near, PASSED[0], seg_len, axis=0)
            if T["FK"]:
                block = after(block, partials[1])
            far_middle.append(lax.ppermute(block, "tp", [(1, 2), (2, 1)]))
        if sub == 2 and on_line:
            partials.append(add_part((2,), (0, 1, 2), "part_b"))
    ordered = [pieces[mask, sub] for mask in range(n_ctx) for sub in range(per_part)]

    channels = rate.shape[0]
    groups = channels // 128

    def spread(values):
        lanes = values.T.reshape(-1, groups, 128)
        return jnp.concatenate([lanes, lanes], axis=1)

    rates = spread(rate)
    decay = jnp.exp(-rates)
    gain = spread(pole_gain(rate, residue, float(seq_len)))
    direct = spread(skip[:, None])[0]

    if on_line:
        most = add_part((3,), (3,), "part_c")

    weights = carry(place, order, rates, n_ctx, seg_len)
    kept, given, locals_ = [], [], []
    state = jnp.zeros_like(decay)
    states = []
    for k, (base, rows) in enumerate(zip(starts, CHUNKS)):
        if on_line:
            n, row = 0, base
            while row >= PASSED[n]:
                row -= PASSED[n]
                n += 1
            block = lax.slice_in_dim(far_middle[n], row, row + rows, axis=0)
            if k in T["E"]:
                block = after(block, most)
            last = lax.ppermute(block, "tp", [(1, 0), (2, 3)])
            if k == 0:
                last = after(last, weights)
            if k in T["S"]:
                last = after(last, states[T["S"][k]])

            def last_part(x, sides):
                return project(
                    plan, place, [far_middle[n], x], own, ordered, 0, most, base, rows,
                    per_quarter, last_plan(per_quarter, row, rows), "project", sides,
                )

            if k < len(CHUNKS) - 1:
                keep, give = last_part(last, (0, 1))
            else:
                (give,) = last_part(last, (1,))
                (keep,) = last_part(after(last, give), (0,))
        else:
            block = lax.slice_in_dim(tokens, base, base + rows, axis=0)
            whole = lax.all_gather(block, "tp", axis=0, tiled=False)
            keep, give = project(
                plan, place, [whole], own, ordered, 0, None, 0, rows,
                2 * plan.half_blocks, gathered_plan(per_quarter), "project",
            )
        got = exchanged(give, "fsdp", 1)
        local, state = scan(keep, got, decay, gain, direct, state)
        states.append(state)
        kept.append(keep)
        given.append(got)
        locals_.append(local)

    ends = [state] + [exchanged(state, "ctx", mask) for mask in range(1, n_ctx)]
    return finish(place, ends, weights, decay, locals_, kept, given, seg_len)


def solution(mesh):
    placed = (
        P(("ctx", "fsdp"), "tp"),
        P("fsdp", None, "tp"),
        P(("tp", "fsdp"), None),
        P(("tp", "fsdp"), None),
        P(("tp", "fsdp")),
        P(),
    )
    return jax.shard_map(
        per_device, mesh=mesh, in_specs=placed, out_specs=P(("tp", "fsdp"), "ctx"), check_vma=False
    )
```

```python
import functools
from typing import NamedTuple

import jax
import jax.numpy as jnp
from jax import lax
from jax.experimental import pallas as pl
from jax.experimental.pallas import tpu as pltpu
from jax.sharding import PartitionSpec as P

MIB = 1 << 20
DEPTH = 256
CHUNKS = (256, 256, 256, 256)
PASSED = (512, 512)
T = {'y_y': True, 'y3_c0': True, 'y2_A': False, 'x_x': [0, False, True, False], 'x_c': [0, 0, 1, 1], 'Ka': 'c3', 'x2_A': False, 'c_A': 9, 'c_P': [3], 'x_P': [], 'c_ser': [1, 0, 0, 0], 'E': [], 'FK': True, 'CH': [256, 256, 256, 256], 'S': {}, 'Kb': 'c3', 'cost': {'part_a': 0, 'part_b': 0, 'part_c': 0, 'project': 0}}
FREE = pl.CostEstimate(flops=0, bytes_accessed=0, transcendentals=0)


class Plan(NamedTuple):
    half_blocks: int
    part_blocks: int
    n_parts: int


def exchanged(block, axis, mask):
    count = lax.axis_size(axis)
    return lax.ppermute(block, axis, [(i, i ^ mask) for i in range(count)])


def after(value, *others):
    return lax.optimization_barrier((value, *others))[0]


def pole_gain(rate, residue, length):
    return residue * jnp.sqrt(jnp.maximum(-jnp.expm1(-2.0 * rate), 1.0 / length))


def choose(low, high, number, act):
    if high - low == 1:
        act(low)
        return
    middle = (low + high) // 2

    @pl.when(number < middle)
    def _():
        choose(low, middle, number, act)

    @pl.when(number >= middle)
    def _():
        choose(middle, high, number, act)


def fetch_weights(plan, place, p, block, own, pieces, first, lanes, target, sem):
    pair, ctx = place[0], place[1]
    local = lax.rem(block, plan.half_blocks)
    here = lax.div(block, plan.half_blocks) == pair

    @pl.when(here)
    def _():
        row = pl.multiple_of(local * DEPTH, DEPTH)
        pltpu.make_async_copy(own.at[p, pl.ds(row, DEPTH), lanes], target, sem).start()

    @pl.when(jnp.logical_not(here))
    def _():
        stride = len(pieces) // plan.n_parts
        number = jnp.bitwise_xor(lax.div(local, plan.part_blocks), ctx) * stride
        number = number + lax.rem(local, plan.part_blocks) - first

        def act(n):
            pltpu.make_async_copy(pieces[n].at[p, :, lanes], target, sem).start()

        choose(0, len(pieces), number, act)


def project_kernel(plan, n_inputs, n_pieces, first, base, sides, blocks, x_plan, place, *refs):
    refs = list(refs)
    inputs = [refs.pop(0) for _ in range(n_inputs)]
    own = refs.pop(0)
    pieces = [refs.pop(0) for _ in range(n_pieces)]
    init = refs.pop(0) if base is not None else None
    final = len(sides) > 0
    outs = [refs.pop(0) for _ in range(max(1, len(sides)))]
    x_buf, w_buf, x_sem, w_sem = refs[:4]
    refs = refs[4:]
    if final:
        i_buf, i_sem = refs if init is not None else (None, None)
    else:
        o_buf, o_sem, i_sem = refs
        i_buf = o_buf
    pair, tp = place[0], place[2]
    rows, depth = x_buf.shape
    width = w_buf.shape[2]
    taken = pl.ds(0, width)
    if len(sides) == 1:
        taken = pl.ds(pl.multiple_of((pair if sides[0] == 0 else 1 - pair) * width, 128), width)
    spans = (slice(0, depth // 2), slice(depth // 2, depth))

    def fetch(p):
        if init is not None:
            pltpu.make_async_copy(
                init.at[p, pl.ds(base, rows), taken], i_buf.at[p], i_sem.at[p]
            ).start()
        for part in (0, 1):

            def one(step, carry):
                where = pl.ds(pl.multiple_of(step * DEPTH, DEPTH), DEPTH)
                block = x_plan(tp, step, inputs, x_buf.at[:, where], x_sem.at[part], p == 0)
                target = w_buf.at[p, where, :]
                fetch_weights(
                    plan, place, p, block, own, pieces, first, taken, target, w_sem.at[p, part]
                )
                return carry

            lax.fori_loop(part * blocks // 2, (part + 1) * blocks // 2, one, 0)

    def await_part(p, part):
        if p == 0:
            target = x_buf.at[:, spans[part]]
            pltpu.make_async_copy(target, target, x_sem.at[part]).wait()
        target = w_buf.at[p, spans[part], :]
        pltpu.make_async_copy(target, target, w_sem.at[p, part]).wait()

    fetch(0)
    fetch(1)
    for p in range(3):
        if init is not None:
            pltpu.make_async_copy(i_buf.at[p], i_buf.at[p], i_sem.at[p]).wait()
        await_part(p, 0)
        if p:
            await_part(p, 1)
        if not final:
            chunk = min(rows, 256)

            def multiply(span, add, m, carry):
                some = pl.ds(pl.multiple_of(m * chunk, chunk), chunk)
                new = jnp.dot(
                    x_buf[some, span], w_buf[p, span, :], preferred_element_type=jnp.float32
                )
                if add or init is not None:
                    new = o_buf[p, some, :] + new
                o_buf[p, some, :] = new
                return carry

            if p == 0:
                lax.fori_loop(0, rows // chunk, functools.partial(multiply, spans[0], False), 0)
                await_part(0, 1)
                fetch(2)
                lax.fori_loop(0, rows // chunk, functools.partial(multiply, spans[1], True), 0)
            else:
                whole = slice(0, depth)
                lax.fori_loop(0, rows // chunk, functools.partial(multiply, whole, False), 0)
            pltpu.make_async_copy(o_buf.at[p], outs[0].at[p], o_sem.at[p]).start()
            continue
        half = outs[0].shape[2]
        lanes = [pl.ds(pl.multiple_of(x * half, 128), half) for x in (pair, 1 - pair)]
        if len(sides) == 1:
            lanes = [pl.ds(0, half)]

        def product(span, n):
            return jnp.dot(
                x_buf[:, span], w_buf[p, span, lanes[n]], preferred_element_type=jnp.float32
            )

        if p == 0:
            early = [product(spans[0], n) for n in range(len(sides))]
            await_part(0, 1)
            fetch(2)
            sums = [early[n] + product(spans[1], n) for n in range(len(sides))]
        else:
            sums = [product(slice(0, depth), n) for n in range(len(sides))]
        for n, side in enumerate(sides):
            new, out = sums[n], outs[n]
            if init is not None:
                new = i_buf[p, :, lanes[n]] + new
            new = new.astype(jnp.bfloat16)
            if side == 0 or p == 0:
                out[p] = new
            elif p == 1:
                out[1] = new
            else:
                both = out[1].astype(jnp.float32) * new.astype(jnp.float32)
                out[1] = both.astype(jnp.bfloat16)
    if not final:
        for p in range(3):
            pltpu.make_async_copy(o_buf.at[p], outs[0].at[p], o_sem.at[p]).wait()


def project(
    plan, place, inputs, own, pieces, first, init, base, rows, blocks, x_plan, name, sides=(0, 1)
):
    final = name == "project"
    sides = sides if final else ()
    width = own.shape[2]
    anywhere = pl.BlockSpec(memory_space=pl.ANY)
    local = pl.BlockSpec(memory_space=pltpu.VMEM)
    operands = list(inputs) + [own] + list(pieces) + ([] if init is None else [init])
    depth = blocks * DEPTH
    half = width // 2
    if len(sides) == 1:
        width = half
    total = (3, rows, width)
    scratch = [
        pltpu.VMEM((rows, depth), jnp.bfloat16),
        pltpu.VMEM((3, depth, width), jnp.bfloat16),
        pltpu.SemaphoreType.DMA((2,)),
        pltpu.SemaphoreType.DMA((3, 2)),
    ]
    if final:
        if init is not None:
            scratch += [pltpu.VMEM(total, jnp.float32), pltpu.SemaphoreType.DMA((3,))]
        out_shape = [
            jax.ShapeDtypeStruct((3 - side, rows, half), jnp.bfloat16) for side in sides
        ]
    else:
        scratch += [pltpu.VMEM(total, jnp.float32)] + [pltpu.SemaphoreType.DMA((3,))] * 2
        out_shape = jax.ShapeDtypeStruct(total, jnp.float32)
    return pl.pallas_call(
        functools.partial(
            project_kernel, plan, len(inputs), len(pieces), first,
            None if init is None else base, sides, blocks, x_plan,
        ),
        grid_spec=pltpu.PrefetchScalarGridSpec(
            num_scalar_prefetch=1,
            grid=(),
            in_specs=[anywhere] * len(operands),
            out_specs=[local] * len(sides) if final else anywhere,
            scratch_shapes=scratch,
        ),
        out_shape=out_shape,
        compiler_params=pltpu.CompilerParams(vmem_limit_bytes=56 * MIB),
        cost_estimate=pl.CostEstimate(
            flops=T["cost"][name], bytes_accessed=0, transcendentals=0
        ),
        name=name,
    )(place, *operands)


def columns(quarter_block):
    return pl.ds(pl.multiple_of(quarter_block * DEPTH, DEPTH), DEPTH)


def gathered_plan(per_quarter):
    def plan(tp, step, inputs, target, sem, copy):
        source = inputs[0].at[lax.div(step, per_quarter), :, columns(lax.rem(step, per_quarter))]
        if copy:
            pltpu.make_async_copy(source, target, sem).start()
        return step

    return plan


def line_ends(tp):
    return (tp == 0) | (tp == 3)


def near_block(plan, tp, step, subs, base, inputs, target, sem, copy):
    span = plan.half_blocks // 2 // plan.part_blocks
    place = lax.div(step, len(subs))
    sub = subs[0] + lax.rem(step, len(subs))
    mine = place < span
    side = jnp.where(mine, lax.rem(tp, 2), 1 - lax.rem(tp, 2))
    within = lax.rem(place, span) * plan.part_blocks + sub
    block = lax.div(tp, 2) * plan.half_blocks + side * span * plan.part_blocks + within
    if not copy:
        return block
    where = columns(within)
    for at, source in ((True, inputs[0]), (False, inputs[1])):
        @pl.when(mine == at)
        def _():
            rows = pl.ds(base, target.shape[0])
            pltpu.make_async_copy(source.at[rows, where], target, sem).start()

    return block


def near_plan(plan, subs, base):
    def x_plan(tp, step, inputs, target, sem, copy):
        return near_block(plan, tp, step, subs, base, inputs, target, sem, copy)

    return x_plan


def middle_plan(plan, subs, late_subs):
    span = plan.half_blocks // plan.part_blocks * len(subs)
    per_quarter = plan.half_blocks // 2

    def x_plan(tp, step, inputs, target, sem, copy):
        middle, ends = inputs[2:]
        late = step - span
        early = jnp.minimum(step, span - 1)
        near = near_block(plan, tp, early, subs, 0, inputs, target, sem, False)
        part, sub = lax.div(late, len(late_subs)), lax.rem(late, len(late_subs))
        within = jnp.maximum(part * plan.part_blocks + late_subs[0] + sub, 0)
        block = jnp.where(late < 0, near, (2 - lax.div(tp, 2)) * per_quarter + within)
        if not copy:
            return block
        where = columns(within)

        @pl.when(late < 0)
        def _():
            near_block(plan, tp, early, subs, 0, inputs, target, sem, True)

        for at_end, source in ((False, middle), (True, ends)):
            @pl.when((late >= 0) & (line_ends(tp) == at_end))
            def _():
                pltpu.make_async_copy(source.at[:, where], target, sem).start()

        return block

    return x_plan


def last_plan(per_quarter, row, rows):
    def plan(tp, step, inputs, target, sem, copy):
        block = jnp.where(tp < 2, 3, 0) * per_quarter + step
        if not copy:
            return block
        middle, ends = inputs
        where = columns(step)

        @pl.when(line_ends(tp))
        def _():
            pltpu.make_async_copy(ends.at[:, where], target, sem).start()

        @pl.when(jnp.logical_not(line_ends(tp)))
        def _():
            pltpu.make_async_copy(middle.at[pl.ds(row, rows), where], target, sem).start()

        return block

    return plan


def scan_kernel(kept, given, decay, gain, skip, state_in, local_ref, state_out, prod):
    poles = decay.shape[0]
    rows = kept.shape[1]
    groups = kept.shape[2] // 128
    for side, ref in enumerate((kept, given)):
        for g in range(groups):
            lanes = slice(g * 128, (g + 1) * 128)
            product = ref[1, :, lanes].astype(jnp.float32)
            if side == 0:
                product = product * ref[2, :, lanes].astype(jnp.float32)
            prod[:, side * groups + g, :] = product
    direct = skip[...]
    factors = [decay[r] for r in range(poles)]
    gains = [gain[r] for r in range(poles)]

    def step(t, states):
        p = prod[t]
        new = [factors[r] * states[r] + gains[r] * p for r in range(poles)]
        total = list(new)
        while len(total) > 1:
            total = [a + b for a, b in zip(total[::2], total[1::2])]
        local_ref[t] = total[0] + direct * p
        return tuple(new)

    states = lax.fori_loop(0, rows, step, tuple(state_in[r] for r in range(poles)), unroll=16)
    for r in range(poles):
        state_out[r] = states[r]


def scan(kept, given, decay, gain, skip, state):
    rows = kept.shape[1]
    local = pl.BlockSpec(memory_space=pltpu.VMEM)
    lanes = decay.shape[1:]
    return pl.pallas_call(
        scan_kernel,
        in_specs=[local] * 6,
        out_specs=[local] * 2,
        out_shape=[
            jax.ShapeDtypeStruct((rows,) + lanes, jnp.float32),
            jax.ShapeDtypeStruct(decay.shape, jnp.float32),
        ],
        scratch_shapes=[pltpu.VMEM((rows,) + lanes, jnp.float32)],
        compiler_params=pltpu.CompilerParams(vmem_limit_bytes=24 * MIB),
        cost_estimate=FREE,
        name="scan",
    )(kept, given, decay, gain, skip, state)


def carry_kernel(n_ctx, seg_len, place, order, rate, weights):
    poles, sublanes, _ = rate.shape
    pair, ctx = place[0], place[1]
    upper = lax.broadcasted_iota(jnp.int32, rate.shape[1:], 0) < sublanes // 2
    targets = (order[2 * ctx + pair], order[2 * ctx + 1 - pair])
    for mask in range(n_ctx):
        origin = jnp.bitwise_xor(ctx, mask)
        sources = (order[2 * origin + pair], order[2 * origin + 1 - pair])
        for cross in (0, 1):
            gaps = [targets[s] - 1 - sources[s ^ cross] for s in (0, 1)]
            gap = jnp.where(upper, gaps[0], gaps[1])
            span = jnp.maximum(gap, 0).astype(jnp.float32) * seg_len
            for r in range(poles):
                weights[mask, cross, r] = jnp.where(gap >= 0, jnp.exp(-rate[r] * span), 0.0)


def carry(place, order, rate, n_ctx, seg_len):
    local = pl.BlockSpec(memory_space=pltpu.VMEM)
    return pl.pallas_call(
        functools.partial(carry_kernel, n_ctx, seg_len),
        grid_spec=pltpu.PrefetchScalarGridSpec(
            num_scalar_prefetch=2, grid=(), in_specs=[local], out_specs=local
        ),
        out_shape=jax.ShapeDtypeStruct((n_ctx, 2) + rate.shape, jnp.float32),
        cost_estimate=FREE,
        name="carry",
    )(place, order, rate)


def finish_kernel(n_ctx, n_chunks, seg_len, place, *refs):
    refs = list(refs)
    ends = [refs.pop(0) for _ in range(n_ctx)]
    weights = refs.pop(0)
    decay = refs.pop(0)
    locals_ = [refs.pop(0) for _ in range(n_chunks)]
    kept = [refs.pop(0) for _ in range(n_chunks)]
    given = [refs.pop(0) for _ in range(n_chunks)]
    out = refs.pop(0)
    conv = refs.pop(0)
    poles, sublanes, _ = decay.shape
    groups = sublanes // 2
    pair = place[0]
    states = [jnp.zeros(decay.shape[1:], jnp.float32) for _ in range(poles)]
    for mask in range(n_ctx):
        for r in range(poles):
            end = ends[mask][r]
            turned = jnp.concatenate([end[groups:], end[:groups]], axis=0)
            states[r] = states[r] + weights[mask, 0, r] * end + weights[mask, 1, r] * turned
    factors = [decay[r] for r in range(poles)]
    states = tuple(states)
    base = 0
    for k in range(n_chunks):
        rows = locals_[k].shape[0]

        def step(t, states):
            new = [factors[r] * states[r] for r in range(poles)]
            total = list(new)
            while len(total) > 1:
                total = [a + b for a, b in zip(total[::2], total[1::2])]
            conv[t] = total[0] + locals_[k][t]
            return tuple(new)

        states = lax.fori_loop(0, rows, step, states, unroll=16)
        for side, ref in enumerate((kept[k], given[k])):
            segment = pair if side == 0 else 1 - pair
            column = pl.multiple_of(segment * seg_len + base, 128)
            for g in range(groups):
                lanes = slice(g * 128, (g + 1) * 128)
                query = ref[0, :, lanes].astype(jnp.float32)
                gated = query * conv[:rows, side * groups + g, :]
                out[lanes, pl.ds(column, rows)] = gated.T.astype(jnp.bfloat16)
        base += rows


def finish(place, ends, weights, decay, locals_, kept, given, seg_len):
    n_chunks = len(locals_)
    local = pl.BlockSpec(memory_space=pltpu.VMEM)
    operands = list(ends) + [weights, decay] + list(locals_) + list(kept) + list(given)
    lanes = decay.shape[1:]
    channels = kept[0].shape[2]
    longest = max(k.shape[1] for k in kept)
    return pl.pallas_call(
        functools.partial(finish_kernel, len(ends), n_chunks, seg_len),
        grid_spec=pltpu.PrefetchScalarGridSpec(
            num_scalar_prefetch=1,
            grid=(),
            in_specs=[local] * len(operands),
            out_specs=local,
            scratch_shapes=[pltpu.VMEM((longest,) + lanes, jnp.float32)],
        ),
        out_shape=jax.ShapeDtypeStruct((channels, 2 * seg_len), jnp.bfloat16),
        compiler_params=pltpu.CompilerParams(vmem_limit_bytes=40 * MIB),
        cost_estimate=pl.CostEstimate(
            flops=32 * seg_len * lanes[0] * lanes[1],
            bytes_accessed=seg_len * lanes[0] * lanes[1] * 8,
            transcendentals=0,
        ),
        name="finish",
    )(place, *operands)


def per_device(tokens, weight, rate, residue, skip, order):
    seg_len = tokens.shape[0]
    n_ctx = lax.axis_size("ctx")
    seq_len = 2 * n_ctx * seg_len
    pair_index = lax.axis_index("fsdp")
    ctx_index = lax.axis_index("ctx")
    place = jnp.stack([pair_index, ctx_index, lax.axis_index("tp")]).astype(jnp.int32)

    starts = [sum(CHUNKS[:k]) for k in range(len(CHUNKS))]
    on_line = lax.axis_size("tp") == 4 and n_ctx == 4
    passed = []
    if on_line:
        near = lax.ppermute(tokens, "tp", [(0, 1), (1, 0), (2, 3), (3, 2)])
        middle = lax.ppermute(tokens, "tp", [(1, 2), (2, 1)])
        ends = lax.ppermute(middle, "tp", [(1, 0), (2, 3)])
        block = lax.slice_in_dim(near, 0, PASSED[0], axis=0)
        far_middle = [lax.ppermute(block, "tp", [(1, 2), (2, 1)])]
        passed = [ends] + far_middle

    own = weight.transpose(1, 0, 2)
    part = own.shape[1] // n_ctx
    piece_len = DEPTH
    per_part = part // piece_len
    plan = Plan(own.shape[1] // DEPTH, part // DEPTH, n_ctx)
    per_quarter = tokens.shape[1] // DEPTH
    partials = [None]

    def add_part(subs, late_subs, name):
        known = range(max(late_subs) + 1) if subs[0] < per_part - 1 else subs
        some = [pieces[m, n] for m in range(n_ctx) for n in known]
        sources, x_plan = [tokens, near], near_plan(plan, subs, 0)
        if name != "part_a":
            sources, x_plan = sources + [middle, ends], middle_plan(plan, subs, late_subs)
        units = n_ctx * len(subs) + (n_ctx // 2 * len(late_subs) if name != "part_a" else 0)
        return project(
            plan, place, sources, own, some, known[0], partials[-1], 0, seg_len, units, x_plan, name
        )

    pieces = {}
    bits = []
    while 1 << len(bits) < n_ctx:
        bits.insert(0, 1 << len(bits))
    first = []
    for sub in range(per_part):
        piece = lax.dynamic_slice_in_dim(own, ctx_index * part + sub * piece_len, piece_len, 1)
        if sub >= 2 and T["y_y"]:
            piece = after(piece, first[sub - 2])
        if sub == 3 and T["y3_c0"]:
            piece = after(piece, *[pieces[m, 0] for m in range(n_ctx)])
        if sub == 2 and T["y2_A"] and on_line:
            piece = after(piece, near, middle)
        first.append(exchanged(piece, "fsdp", 1))
        held = {0: first[sub]}
        for bit in bits:
            for mask in list(held):
                block = held[mask]
                if bit == bits[0] and sub and T["x_x"][sub]:
                    block = after(block, pieces[bit, sub - 1])
                if bit == bits[0] and sub >= 2 and T["x_c"][sub]:
                    block = after(block, *[pieces[m, sub - 2] for m in range(n_ctx)])
                if on_line:
                    if bit == bits[0] and sub == 3 and T["Ka"] == "x3":
                        block = after(block, partials[1])
                    if bit == bits[-1] and T["Ka"] == "c%d" % sub:
                        block = after(block, partials[1])
                    if bit == bits[0] and sub == 3 and T["Kb"] == "x3":
                        block = after(block, partials[2])
                    if bit == bits[-1] and sub == 3 and T["Kb"] == "c3":
                        block = after(block, partials[2])
                    if bit == bits[0] and sub == 2 and T["x2_A"]:
                        block = after(block, near, middle)
                    if bit == bits[-1] and T["c_A"] == sub:
                        block = after(block, near, middle)
                    if bit == bits[-1] and sub in T["c_P"]:
                        block = after(block, *passed)
                    if bit == bits[0] and sub in T["x_P"]:
                        block = after(block, *passed)
                if bit == bits[-1] and mask and T["c_ser"][sub]:
                    block = after(block, latest)
                latest = exchanged(block, "ctx", bit)
                held[mask | bit] = latest
        for mask in range(n_ctx):
            pieces[mask, sub] = held[mask]
        if sub == 1 and on_line:
            partials.append(add_part((0, 1), (0, 1), "part_a"))
            block = lax.slice_in_dim(near, PASSED[0], seg_len, axis=0)
            if T["FK"]:
                block = after(block, partials[1])
            far_middle.append(lax.ppermute(block, "tp", [(1, 2), (2, 1)]))
        if sub == 2 and on_line:
            partials.append(add_part((2,), (0, 1, 2), "part_b"))
    ordered = [pieces[mask, sub] for mask in range(n_ctx) for sub in range(per_part)]

    channels = rate.shape[0]
    groups = channels // 128

    def spread(values):
        lanes = values.T.reshape(-1, groups, 128)
        return jnp.concatenate([lanes, lanes], axis=1)

    rates = spread(rate)
    decay = jnp.exp(-rates)
    gain = spread(pole_gain(rate, residue, float(seq_len)))
    direct = spread(skip[:, None])[0]

    if on_line:
        most = add_part((3,), (3,), "part_c")

    weights = carry(place, order, rates, n_ctx, seg_len)
    kept, given, locals_ = [], [], []
    state = jnp.zeros_like(decay)
    states = []
    for k, (base, rows) in enumerate(zip(starts, CHUNKS)):
        if on_line:
            n, row = 0, base
            while row >= PASSED[n]:
                row -= PASSED[n]
                n += 1
            block = lax.slice_in_dim(far_middle[n], row, row + rows, axis=0)
            if k in T["E"]:
                block = after(block, most)
            last = lax.ppermute(block, "tp", [(1, 0), (2, 3)])
            if k == 0:
                last = after(last, weights)
            if k in T["S"]:
                last = after(last, states[T["S"][k]])

            def last_part(x, sides):
                return project(
                    plan, place, [far_middle[n], x], own, ordered, 0, most, base, rows,
                    per_quarter, last_plan(per_quarter, row, rows), "project", sides,
                )

            if k < len(CHUNKS) - 1:
                keep, give = last_part(last, (0, 1))
            else:
                (give,) = last_part(last, (1,))
                (keep,) = last_part(after(last, give), (0,))
        else:
            block = lax.slice_in_dim(tokens, base, base + rows, axis=0)
            whole = lax.all_gather(block, "tp", axis=0, tiled=False)
            keep, give = project(
                plan, place, [whole], own, ordered, 0, None, 0, rows,
                2 * plan.half_blocks, gathered_plan(per_quarter), "project",
            )
        got = exchanged(give, "fsdp", 1)
        local, state = scan(keep, got, decay, gain, direct, state)
        states.append(state)
        kept.append(keep)
        given.append(got)
        locals_.append(local)

    ends = [state] + [exchanged(state, "ctx", mask) for mask in range(1, n_ctx)]
    return finish(place, ends, weights, decay, locals_, kept, given, seg_len)


def solution(mesh):
    placed = (
        P(("ctx", "fsdp"), "tp"),
        P("fsdp", None, "tp"),
        P(("tp", "fsdp"), None),
        P(("tp", "fsdp"), None),
        P(("tp", "fsdp")),
        P(),
    )
    return jax.shard_map(
        per_device, mesh=mesh, in_specs=placed, out_specs=P(("tp", "fsdp"), "ctx"), check_vma=False
    )
```
